256 devices in a mesh: dp: 32 (over y_lo, z, core), ctx: 8 (over y_hi, x).
Axes of the slice: x: 4, y: 4 (y_hi: 2, y_lo: 2; y = y_hi * 2 + y_lo), z: 8, core: 2. Of those that a mesh axis runs over, the one named last changes fastest.
Arguments:
- queries: bfloat16 [32, 2048, 2560], P('dp', 'ctx'), may hold values from -9 to 9
- keys: bfloat16 [32, 2048, 512], P('dp', 'ctx'), may hold values from -9 to 9
- values: bfloat16 [32, 2048, 512], P('dp', 'ctx'), may hold values from -6 to 6
- output_gradient: bfloat16 [32, 2048, 5120], P('dp', 'ctx'), may hold values from -6 to 6
- advantages: int32 [32, 2048], P('dp', 'ctx'), may hold values from -384 to 384
- token_branch_index: int32 [32, 8, 256], P('dp', 'ctx'), may hold values from 0 to 15, as said below
- parent_of_block: int32 [32, 8], P('dp'), may hold values from 0 to 7, as said below
- adapter_down_weight: bfloat16 [2560, 256], replicated, may hold values from -0.125 to 0.125
- adapter_up_weight: bfloat16 [256, 5120], replicated, may hold values from -0.375 to 0.375
Outputs:
- grad_down: float32 [2560, 256], P('ctx')
- grad_up: float32 [256, 5120], P(None, 'ctx')
The draws below stay inside these ranges and needn't reach their ends.
Inputs may be any that keep to these rules, and one draw needn't show every extreme that they name: `token_branch_index`: within each block the first 64 positions carry 0, ids never fall along the block, and every id from 0 to 15 occurs in every block. `parent_of_block`: each block's entry is a lower block of the same group or the block itself, which then has no parent; in the first group the last block's parent is block 6, and in the second group the last block has no parent.
All inputs are finite; a program needn't handle non-finite values.
Results may differ from the reference program's by a relative error of at most 0.0053.
Values may be sent and summed in bfloat16 or wider, within the bound.
A program may use at most 128 MiB of HBM per device.

```python
import math
import jax
import jax.numpy as jnp
from jax import lax

MODEL_FEATURES = 5120
HEAD_DIM = 128
QUERY_HEADS = 20
KV_HEADS = 4
ADAPTER_RANK = 256
TOK_DEV = 256
BRANCHES = 16
ATTENTION_WIDTH = 2560
BLOCKS = 8
TOKENS = 2048
GROUPS = 32
ALL_TOKENS = 65536


def draw_queries(key, part):
    key = jax.random.fold_in(key, 1)
    drawn = jnp.clip(1.5 * jax.random.normal(key, (GROUPS, TOKENS, QUERY_HEADS * HEAD_DIM), jnp.float32), -9.0, 9.0)
    return drawn.astype(jnp.bfloat16)


def draw_keys(key, part):
    key = jax.random.fold_in(key, 2)
    drawn = jnp.clip(1.5 * jax.random.normal(key, (GROUPS, TOKENS, KV_HEADS * HEAD_DIM), jnp.float32), -9.0, 9.0)
    return drawn.astype(jnp.bfloat16)


def draw_token_branch_index(key, part):
    key = jax.random.fold_in(key, 3)
    span_len = TOK_DEV - TOK_DEV // 4
    row_keys = jax.random.split(key, GROUPS * BLOCKS)
    cut_points = jax.vmap(lambda row_key: jax.random.permutation(row_key, span_len - 1)[:BRANCHES - 2] + 1)(row_keys)
    offsets = jnp.arange(TOK_DEV, dtype=jnp.int32) - TOK_DEV // 4
    branch_num = 1 + jnp.sum((cut_points[:, None, :] <= offsets[None, :, None]).astype(jnp.int32), axis=-1)
    branch_num = jnp.where(offsets[None, :] < 0, 0, branch_num)
    return branch_num.reshape(GROUPS, BLOCKS, TOK_DEV).astype(jnp.int32)


def draw_parent_of_block(key, part):
    key = jax.random.fold_in(key, 4)
    raw_draw = jax.random.randint(key, (GROUPS, BLOCKS), 0, 1 << 20, dtype=jnp.int32)
    root_draw = jax.random.randint(jax.random.fold_in(key, 5), (GROUPS, BLOCKS), 0, 8, dtype=jnp.int32)
    places = jnp.arange(BLOCKS, dtype=jnp.int32)
    parents = (raw_draw % jnp.maximum(places, 1)[None, :]).astype(jnp.int32)
    parents = jnp.where((root_draw == 0) & (places[None, :] > 0), places[None, :], parents)
    group_places = jnp.arange(GROUPS, dtype=jnp.int32)
    last_block = places[None, :] == BLOCKS - 1
    parents = jnp.where((group_places[:, None] == 1) & last_block, BLOCKS - 1, parents)
    parents = jnp.where((group_places[:, None] == 0) & last_block, BLOCKS - 2, parents)
    return parents.astype(jnp.int32)


def with_ends(values, own_key, low, high):
    dims = values.shape
    place = [jax.random.randint(jax.random.fold_in(own_key, axis), (), 0, dims[axis]) for axis in range(len(dims))]
    values = values.at[tuple(place)].set(low)
    longest = dims.index(max(dims))
    place[longest] = (place[longest] + 1) % dims[longest]
    return values.at[tuple(place)].set(high)


def strengthened(array, own_key, source, target, shards_of, factor):
    owner, partner = [(jnp.arange(array.shape[dim]) // (array.shape[dim] // shards_of)).reshape([-1 if axis == dim else 1 for axis in range(array.ndim)]) for dim in (source, target)]
    chosen = jax.random.permutation(own_key, shards_of)[partner]
    strong = (owner == chosen) | (owner == (partner + shards_of // 2) % shards_of)
    return jnp.where(strong, factor * array, array)


def block_levels(own_key, dims, cuts, least, largest):
    def one(dim, parts):
        steps = jax.random.uniform(jax.random.fold_in(jax.random.fold_in(own_key, 6), dim), (parts,), jnp.float32, least / len(cuts), largest / len(cuts))
        return jnp.repeat(jnp.exp(steps), dims[dim] // parts).reshape((-1,) + (1,) * (len(dims) - dim - 1))

    factor_of = one(*cuts[0])
    for cut in cuts[1:]:
        factor_of = factor_of * one(*cut)
    return factor_of


def noise(rng, dims, deviation, reach, pieces=(), kind=jnp.bfloat16):
    gain = block_levels(rng, dims, pieces, -0.22, 0.18) if pieces else 1.0
    values = jax.random.normal(rng, dims, jnp.float32) * deviation * gain
    return jnp.minimum(jnp.maximum(values, -reach), reach).astype(kind)


def noise_with(stream_key, extent, width, bound, pieces, heavy, kind=jnp.bfloat16):
    array = width * jax.random.normal(stream_key, extent, jnp.float32)
    if pieces:
        array = array * block_levels(stream_key, extent, pieces, -0.22, 0.18)
    return jnp.clip(strengthened(array, jax.random.fold_in(stream_key, 3), *heavy), -bound, bound).astype(kind)


def setup_inputs(seed: int = 0) -> dict:
    splits = jax.random.split(jax.random.key(seed), 10)
    return {
        "queries": draw_queries(jax.random.fold_in(splits[9], 71), 0),
        "keys": draw_keys(jax.random.fold_in(splits[9], 71), 0),
        "values": noise(splits[2], (GROUPS, TOKENS, KV_HEADS * HEAD_DIM), 1.0, 6.0, ((0, 32), (1, 8))),
        "output_gradient": noise_with(splits[3], (GROUPS, TOKENS, MODEL_FEATURES), 1.0, 6.0, ((0, 32), (1, 8)), (1, 2, 8, 2.0)),
        "advantages": with_ends(jax.random.randint(splits[4], (GROUPS, TOKENS), -384, 385), jax.random.fold_in(splits[4], 1), -384, 384).astype(jnp.int32),
        "token_branch_index": draw_token_branch_index(jax.random.fold_in(splits[9], 71), 0),
        "parent_of_block": draw_parent_of_block(jax.random.fold_in(splits[9], 71), 0),
        "adapter_down_weight": noise(splits[7], (ATTENTION_WIDTH, ADAPTER_RANK), ATTENTION_WIDTH ** -0.5, 0.125),
        "adapter_up_weight": noise(splits[8], (ADAPTER_RANK, MODEL_FEATURES), ADAPTER_RANK ** -0.5, 0.375),
    }


NEGATIVE = -1e+30

def ancestry(parents):
    block_count = parents.shape[0]
    places = jnp.arange(block_count, dtype=jnp.int32)

    def follow(step_index, loop_state):
        current, ancestor_marks = loop_state
        current = parents[current].astype(jnp.int32)
        ancestor_marks = ancestor_marks | (current[:, None] == places[None, :])
        return (current, ancestor_marks)
    empty_marks = jnp.zeros((block_count, block_count), jnp.int32) > 0
    current, ancestor_marks = lax.fori_loop(0, block_count, follow, (places, empty_marks))
    return ancestor_marks & (places[:, None] != places[None, :])

def group_context(group_queries, group_keys, group_values, group_branches, group_parents):
    ancestor_marks = ancestry(group_parents)
    key_places = jnp.arange(TOKENS, dtype=jnp.int32)
    key_block = key_places // TOK_DEV
    key_offset = key_places % TOK_DEV
    key_branch = group_branches.reshape(TOKENS)
    keys_wide = group_keys.astype(jnp.float32).reshape(TOKENS, KV_HEADS, HEAD_DIM)
    values_wide = group_values.astype(jnp.float32).reshape(TOKENS, KV_HEADS, HEAD_DIM)
    score_scale = 1.0 / math.sqrt(HEAD_DIM)

    def one_block(block_index):
        first_row = (block_index * TOK_DEV).astype(jnp.int32)
        query_rows = lax.dynamic_slice_in_dim(group_queries, first_row, TOK_DEV, 0).astype(jnp.float32)
        query_rows = query_rows.reshape(TOK_DEV, KV_HEADS, QUERY_HEADS // KV_HEADS, HEAD_DIM)
        query_branch = lax.dynamic_slice_in_dim(key_branch, first_row, TOK_DEV, 0)
        query_offset = jnp.arange(TOK_DEV, dtype=jnp.int32)
        ancestor_columns = ancestor_marks[block_index][key_block]
        same_block = (key_block == block_index)[None, :] & (key_offset[None, :] <= query_offset[:, None])
        same_block = same_block & ((key_branch[None, :] == query_branch[:, None]) | (key_branch[None, :] == 0))
        visible = ancestor_columns[None, :] | same_block
        scores = jnp.einsum('tkgd,skd->kgts', query_rows, keys_wide) * score_scale
        scores = jnp.where(visible[None, None], scores, NEGATIVE)
        row_top = lax.optimization_barrier(jnp.max(scores, axis=-1, keepdims=True))
        weights = jnp.exp(scores - row_top)
        denominator = lax.optimization_barrier(jnp.sum(weights, axis=-1))
        rounded = weights.astype(jnp.bfloat16).astype(jnp.float32)
        mixed_heads = jnp.einsum('kgts,skd->kgtd', rounded, values_wide) / denominator[..., None]
        return mixed_heads.transpose(2, 0, 1, 3).reshape(TOK_DEV, QUERY_HEADS * HEAD_DIM).astype(jnp.bfloat16)
    block_outputs = lax.map(one_block, jnp.arange(BLOCKS, dtype=jnp.int32))
    return block_outputs.reshape(TOKENS, QUERY_HEADS * HEAD_DIM)

def reference(queries, keys, values, output_gradient, advantages, token_branch_index, parent_of_block, adapter_down_weight, adapter_up_weight):
    attention_context = lax.map(lambda packed: group_context(*packed), (queries, keys, values, token_branch_index, parent_of_block))
    adv_unit = 1.0 / (128.0 * math.sqrt(ALL_TOKENS))
    output_cotangent = (advantages.astype(jnp.float32)[..., None] * adv_unit * output_gradient.astype(jnp.float32)).astype(jnp.bfloat16)
    flattened_context = attention_context.reshape(ALL_TOKENS, QUERY_HEADS * HEAD_DIM)
    flattened_cotangent = output_cotangent.reshape(ALL_TOKENS, MODEL_FEATURES)
    reduced_rank_state = jnp.dot(flattened_context, adapter_down_weight, preferred_element_type=jnp.float32).astype(jnp.bfloat16)
    backward_rank_path = jnp.dot(flattened_cotangent, adapter_up_weight.T, preferred_element_type=jnp.float32).astype(jnp.bfloat16)
    grad_down = jnp.dot(flattened_context.T, backward_rank_path, preferred_element_type=jnp.float32)
    grad_up = jnp.dot(reduced_rank_state.T, flattened_cotangent, preferred_element_type=jnp.float32)
    return (grad_down, grad_up)
```

```python
import functools
import math

import jax
import jax.numpy as jnp
from jax import lax
from jax.experimental import pallas as pl
from jax.experimental.pallas import tpu as pltpu
from jax.sharding import PartitionSpec as P

MESH = pl.DeviceIdType.MESH
BF16 = jnp.bfloat16
F32 = jnp.float32
D = 128
T = 256
KVH = 4
GROUP = 5
BLOCKS = 8
FEATURES = 5120
ATTN = 2560
RANK = 256
MASKED = -1e30
MIB = 1 << 20


def place():
    dp = lax.axis_index("dp")
    ctx = lax.axis_index("ctx")
    return dp // 16, (dp // 2) % 8, dp % 2, ctx // 4, ctx % 4


def device(yl, z, core, yh, x):
    return ((yl * 8 + z) * 2 + core, yh * 4 + x)


def remote(src, dst, send, recv, to):
    return pltpu.make_async_remote_copy(
        src_ref=src, dst_ref=dst, send_sem=send, recv_sem=recv, device_id=to, device_id_type=MESH
    )


def greet(devices):
    barrier = pltpu.get_barrier_semaphore()
    for to in devices:
        pl.semaphore_signal(barrier, inc=1, device_id=to, device_id_type=MESH)
    pl.semaphore_wait(barrier, len(devices))


def gather_kernel(
    adv_ref, q_hbm, k_hbm, v_hbm, og_hbm, wu_hbm, wd_hbm,
    kv_out, cot_out, bl_out, qt_out, wdt_out,
    kbuf, vbuf, own, relay, qbuf, ogbuf, wubuf, wdbuf, cotbuf, qtbuf, wdtbuf, acc,
    load_sem, store_sem, send, recv,
):
    yl, z, core, yh, x = place()
    right = device(yl, z, core, yh, (x + 1) % 4)
    left = device(yl, z, core, yh, (x + 3) % 4)
    near = device(1 - yl, z, core, yh, x)
    over = device(1 - yl, z, core, 1 - yh, x)

    loads = []
    for i, (src, dst) in enumerate(
        ((k_hbm, kbuf), (v_hbm, vbuf), (og_hbm, ogbuf), (wu_hbm, wubuf), (q_hbm, qbuf), (wd_hbm, wdbuf))
    ):
        copy = pltpu.make_async_copy(src, dst, load_sem.at[i])
        copy.start()
        loads.append(copy)

    greet((right, left, near, over))

    def link(step, h, src, dst, to):
        return remote(src, dst, send.at[step, h], recv.at[step, h], to)

    first, second = pl.ds(0, 256), pl.ds(256, 256)

    def hops(h):
        return (
            link(0, h, own.at[h], kv_out.at[1, h], right),
            link(1, h, own.at[h], kv_out.at[2, h], left),
            link(2, h, own.at[h, first], relay.at[0, h], near),
            link(3, h, own.at[h, second], relay.at[1, h], over),
            link(4, h, kv_out.at[1, h, first], kv_out.at[3, h, first], right),
            link(5, h, kv_out.at[2, h, second], kv_out.at[3, h, second], left),
            link(6, h, relay.at[0, h], kv_out.at[4, h, first], over),
            link(7, h, relay.at[1, h], kv_out.at[4, h, second], near),
            link(8, h, kv_out.at[4, h], kv_out.at[5, h], right),
            link(9, h, kv_out.at[4, h], kv_out.at[6, h], left),
            link(10, h, kv_out.at[3, h, first], relay.at[2, h], near),
            link(11, h, kv_out.at[3, h, second], relay.at[3, h], over),
            link(12, h, relay.at[2, h], kv_out.at[7, h, first], over),
            link(13, h, relay.at[3, h], kv_out.at[7, h, second], near),
        )

    copies = [hops(h) for h in range(KVH)]
    loads[0].wait()
    loads[1].wait()

    def prepare(h):
        own[h, 0:256, :] = kbuf[:, h * D:(h + 1) * D]
        for part in range(2):
            piece = vbuf[part * 128:(part + 1) * 128, h * D:(h + 1) * D]
            own[h, 256 + part * 128:384 + part * 128, :] = piece.astype(F32).T.astype(BF16)

    wide = FEATURES // 8

    def cotangent(part):
        if part == 0:
            loads[2].wait()
            loads[3].wait()
        scale = adv_ref[...].astype(F32) * (1.0 / (128.0 * 256.0))
        column = jnp.broadcast_to(scale, (128, T)).T
        cols = pl.ds(part * wide, wide)
        for i in range(wide // 128):
            at = part * wide + i * 128
            cotbuf[:, at:at + 128] = (column * ogbuf[:, at:at + 128].astype(F32)).astype(BF16)
        term = lax.dot_general(
            cotbuf[:, cols], wubuf[:, cols], (((1,), (1,)), ((), ())), preferred_element_type=F32
        )
        if part == 0:
            acc[...] = term
        else:
            acc[...] += term

    def turn_queries():
        loads[4].wait()

        @pl.loop(0, ATTN // D)
        def _(i):
            at = pl.multiple_of(i * D, D)
            qtbuf[pl.ds(at, D), :] = qbuf[:, pl.ds(at, D)].astype(F32).T.astype(BF16)

    def turn_down():
        loads[5].wait()
        for h in range(KVH):

            @pl.loop(0, GROUP)
            def _(i):
                at = pl.multiple_of(i * D, D)
                rows = pl.ds(pl.multiple_of(h * GROUP * D + i * D, D), D)
                wdtbuf[h, :, pl.ds(at, D)] = wdbuf[rows, :].astype(F32).T.astype(BF16)

    stores = []

    def store(src, dst):
        copy = pltpu.make_async_copy(src, dst, store_sem.at[len(stores)])
        copy.start()
        stores.append(copy)

    for turn in range(KVH + 4):
        h = turn - 3
        if 0 <= h < KVH:
            for got, then in ((10, 12), (11, 13)):
                copies[h][got].wait_recv()
                copies[h][then].start()
        h = turn - 2
        if 0 <= h < KVH:
            copies[h][6].wait_recv()
            copies[h][7].wait_recv()
            copies[h][8].start()
            copies[h][9].start()
            copies[h][4].wait_recv()
            copies[h][10].start()
            copies[h][5].wait_recv()
            copies[h][11].start()
        h = turn - 1
        if 0 <= h < KVH:
            for got, then in ((0, 4), (1, 5), (2, 6), (3, 7)):
                copies[h][got].wait_recv()
                copies[h][then].start()
        if turn < KVH:
            prepare(turn)
            for step in range(4):
                copies[turn][step].start()
        if turn < 4:
            cotangent(2 * turn)
            cotangent(2 * turn + 1)
        if turn == 3:
            store(own, kv_out.at[0])
            store(cotbuf, cot_out)
            bl_out[...] = acc[...].astype(BF16)
        if turn == 4:
            turn_queries()
            store(qtbuf, qt_out)
        if turn == 5:
            turn_down()
            store(wdtbuf, wdt_out)

    for h in range(KVH):
        for step in (8, 9, 12, 13):
            copies[h][step].wait_recv()
    for h in range(KVH):
        for step in range(14):
            copies[h][step].wait_send()
    for copy in stores:
        copy.wait()


def gather(adv, q, k, v, og, wu, wd):
    anywhere = pl.BlockSpec(memory_space=pl.ANY)
    vmem = pl.BlockSpec(memory_space=pltpu.VMEM)
    return pl.pallas_call(
        gather_kernel,
        name="gather",
        out_shape=(
            jax.ShapeDtypeStruct((BLOCKS, KVH, 512, D), BF16),
            jax.ShapeDtypeStruct((T, FEATURES), BF16),
            jax.ShapeDtypeStruct((T, RANK), BF16),
            jax.ShapeDtypeStruct((ATTN, T), BF16),
            jax.ShapeDtypeStruct((KVH, RANK, GROUP * D), BF16),
        ),
        in_specs=[vmem] + [anywhere] * 6,
        out_specs=(anywhere, anywhere, vmem, anywhere, anywhere),
        scratch_shapes=[
            pltpu.VMEM((T, KVH * D), BF16),
            pltpu.VMEM((T, KVH * D), BF16),
            pltpu.VMEM((KVH, 512, D), BF16),
            pltpu.VMEM((4, KVH, 256, D), BF16),
            pltpu.VMEM((T, ATTN), BF16),
            pltpu.VMEM((T, FEATURES), BF16),
            pltpu.VMEM((RANK, FEATURES), BF16),
            pltpu.VMEM((ATTN, RANK), BF16),
            pltpu.VMEM((T, FEATURES), BF16),
            pltpu.VMEM((ATTN, T), BF16),
            pltpu.VMEM((KVH, RANK, GROUP * D), BF16),
            pltpu.VMEM((T, RANK), F32),
            pltpu.SemaphoreType.DMA((6,)),
            pltpu.SemaphoreType.DMA((4,)),
            pltpu.SemaphoreType.DMA((14, KVH)),
            pltpu.SemaphoreType.DMA((14, KVH)),
        ],
        compiler_params=pltpu.CompilerParams(
            collective_id=0, has_side_effects=True, vmem_limit_bytes=40 * MIB
        ),
    )(adv, q, k, v, og, wu, wd)


def attend_kernel(
    parents, branch_ref, qt_ref, bl_ref, kv_hbm, cot_hbm, wdt_hbm,
    g_ref,
    kv, cot, wdt, scores, bias, top, total, out, ctx_t, low, flags, slots,
    kv_sem, load_sem,
):
    ctx = lax.axis_index("ctx")
    yh, x = ctx // 4, ctx % 4
    for b in range(BLOCKS):
        flags[b] = 0
    cur = ctx
    for _ in range(BLOCKS):
        cur = parents[0, cur]
        flags[cur] = 1
    slots[0] = 0
    count = jnp.int32(1)
    for s in range(1, BLOCKS):
        row = yh if s < 4 else 1 - yh
        block = row * 4 + (x + (0, 3, 1, 2)[s % 4]) % 4
        slots[count] = s
        count = count + jnp.where(block == ctx, 0, flags[block])

    def fetch(i):
        return pltpu.make_async_copy(kv_hbm.at[slots[i]], kv.at[i], kv_sem.at[i])

    def start(i, carry):
        fetch(i).start()
        return carry

    lax.fori_loop(0, count, start, 0)
    load_wdt = pltpu.make_async_copy(wdt_hbm, wdt, load_sem.at[0])
    load_wdt.start()
    load_cot = pltpu.make_async_copy(cot_hbm, cot, load_sem.at[1])
    load_cot.start()

    key_pos = lax.broadcasted_iota(jnp.int32, (T, T), 0)
    query_pos = lax.broadcasted_iota(jnp.int32, (T, T), 1)
    of_query = jnp.broadcast_to(branch_ref[...].astype(F32), (T, T))
    of_key = of_query.T
    seen = (key_pos <= query_pos) & ((of_key == of_query) | (of_key == 0.0))
    bias[...] = jnp.where(seen, 0.0, MASKED)
    factor = math.log2(math.e) / math.sqrt(D)

    def wait_kv(i, carry):
        fetch(i).wait()
        return carry

    lax.fori_loop(0, count, wait_kv, 0)
    low[...] = jnp.zeros_like(low)

    def head(h, carry):
        def score(i, g):
            rows = pl.ds(pl.multiple_of((h * GROUP + g) * D, D), D)
            return jnp.dot(kv[i, h, 0:256, :], qt_ref[rows, :], preferred_element_type=F32) * factor

        for g in range(GROUP):
            s = score(0, g) + bias[...]
            scores[0, g] = s
            top[g] = jnp.max(s.reshape(T // 8, 8, T), axis=0)

        def first(i, inner):
            for g in range(GROUP):
                s = score(i, g)
                scores[i, g] = s
                top[g] = jnp.maximum(top[g], jnp.max(s.reshape(T // 8, 8, T), axis=0))
            return inner

        lax.fori_loop(1, count, first, 0)
        for g in range(GROUP):
            top[g] = jnp.broadcast_to(jnp.max(top[g], axis=0, keepdims=True), (8, T))
            total[g] = jnp.zeros((8, T), F32)
            out[g] = jnp.zeros((D, T), F32)

        def second(i, inner):
            vt = jnp.concatenate([kv[i, h, 256:384, :], kv[i, h, 384:512, :]], axis=1)
            for g in range(GROUP):
                w = jnp.exp2(scores[i, g].reshape(T // 8, 8, T) - top[g][None])
                total[g] += jnp.sum(w, axis=0)
                out[g] += jnp.dot(vt, w.reshape(T, T).astype(BF16), preferred_element_type=F32)
            return inner

        lax.fori_loop(0, count, second, 0)
        for g in range(GROUP):
            bottom = jnp.sum(total[g], axis=0, keepdims=True)
            ctx_t[g * D:(g + 1) * D, :] = (out[g] / bottom).astype(BF16)

        @pl.when(h == 0)
        def _():
            load_wdt.wait()

        low[...] += jnp.dot(wdt[h], ctx_t[...], preferred_element_type=F32)
        down = jnp.dot(ctx_t[...], bl_ref[...], preferred_element_type=F32).astype(BF16)
        for half in range(2):
            for part in range(2):
                g_ref[part, 2 * h + half, 0:320, :] = down[
                    half * 320:(half + 1) * 320, part * 128:(part + 1) * 128
                ]
        return carry

    lax.fori_loop(0, KVH, head, 0)
    low_t = low[...].astype(BF16)
    load_cot.wait()

    def up_terms(c, carry):
        cols = pl.ds(pl.multiple_of(c * 640, 128), 640)
        up = jnp.dot(low_t, cot[:, cols], preferred_element_type=F32).astype(BF16)
        for part in range(2):
            for j in range(5):
                g_ref[part, c, 320 + j * 128:448 + j * 128, :] = up[
                    part * 128:(part + 1) * 128, j * 128:(j + 1) * 128
                ]
        return carry

    lax.fori_loop(0, BLOCKS, up_terms, 0)


def attend(parents, branch, qt, bl, kv, cot, wdt):
    anywhere = pl.BlockSpec(memory_space=pl.ANY)
    vmem = pl.BlockSpec(memory_space=pltpu.VMEM)
    return pl.pallas_call(
        attend_kernel,
        name="attend",
        out_shape=jax.ShapeDtypeStruct((2, BLOCKS, 960, 128), BF16),
        in_specs=[pl.BlockSpec(memory_space=pltpu.SMEM), vmem, vmem, vmem, anywhere, anywhere, anywhere],
        out_specs=vmem,
        scratch_shapes=[
            pltpu.VMEM((BLOCKS, KVH, 512, D), BF16),
            pltpu.VMEM((T, FEATURES), BF16),
            pltpu.VMEM((KVH, RANK, GROUP * D), BF16),
            pltpu.VMEM((BLOCKS, GROUP, T, T), F32),
            pltpu.VMEM((T, T), F32),
            pltpu.VMEM((GROUP, 8, T), F32),
            pltpu.VMEM((GROUP, 8, T), F32),
            pltpu.VMEM((GROUP, D, T), F32),
            pltpu.VMEM((GROUP * D, T), BF16),
            pltpu.VMEM((RANK, T), F32),
            pltpu.SMEM((BLOCKS,), jnp.int32),
            pltpu.SMEM((BLOCKS + 1,), jnp.int32),
            pltpu.SemaphoreType.DMA((BLOCKS,)),
            pltpu.SemaphoreType.DMA((2,)),
        ],
        compiler_params=pltpu.CompilerParams(vmem_limit_bytes=48 * MIB),
    )(parents, branch, qt, bl, kv, cot, wdt)


class Ring:
    def __init__(self, plus, minus, parts, bufs, send, recv):
        self.opposite, self.plus_part, self.minus_part = parts
        opp_a, opp_b, dir_a, dir_b, sum_a, sum_b, out_a, out_b = bufs
        self.bufs = bufs
        oa, ob = self.opposite
        pa, pb = self.plus_part
        ma, mb = self.minus_part
        link = lambda i, src, dst, to: remote(src, dst, send.at[i], recv.at[i], to)
        self.copies = (
            link(0, oa, opp_a, plus),
            link(1, ob, opp_b, minus),
            link(2, pb, dir_b, plus),
            link(3, ma, dir_a, minus),
            link(4, out_a, sum_a, plus),
            link(5, out_b, sum_b, minus),
        )

    def begin(self):
        for copy in self.copies[:4]:
            copy.start()

    def middle(self):
        opp_a, opp_b, _, _, _, _, out_a, out_b = self.bufs
        self.copies[0].wait_recv()
        out_a[...] = (self.plus_part[0][...].astype(F32) + opp_a[...].astype(F32)).astype(BF16)
        self.copies[4].start()
        self.copies[1].wait_recv()
        out_b[...] = (self.minus_part[1][...].astype(F32) + opp_b[...].astype(F32)).astype(BF16)
        self.copies[5].start()

    def end(self, own_a, own_b):
        _, _, dir_a, dir_b, sum_a, sum_b, _, _ = self.bufs
        for i in (2, 3, 4, 5):
            self.copies[i].wait_recv()
        a = own_a[...].astype(F32) + dir_a[...].astype(F32) + sum_a[...].astype(F32)
        b = own_b[...].astype(F32) + dir_b[...].astype(F32) + sum_b[...].astype(F32)
        return a, b

    def finish(self):
        for copy in self.copies:
            copy.wait_send()


def reduce_kernel(
    g_hbm,
    down_ref, up_ref,
    mine, theirs, terms, halves_x, halves_y, left_x, left_y, quarter, pieces, final, rows,
    x1, y1, x2, y2,
    own_sem, core_send, core_recv, ring_send, ring_recv, z_send, z_recv, out_send, out_recv,
):
    yl, z, core, yh, x = place()
    right = device(yl, z, core, yh, (x + 1) % 4)
    left = device(yl, z, core, yh, (x + 3) % 4)
    near = device(1 - yl, z, core, yh, x)
    twin = device(yl, z, 1 - core, yh, x)
    y = yh * 2 + yl
    yp, ym = (y + 1) % 4, (y + 3) % 4
    up_dev = device(yp % 2, z, core, yp // 2, x)
    down_dev = device(ym % 2, z, core, ym // 2, x)
    peers = [device(yl, (z + d) % 8, core, yh, x) for d in range(1, 8)]

    own_copy = pltpu.make_async_copy(g_hbm.at[core], mine, own_sem)
    own_copy.start()
    greet([right, left, up_dev, down_dev, twin] + peers)

    order = []
    for step in (2, 1, 3, 0):
        for row in range(2):
            order.append((row, (x + step) % 4))
    core_copies = []
    for i, (row, col) in enumerate(order):
        c = row * 4 + col
        copy = remote(g_hbm.at[1 - core, c], theirs.at[c], core_send.at[i], core_recv.at[i], twin)
        copy.start()
        core_copies.append(copy)
    own_copy.wait()
    for i, (row, col) in enumerate(order):
        c = row * 4 + col
        core_copies[i].wait_recv()
        terms[row, col] = (mine[c].astype(F32) + theirs[c].astype(F32)).astype(BF16)

    xo, xp, xm = (x + 2) % 4, (x + 1) % 4, (x + 3) % 4
    lo, hi = pl.ds(0, 240), pl.ds(240, 240)

    def by_x(col):
        return terms.at[:, col, lo], terms.at[:, col, hi]

    def by_y(at):
        band = pl.ds(pl.multiple_of(480 + (at % 2) * 240, 16), 240)
        return terms.at[at // 2, pl.ds(0, 2), band], terms.at[at // 2, pl.ds(2, 2), band]

    yo = (y + 2) % 4
    ring_x = Ring(
        right, left, (by_x(xo), by_x(xp), by_x(xm)), [x1.at[i] for i in range(8)], ring_send.at[0], ring_recv.at[0]
    )
    ring_y = Ring(
        up_dev, down_dev, (by_y(yo), by_y(yp), by_y(ym)), [y1.at[i] for i in range(8)], ring_send.at[1], ring_recv.at[1]
    )
    ring_x.begin()
    ring_y.begin()
    ring_x.middle()
    ring_y.middle()
    a, b = ring_x.end(*by_x(x))
    left_x[:, 0:240, :] = a.astype(BF16)
    left_x[:, 240:480, :] = b.astype(BF16)

    a_rows, b_rows = pl.ds(0, 128), pl.ds(128, 112)

    def x_by_y(at):
        start = (at % 2) * 240
        return (
            left_x.at[at // 2, pl.ds(pl.multiple_of(start, 16), 128)],
            left_x.at[at // 2, pl.ds(pl.multiple_of(start + 128, 16), 112)],
        )

    def y_by_x(col):
        return left_y.at[col, a_rows], left_y.at[col, b_rows]

    def split(buf):
        return [buf.at[i, pl.ds(0, 128 if i % 2 == 0 else 112)] for i in range(8)]

    ring_xy = Ring(
        up_dev, down_dev, (x_by_y(yo), x_by_y(yp), x_by_y(ym)), split(x2), ring_send.at[2], ring_recv.at[2]
    )
    ring_yx = Ring(
        right, left, (y_by_x(xo), y_by_x(xp), y_by_x(xm)), split(y2), ring_send.at[3], ring_recv.at[3]
    )
    ring_xy.begin()
    a, b = ring_y.end(*by_y(y))
    left_y[0:2] = a.astype(BF16)
    left_y[2:4] = b.astype(BF16)
    ring_yx.begin()
    ring_xy.middle()
    ring_yx.middle()
    a, b = ring_xy.end(*x_by_y(y))
    quarter[0:128] = a.astype(BF16)
    quarter[128:240] = b.astype(BF16)
    a, b = ring_yx.end(*y_by_x(x))
    quarter[240:368] = a.astype(BF16)
    quarter[368:480] = b.astype(BF16)
    quarter[480:512] = jnp.zeros((32, 128), BF16)

    def chunk(at):
        return pl.ds(pl.multiple_of(at * 64, 64), 64)

    z_copies = []
    for d in range(1, 8):
        copy = remote(
            quarter.at[chunk((z + d) % 8)], pieces.at[d - 1], z_send.at[0, d - 1], z_recv.at[0, d - 1], peers[d - 1]
        )
        copy.start()
        z_copies.append(copy)
    piece = quarter[chunk(z), :].astype(F32)
    for d in range(1, 8):
        z_copies[d - 1].wait_recv()
        piece = piece + pieces[d - 1].astype(F32)
    final[core, yl, chunk(z), :] = piece.astype(BF16)
    for d in range(1, 8):
        here = final.at[core, yl, chunk(z)]
        copy = remote(here, here, z_send.at[1, d - 1], z_recv.at[1, d - 1], peers[d - 1])
        copy.start()
        z_copies.append(copy)
    for d in range(1, 8):
        z_copies[6 + d].wait_recv()

    here = final.at[core, yl]
    to_near = remote(here, here, out_send.at[0], out_recv.at[0], near)
    to_near.start()
    to_twin = remote(here, here, out_send.at[1], out_recv.at[1], twin)
    to_twin.start()
    there = final.at[core, 1 - yl]
    to_near.wait_recv()
    on_twin = remote(there, there, out_send.at[2], out_recv.at[2], twin)
    on_twin.start()
    to_twin.wait_recv()
    on_twin.wait_recv()

    for k in range(2):
        for band in range(2):
            rows[k, band * 240:band * 240 + 240, :] = final[k, band, 0:240, :].astype(F32)
            rows[k, 480 + band * 240:720 + band * 240, :] = final[k, band, 240:480, :].astype(F32)
    for k in range(2):
        down_ref[:, k * 128:(k + 1) * 128] = rows[k, 0:320, :]
        for j in range(5):
            up_ref[k * 128:(k + 1) * 128, j * 128:(j + 1) * 128] = rows[k, 320 + j * 128:448 + j * 128, :]

    for copy in core_copies + z_copies + [to_near, to_twin, on_twin]:
        copy.wait_send()
    for ring in (ring_x, ring_y, ring_xy, ring_yx):
        ring.finish()


def reduce_terms(g):
    vmem = pl.BlockSpec(memory_space=pltpu.VMEM)
    return pl.pallas_call(
        reduce_kernel,
        name="reduce",
        out_shape=(
            jax.ShapeDtypeStruct((320, RANK), F32),
            jax.ShapeDtypeStruct((RANK, 640), F32),
        ),
        in_specs=[pl.BlockSpec(memory_space=pl.ANY)],
        out_specs=(vmem, vmem),
        scratch_shapes=[
            pltpu.VMEM((BLOCKS, 960, 128), BF16),
            pltpu.VMEM((BLOCKS, 960, 128), BF16),
            pltpu.VMEM((2, 4, 960, 128), BF16),
            pltpu.VMEM((8, 128), BF16),
            pltpu.VMEM((8, 128), BF16),
            pltpu.VMEM((2, 480, 128), BF16),
            pltpu.VMEM((4, 240, 128), BF16),
            pltpu.VMEM((512, 128), BF16),
            pltpu.VMEM((7, 64, 128), BF16),
            pltpu.VMEM((2, 2, 512, 128), BF16),
            pltpu.VMEM((2, 960, 128), F32),
            pltpu.VMEM((8, 2, 240, 128), BF16),
            pltpu.VMEM((8, 2, 240, 128), BF16),
            pltpu.VMEM((8, 128, 128), BF16),
            pltpu.VMEM((8, 128, 128), BF16),
            pltpu.SemaphoreType.DMA,
            pltpu.SemaphoreType.DMA((8,)),
            pltpu.SemaphoreType.DMA((8,)),
            pltpu.SemaphoreType.DMA((4, 6)),
            pltpu.SemaphoreType.DMA((4, 6)),
            pltpu.SemaphoreType.DMA((2, 7)),
            pltpu.SemaphoreType.DMA((2, 7)),
            pltpu.SemaphoreType.DMA((3,)),
            pltpu.SemaphoreType.DMA((3,)),
        ],
        compiler_params=pltpu.CompilerParams(
            collective_id=1, has_side_effects=True, vmem_limit_bytes=40 * MIB
        ),
    )(g)


def on_device(q, k, v, og, adv, branch, parents, wd, wu):
    kv, cot, bl, qt, wdt = gather(adv, q[0], k[0], v[0], og[0], wu, wd)
    g = attend(parents, branch[0], qt, bl, kv, cot, wdt)
    return reduce_terms(g)


def solution(mesh):
    return jax.shard_map(
        on_device,
        mesh=mesh,
        in_specs=(
            P("dp", "ctx", None),
            P("dp", "ctx", None),
            P("dp", "ctx", None),
            P("dp", "ctx", None),
            P("dp", "ctx"),
            P("dp", "ctx", None),
            P("dp", None),
            P(),
            P(),
        ),
        out_specs=(P("ctx", None), P(None, "ctx")),
        check_vma=False,
    )
```

```python
import math

import jax
import jax.numpy as jnp
from jax import lax
from jax.experimental import pallas as pl
from jax.experimental.pallas import tpu as pltpu
from jax.sharding import PartitionSpec as P

MESH = pl.DeviceIdType.MESH
BF16 = jnp.bfloat16
F32 = jnp.float32
D = 128
T = 256
KVH = 4
GROUP = 5
BLOCKS = 8
FEATURES = 5120
ATTN = 2560
RANK = 256
MASKED = -1e30
MIB = 1 << 20
FACTOR = math.log2(math.e) / math.sqrt(D)


def place():
    dp = lax.axis_index("dp")
    ctx = lax.axis_index("ctx")
    return dp // 16, (dp // 2) % 8, dp % 2, ctx // 4, ctx % 4


def device(yl, z, core, yh, x):
    return ((yl * 8 + z) * 2 + core, yh * 4 + x)


def remote(src, dst, send, recv, to):
    return pltpu.make_async_remote_copy(
        src_ref=src, dst_ref=dst, send_sem=send, recv_sem=recv, device_id=to, device_id_type=MESH
    )


def rows16(start, size):
    return pl.ds(pl.multiple_of(start, 16), size)


class Ring:
    def __init__(self, plus, minus, parts, bufs, send, recv):
        self.opposite, self.plus_part, self.minus_part, self.own = parts
        self.bufs = bufs
        opp_a, opp_b, dir_a, dir_b, sum_a, sum_b, out_a, out_b = bufs
        self.copies = tuple(
            remote(src, dst, send.at[i], recv.at[i], to)
            for i, (src, dst, to) in enumerate((
                (self.opposite[0], opp_a, plus),
                (self.opposite[1], opp_b, minus),
                (self.plus_part[1], dir_b, plus),
                (self.minus_part[0], dir_a, minus),
                (out_a, sum_a, plus),
                (out_b, sum_b, minus),
            ))
        )

    def start(self, *which):
        for i in which:
            self.copies[i].start()

    def middle(self):
        opp_a, opp_b, _, _, _, _, out_a, out_b = self.bufs
        self.copies[0].wait_recv()
        out_a[...] = (self.plus_part[0][...].astype(F32) + opp_a[...].astype(F32)).astype(BF16)
        self.copies[4].start()
        self.copies[1].wait_recv()
        out_b[...] = (self.minus_part[1][...].astype(F32) + opp_b[...].astype(F32)).astype(BF16)
        self.copies[5].start()

    def end(self):
        _, _, dir_a, dir_b, sum_a, sum_b, _, _ = self.bufs
        for i in (2, 3, 4, 5):
            self.copies[i].wait_recv()
        a = self.own[0][...].astype(F32) + dir_a[...].astype(F32) + sum_a[...].astype(F32)
        b = self.own[1][...].astype(F32) + dir_b[...].astype(F32) + sum_b[...].astype(F32)
        return a, b

    def finish(self):
        for copy in self.copies:
            copy.wait_send()


class Direct:
    def __init__(self, opposite, plus, minus, parts, bufs, send, recv):
        self.own = parts[3]
        self.bufs = bufs
        self.copies = tuple(
            remote(parts[i], bufs.at[i], send.at[i], recv.at[i], to)
            for i, to in enumerate((opposite, plus, minus))
        )

    def begin(self):
        for copy in self.copies:
            copy.start()

    def end(self):
        total = self.own[...].astype(F32)
        for i in (1, 2, 0):
            self.copies[i].wait_recv()
            total = total + self.bufs[i].astype(F32)
        return total

    def finish(self):
        for copy in self.copies:
            copy.wait_send()


SLOT_ROW = (0, 0, 0, 1, 0, 1, 1, 1)
SLOT_STEP = (0, 3, 1, 0, 2, 3, 1, 2)


def kernel(
    parents, adv_ref, branch_ref, q_hbm, k_hbm, v_hbm, og_hbm, wu_hbm, wd_hbm,
    down_ref, up_ref,
    kbuf, vbuf, kv, qbuf, qt, ogbuf, wubuf, wdbuf, wdt, cot, cot2, acc, blh, bl2, ctx_t, ctx2, low, lowh, low2,
    scores, top, bias, vt, offs,
    downb, zin, zs, zin2, fdown,
    terms, x1, y1, left_x, left_y, x2, y2, quarter, pieces, final, rows,
    load_sem, kv_send, kv_recv, core_send, core_recv, z1_send, z1_recv, z2_send, z2_recv, z4_send, z4_recv,
    ring_send, ring_recv, dir_send, dir_recv, z_send, z_recv, out_send, out_recv,
):
    yl, z, core, yh, x = place()
    y = yh * 2 + yl
    xp, xm, xo = (x + 1) % 4, (x + 3) % 4, (x + 2) % 4
    yp, ym, yo = (y + 1) % 4, (y + 3) % 4, (y + 2) % 4

    def in_plane(to_y, to_x):
        return device(to_y % 2, z, core, to_y // 2, to_x)

    right, left = in_plane(y, xp), in_plane(y, xm)
    plus_y, minus_y, cross = in_plane(yp, x), in_plane(ym, x), in_plane(yo, x)
    near = device(1 - yl, z, core, yh, x)
    twin = device(yl, z, 1 - core, yh, x)
    peers = [device(yl, (z + d) % 8, core, yh, x) for d in range(1, 8)]
    plane = [in_plane((y + dy) % 4, (x + dx) % 4) for dy in range(4) for dx in range(4) if dy or dx]

    loads = []
    for i, (src, dst) in enumerate(
        ((k_hbm, kbuf), (v_hbm, vbuf), (og_hbm, ogbuf), (wu_hbm, wubuf), (q_hbm, qbuf), (wd_hbm, wdbuf))
    ):
        copy = pltpu.make_async_copy(src, dst, load_sem.at[i])
        copy.start()
        loads.append(copy)
    barrier = pltpu.get_barrier_semaphore()
    greeted = plane + peers + [twin]
    for to in greeted:
        pl.semaphore_signal(barrier, inc=1, device_id=to, device_id_type=MESH)

    first, second = pl.ds(0, 256), pl.ds(256, 256)

    def hops(h):
        return tuple(
            remote(src, dst, kv_send.at[i, h], kv_recv.at[i, h], to)
            for i, (src, dst, to) in enumerate((
                (kv.at[0, h], kv.at[1, h], right),
                (kv.at[0, h], kv.at[2, h], left),
                (kv.at[0, h], kv.at[3, h], cross),
                (kv.at[1, h, first], kv.at[4, h, first], right),
                (kv.at[2, h, second], kv.at[4, h, second], left),
                (kv.at[3, h], kv.at[5, h], right),
                (kv.at[3, h], kv.at[6, h], left),
                (kv.at[4, h], kv.at[7, h], cross),
            ))
        )

    links = [hops(h) for h in range(KVH)]

    def start(h, *steps):
        for i in steps:
            links[h][i].start()

    def arrived(h, *steps):
        for i in steps:
            links[h][i].wait_recv()

    loads[0].wait()
    loads[1].wait()
    for h in range(KVH):
        kv[0, h, 0:256, :] = kbuf[:, h * D:(h + 1) * D]
        for part in range(2):
            piece = vbuf[part * 128:(part + 1) * 128, h * D:(h + 1) * D]
            kv[0, h, 256 + part * 128:384 + part * 128, :] = piece.astype(F32).T.astype(BF16)
    pl.semaphore_wait(barrier, len(greeted))
    start(0, 0, 1, 2)
    start(1, 0, 1, 2)

    scale = adv_ref[...].astype(F32) * (1.0 / (128.0 * 256.0))
    column = jnp.broadcast_to(scale, (128, T)).T
    wide = FEATURES // 8

    def cotangent(part):
        cols = slice(part * wide, (part + 1) * wide)
        for at in range(part * wide, (part + 1) * wide, 128):
            cot[:, at:at + 128] = (column * ogbuf[:, at:at + 128].astype(F32)).astype(BF16)
        term = lax.dot_general(
            cot[:, cols], wubuf[:, cols], (((1,), (1,)), ((), ())), preferred_element_type=F32
        )
        if part == 0:
            acc[...] = term
        else:
            acc[...] += term

    loads[2].wait()
    loads[3].wait()
    for part in range(4):
        cotangent(part)
    arrived(0, 0, 1, 2)
    start(0, 3, 4, 5, 6)
    for part in range(4, 8):
        cotangent(part)
    for half in range(2):
        blh[half] = acc[:, half * 128:(half + 1) * 128].astype(BF16)
    cot_copy = remote(cot, cot2, core_send.at[0], core_recv.at[0], twin)
    cot_copy.start()
    bl_copy = remote(blh.at[1 - core], bl2, core_send.at[1], core_recv.at[1], twin)
    bl_copy.start()

    loads[4].wait()

    @pl.loop(0, ATTN // D)
    def _(i):
        at = pl.multiple_of(i * D, D)
        qt[pl.ds(at, D), :] = qbuf[:, pl.ds(at, D)].astype(F32).T.astype(BF16)

    arrived(1, 0, 1, 2)
    start(2, 0, 1, 2)
    start(1, 3, 4, 5, 6)
    arrived(0, 3, 4)
    start(0, 7)

    loads[5].wait()
    for h in range(KVH):

        @pl.loop(0, GROUP)
        def _(i):
            at = pl.multiple_of(i * D, D)
            wdt[h, :, pl.ds(at, D)] = wdbuf[
                pl.ds(pl.multiple_of(h * GROUP * D + i * D, D), D), :
            ].astype(F32).T.astype(BF16)

    ctx = yh * 4 + x
    marked = [jnp.int32(0)] * BLOCKS
    cur = ctx
    for _ in range(BLOCKS):
        cur = parents[0, cur]
        marked = [jnp.where(cur == b, 1, marked[b]) for b in range(BLOCKS)]
    for s in range(1, BLOCKS):
        block = (yh if SLOT_ROW[s] == 0 else 1 - yh) * 4 + (x + SLOT_STEP[s]) % 4
        seen = jnp.int32(0)
        for b in range(BLOCKS):
            seen = jnp.where(block == b, marked[b], seen)
        offs[s] = jnp.where(seen > 0, 0.0, MASKED)
    key_pos = lax.broadcasted_iota(jnp.int32, (T, T), 0)
    query_pos = lax.broadcasted_iota(jnp.int32, (T, T), 1)
    of_query = jnp.broadcast_to(branch_ref[...].astype(F32), (T, T))
    of_key = of_query.T
    local = (key_pos <= query_pos) & ((of_key == of_query) | (of_key == 0.0))
    bias[...] = jnp.where(local, 0.0, MASKED)

    def score(h, *slots):
        for s in slots:
            for g in range(GROUP):
                at = (h * GROUP + g) * D
                value = jnp.dot(kv[s, h, 0:256, :], qt[at:at + D, :], preferred_element_type=F32)
                if s == 0:
                    value = value + bias[...]
                scores[s, g] = value
                peak = jnp.max(value.reshape(T // 8, 8, T), axis=0)
                top[g] = peak if s == 0 else jnp.maximum(top[g], peak + offs[s])

    def weigh(h):
        for s in range(BLOCKS):
            vt[:, s * T:s * T + 128] = kv[s, h, 256:384, :]
            vt[:, s * T + 128:(s + 1) * T] = kv[s, h, 384:512, :]
        for g in range(GROUP):
            peak = jnp.max(top[g], axis=0, keepdims=True) * FACTOR
            total = jnp.zeros((8, T), F32)
            out = jnp.zeros((D, T), F32)
            for s in range(BLOCKS):
                shift = peak if s == 0 else peak - offs[s]
                weight = jnp.exp2(scores[s, g] * FACTOR - shift)
                total = total + jnp.sum(weight.reshape(T // 8, 8, T), axis=0)
                out = out + jnp.dot(vt[:, s * T:(s + 1) * T], weight.astype(BF16), preferred_element_type=F32)
            bottom = jnp.sum(total, axis=0, keepdims=True)
            ctx_t[h, g * D:(g + 1) * D, :] = (out / bottom).astype(BF16)

    ctx_copies = [
        remote(ctx_t.at[h], ctx2.at[h], core_send.at[2 + h], core_recv.at[2 + h], twin) for h in range(KVH)
    ]

    def after(h):
        ctx_copies[h].start()
        term = jnp.dot(wdt[h], ctx_t[h], preferred_element_type=F32)
        if h == 0:
            low[...] = term
        else:
            low[...] += term

    def band(at):
        return rows16(at * 80, 80)

    z1 = [
        [
            remote(
                downb.at[h, band((z + d) % 8)], zin.at[h, d - 1], z1_send.at[h, d - 1], z1_recv.at[h, d - 1], peers[d - 1]
            )
            for d in range(1, 8)
        ]
        for h in range(KVH)
    ]

    def down_terms(h):
        ctx_copies[h].wait_recv()
        term = jnp.dot(ctx_t[h], blh[core], preferred_element_type=F32)
        term = term + jnp.dot(ctx2[h], bl2[...], preferred_element_type=F32)
        downb[h] = term.astype(BF16)
        for copy in z1[h]:
            copy.start()

    me = y * 4 + x
    z2 = []
    for h in range(KVH):
        for to_yl in range(2):
            to_y = (h // 2) * 2 + to_yl
            to_x = 2 * (h % 2) + z // 4
            z2.append((
                to_y * 4 + to_x != me,
                remote(zs.at[h], zin2.at[me], z2_send.at[h, to_yl], z2_recv.at[me], in_plane(to_y, to_x)),
            ))

    def band_sum(h):
        total = downb[h, band(z), :].astype(F32)
        for d in range(1, 8):
            z1[h][d - 1].wait_recv()
            total = total + zin[h, d - 1].astype(F32)
        zs[h] = total.astype(BF16)
        for elsewhere, copy in z2[2 * h:2 * h + 2]:
            pl.when(elsewhere)(copy.start)

    score(0, 0, 1, 2, 3, 4)
    arrived(0, 5, 6)
    score(0, 5, 6)
    arrived(2, 0, 1, 2)
    start(3, 0, 1, 2)
    start(2, 3, 4, 5, 6)
    arrived(1, 3, 4)
    start(1, 7)
    arrived(0, 7)
    score(0, 7)
    weigh(0)
    after(0)

    score(1, 0, 1, 2, 3, 4)
    arrived(1, 5, 6)
    score(1, 5, 6)
    arrived(3, 0, 1, 2)
    start(3, 3, 4, 5, 6)
    arrived(2, 3, 4)
    start(2, 7)
    arrived(1, 7)
    score(1, 7)
    bl_copy.wait_recv()
    weigh(1)
    after(1)
    down_terms(0)

    score(2, 0, 1, 2, 3, 4)
    arrived(2, 5, 6)
    score(2, 5, 6)
    arrived(3, 3, 4)
    start(3, 7)
    arrived(2, 7)
    score(2, 7)
    weigh(2)
    after(2)
    down_terms(1)
    band_sum(0)

    score(3, 0, 1, 2, 3, 4)
    arrived(3, 5, 6)
    score(3, 5, 6)
    arrived(3, 7)
    score(3, 7)
    down_terms(2)
    band_sum(1)
    weigh(3)
    after(3)

    for half in range(2):
        lowh[half] = low[half * 128:(half + 1) * 128, :].astype(BF16)
    low_copy = remote(lowh.at[1 - core], low2, core_send.at[6], core_recv.at[6], twin)
    low_copy.start()
    down_terms(3)
    cot_copy.wait_recv()
    low_copy.wait_recv()

    def up_terms(row, col):
        cols = pl.ds(pl.multiple_of((row * 4 + col) * 640, 128), 640)
        term = jnp.dot(lowh[core], cot[:, cols], preferred_element_type=F32)
        term = term + jnp.dot(low2[...], cot2[:, cols], preferred_element_type=F32)
        for j in range(5):
            terms[row, col, j * 128:(j + 1) * 128, :] = term[:, j * 128:(j + 1) * 128].astype(BF16)

    def by_x(col):
        return terms.at[:, col, pl.ds(0, 160)], terms.at[:, col, pl.ds(160, 160)]

    def by_y(at):
        part = rows16(320 + (at % 2) * 160, 160)
        return terms.at[at // 2, pl.ds(0, 2), part], terms.at[at // 2, pl.ds(2, 2), part]

    ring_x = Ring(
        right, left, (by_x(xo), by_x(xp), by_x(xm), by_x(x)),
        [x1.at[i] for i in range(8)], ring_send.at[0], ring_recv.at[0],
    )
    ring_y = Ring(
        plus_y, minus_y, (by_y(yo), by_y(yp), by_y(ym), by_y(y)),
        [y1.at[i] for i in range(8)], ring_send.at[1], ring_recv.at[1],
    )
    up_terms(yh, xo)
    up_terms(1 - yh, xo)
    ring_x.start(0, 1)
    up_terms(1 - yh, x)
    up_terms(1 - yh, xp)
    up_terms(1 - yh, xm)
    ring_y.start(0, 1)
    up_terms(yh, xp)
    up_terms(yh, xm)
    ring_x.start(2, 3)
    up_terms(yh, x)
    ring_y.start(2, 3)
    band_sum(2)
    ring_x.middle()
    ring_y.middle()
    band_sum(3)

    def x_by_y(at):
        return left_x.at[at // 2, rows16((at % 2) * 160, 160)]

    direct_xy = Direct(
        cross, plus_y, minus_y, (x_by_y(yo), x_by_y(yp), x_by_y(ym), x_by_y(y)), x2, dir_send.at[0], dir_recv.at[0]
    )
    direct_yx = Direct(
        in_plane(y, xo), right, left, (left_y.at[xo], left_y.at[xp], left_y.at[xm], left_y.at[x]),
        y2, dir_send.at[1], dir_recv.at[1],
    )
    a, b = ring_x.end()
    left_x[:, 0:160, :] = a.astype(BF16)
    left_x[:, 160:320, :] = b.astype(BF16)
    direct_xy.begin()
    a, b = ring_y.end()
    left_y[0:2] = a.astype(BF16)
    left_y[2:4] = b.astype(BF16)
    direct_yx.begin()

    owner = x % 2 == z // 4
    mine = 2 * yh + x // 2
    spot = final_band = rows16((z % 4) * 80, 80)
    z4 = [
        remote(fdown.at[core, spot], fdown.at[core, spot], z4_send.at[d - 1], z4_recv.at[z % 4], peers[d - 1])
        for d in range(1, 8)
    ]

    @pl.when(owner)
    def _():
        for i in range(16):

            @pl.when(i != me)
            def _():
                remote(zs.at[0], zin2.at[i], z2_send.at[0, 0], z2_recv.at[i], twin).wait_recv()

            @pl.when(i == me)
            def _():
                zin2[i] = zs[mine]

        total = zin2[0].astype(F32)
        for i in range(1, 16):
            total = total + zin2[i].astype(F32)
        fdown[core, final_band, :] = total.astype(BF16)
        for copy in z4:
            copy.start()

    quarter[0:160] = direct_xy.end().astype(BF16)
    quarter[160:320] = direct_yx.end().astype(BF16)
    quarter[320:384] = jnp.zeros((64, 128), BF16)

    def chunk(at):
        return rows16(at * 48, 48)

    z_copies = []
    for d in range(1, 8):
        copy = remote(
            quarter.at[chunk((z + d) % 8)], pieces.at[d - 1], z_send.at[0, d - 1], z_recv.at[0, d - 1], peers[d - 1]
        )
        copy.start()
        z_copies.append(copy)

    for i in range(4):
        at = pl.ds(i * 80, 80)
        part = fdown.at[core, at]

        @pl.when(jnp.logical_not(owner) | (z % 4 != i))
        def _():
            remote(part, part, z4_send.at[0], z4_recv.at[i], twin).wait_recv()

    down_out = remote(fdown.at[core], fdown.at[core], out_send.at[3], out_recv.at[3], twin)
    down_out.start()

    piece = quarter[chunk(z), :].astype(F32)
    for d in range(1, 8):
        z_copies[d - 1].wait_recv()
        piece = piece + pieces[d - 1].astype(F32)
    final[core, yl, chunk(z), :] = piece.astype(BF16)
    for d in range(1, 8):
        here = final.at[core, yl, chunk(z)]
        copy = remote(here, here, z_send.at[1, d - 1], z_recv.at[1, d - 1], peers[d - 1])
        copy.start()
        z_copies.append(copy)

    down_out.wait_recv()
    for k in range(2):
        down_ref[:, k * 128:(k + 1) * 128] = fdown[k].astype(F32)

    for d in range(1, 8):
        z_copies[6 + d].wait_recv()
    here = final.at[core, yl]
    to_near = remote(here, here, out_send.at[0], out_recv.at[0], near)
    to_near.start()
    to_twin = remote(here, here, out_send.at[1], out_recv.at[1], twin)
    to_twin.start()
    there = final.at[core, 1 - yl]
    to_near.wait_recv()
    on_twin = remote(there, there, out_send.at[2], out_recv.at[2], twin)
    on_twin.start()
    to_twin.wait_recv()
    on_twin.wait_recv()
    for k in range(2):
        for part in range(2):
            rows[k, part * 160:part * 160 + 160, :] = final[k, part, 0:160, :].astype(F32)
            rows[k, 320 + part * 160:480 + part * 160, :] = final[k, part, 160:320, :].astype(F32)
    for k in range(2):
        for j in range(5):
            up_ref[k * 128:(k + 1) * 128, j * 128:(j + 1) * 128] = rows[k, j * 128:(j + 1) * 128, :]

    for h in range(KVH):
        for copy in links[h] + tuple(z1[h]):
            copy.wait_send()
    for elsewhere, copy in z2:
        pl.when(elsewhere)(copy.wait_send)

    @pl.when(owner)
    def _():
        for copy in z4:
            copy.wait_send()

    for copy in ctx_copies + z_copies + [cot_copy, bl_copy, low_copy, down_out, to_near, to_twin, on_twin]:
        copy.wait_send()
    for ring in (ring_x, ring_y, direct_xy, direct_yx):
        ring.finish()


def on_device(q, k, v, og, adv, branch, parents, wd, wu):
    anywhere = pl.BlockSpec(memory_space=pl.ANY)
    vmem = pl.BlockSpec(memory_space=pltpu.VMEM)
    dma = pltpu.SemaphoreType.DMA
    return pl.pallas_call(
        kernel,
        name="adapter_gradients",
        out_shape=(
            jax.ShapeDtypeStruct((320, RANK), F32),
            jax.ShapeDtypeStruct((RANK, 640), F32),
        ),
        in_specs=[pl.BlockSpec(memory_space=pltpu.SMEM), vmem, vmem] + [anywhere] * 6,
        out_specs=(vmem, vmem),
        scratch_shapes=[
            pltpu.VMEM((T, KVH * D), BF16),
            pltpu.VMEM((T, KVH * D), BF16),
            pltpu.VMEM((BLOCKS, KVH, 512, D), BF16),
            pltpu.VMEM((T, ATTN), BF16),
            pltpu.VMEM((ATTN, T), BF16),
            pltpu.VMEM((T, FEATURES), BF16),
            pltpu.VMEM((RANK, FEATURES), BF16),
            pltpu.VMEM((ATTN, RANK), BF16),
            pltpu.VMEM((KVH, RANK, GROUP * D), BF16),
            pltpu.VMEM((T, FEATURES), BF16),
            pltpu.VMEM((T, FEATURES), BF16),
            pltpu.VMEM((T, RANK), F32),
            pltpu.VMEM((2, T, 128), BF16),
            pltpu.VMEM((T, 128), BF16),
            pltpu.VMEM((KVH, GROUP * D, T), BF16),
            pltpu.VMEM((KVH, GROUP * D, T), BF16),
            pltpu.VMEM((RANK, T), F32),
            pltpu.VMEM((2, 128, T), BF16),
            pltpu.VMEM((128, T), BF16),
            pltpu.VMEM((BLOCKS, GROUP, T, T), F32),
            pltpu.VMEM((GROUP, 8, T), F32),
            pltpu.VMEM((T, T), F32),
            pltpu.VMEM((D, BLOCKS * T), BF16),
            pltpu.SMEM((BLOCKS,), F32),
            pltpu.VMEM((KVH, GROUP * D, 128), BF16),
            pltpu.VMEM((KVH, 7, 80, 128), BF16),
            pltpu.VMEM((KVH, 80, 128), BF16),
            pltpu.VMEM((16, 80, 128), BF16),
            pltpu.VMEM((2, 320, 128), BF16),
            pltpu.VMEM((2, 4, 640, 128), BF16),
            pltpu.VMEM((8, 2, 160, 128), BF16),
            pltpu.VMEM((8, 2, 160, 128), BF16),
            pltpu.VMEM((2, 320, 128), BF16),
            pltpu.VMEM((4, 160, 128), BF16),
            pltpu.VMEM((3, 160, 128), BF16),
            pltpu.VMEM((3, 160, 128), BF16),
            pltpu.VMEM((384, 128), BF16),
            pltpu.VMEM((7, 48, 128), BF16),
            pltpu.VMEM((2, 2, 384, 128), BF16),
            pltpu.VMEM((2, 640, 128), F32),
            dma((6,)),
            dma((8, KVH)), dma((8, KVH)),
            dma((7,)), dma((7,)),
            dma((KVH, 7)), dma((KVH, 7)),
            dma((KVH, 2)), dma((16,)),
            dma((7,)), dma((4,)),
            dma((2, 6)), dma((2, 6)),
            dma((2, 3)), dma((2, 3)),
            dma((2, 7)), dma((2, 7)),
            dma((4,)), dma((4,)),
        ],
        compiler_params=pltpu.CompilerParams(
            collective_id=0, has_side_effects=True, vmem_limit_bytes=60 * MIB
        ),
    )(parents, adv, branch[0], q[0], k[0], v[0], og[0], wu, wd)


def solution(mesh):
    return jax.shard_map(
        on_device,
        mesh=mesh,
        in_specs=(
            P("dp", "ctx", None),
            P("dp", "ctx", None),
            P("dp", "ctx", None),
            P("dp", "ctx", None),
            P("dp", "ctx"),
            P("dp", "ctx", None),
            P("dp", None),
            P(),
            P(),
        ),
        out_specs=(P("ctx", None), P(None, "ctx")),
        check_vma=False,
    )
```

```python
import math

import jax
import jax.numpy as jnp
from jax import lax
from jax.experimental import pallas as pl
from jax.experimental.pallas import tpu as pltpu
from jax.sharding import PartitionSpec as P

MESH = pl.DeviceIdType.MESH
BF16 = jnp.bfloat16
F32 = jnp.float32
D = 128
T = 256
KVH = 4
GROUP = 5
BLOCKS = 8
FEATURES = 5120
ATTN = 2560
RANK = 256
MASKED = -1e30
MIB = 1 << 20
FACTOR = math.log2(math.e) / math.sqrt(D)


def place():
    dp = lax.axis_index("dp")
    ctx = lax.axis_index("ctx")
    return dp // 16, (dp // 2) % 8, dp % 2, ctx // 4, ctx % 4


def device(yl, z, core, yh, x):
    return ((yl * 8 + z) * 2 + core, yh * 4 + x)


def remote(src, dst, send, recv, to):
    return pltpu.make_async_remote_copy(
        src_ref=src, dst_ref=dst, send_sem=send, recv_sem=recv, device_id=to, device_id_type=MESH
    )


def rows16(start, size):
    return pl.ds(pl.multiple_of(start, 16), size)


class Ring:
    def __init__(self, plus, minus, parts, bufs, send, recv):
        self.opposite, self.plus_part, self.minus_part, self.own = parts
        self.bufs = bufs
        opp_a, opp_b, dir_a, dir_b, sum_a, sum_b, out_a, out_b = bufs
        self.copies = tuple(
            remote(src, dst, send.at[i], recv.at[i], to)
            for i, (src, dst, to) in enumerate((
                (self.opposite[0], opp_a, plus),
                (self.opposite[1], opp_b, minus),
                (self.plus_part[1], dir_b, plus),
                (self.minus_part[0], dir_a, minus),
                (out_a, sum_a, plus),
                (out_b, sum_b, minus),
            ))
        )

    def start(self, *which):
        for i in which:
            self.copies[i].start()

    def middle(self):
        opp_a, opp_b, _, _, _, _, out_a, out_b = self.bufs
        self.copies[0].wait_recv()
        out_a[...] = (self.plus_part[0][...].astype(F32) + opp_a[...].astype(F32)).astype(BF16)
        self.copies[4].start()
        self.copies[1].wait_recv()
        out_b[...] = (self.minus_part[1][...].astype(F32) + opp_b[...].astype(F32)).astype(BF16)
        self.copies[5].start()

    def end(self):
        _, _, dir_a, dir_b, sum_a, sum_b, _, _ = self.bufs
        for i in (2, 3, 4, 5):
            self.copies[i].wait_recv()
        a = self.own[0][...].astype(F32) + dir_a[...].astype(F32) + sum_a[...].astype(F32)
        b = self.own[1][...].astype(F32) + dir_b[...].astype(F32) + sum_b[...].astype(F32)
        return a, b

    def finish(self):
        for copy in self.copies:
            copy.wait_send()


class Direct:
    def __init__(self, opposite, plus, minus, parts, bufs, send, recv):
        self.own = parts[3]
        self.bufs = bufs
        self.copies = tuple(
            remote(parts[i], bufs.at[i], send.at[i], recv.at[i], to)
            for i, to in enumerate((opposite, plus, minus))
        )

    def begin(self):
        for copy in self.copies:
            copy.start()

    def end(self):
        total = self.own[...].astype(F32)
        for i in (1, 2, 0):
            self.copies[i].wait_recv()
            total = total + self.bufs[i].astype(F32)
        return total

    def finish(self):
        for copy in self.copies:
            copy.wait_send()


SLOT_ROW = (0, 0, 0, 1, 0, 1, 1, 1)
SLOT_STEP = (0, 3, 1, 0, 2, 3, 1, 2)


def kernel(
    parents, adv_ref, branch_ref, q_hbm, k_hbm, v_hbm, og_hbm, wu_hbm, wd_hbm,
    fdown, final,
    kbuf, vbuf, kv, qbuf, qt, wubuf, wdbuf, wdt, cot, cot2, acc, blh, bl2, ctx_t, ctx2, low, lowh, low2,
    scores, top, bias, vt, offs,
    downb, zin, zs, zin2,
    terms, x1, y1, left_x, left_y, x2, y2, quarter, pieces,
    load_sem, kv_send, kv_recv, core_send, core_recv, z1_send, z1_recv, z2_send, z2_recv, z4_send, z4_recv,
    ring_send, ring_recv, dir_send, dir_recv, z_send, z_recv, near_send, near_recv, out_send, out_recv,
):
    yl, z, core, yh, x = place()
    y = yh * 2 + yl
    xp, xm, xo = (x + 1) % 4, (x + 3) % 4, (x + 2) % 4
    yp, ym, yo = (y + 1) % 4, (y + 3) % 4, (y + 2) % 4

    def in_plane(to_y, to_x):
        return device(to_y % 2, z, core, to_y // 2, to_x)

    right, left = in_plane(y, xp), in_plane(y, xm)
    plus_y, minus_y, cross = in_plane(yp, x), in_plane(ym, x), in_plane(yo, x)
    near = device(1 - yl, z, core, yh, x)
    twin = device(yl, z, 1 - core, yh, x)
    peers = [device(yl, (z + d) % 8, core, yh, x) for d in range(1, 8)]
    plane = [in_plane((y + dy) % 4, (x + dx) % 4) for dy in range(4) for dx in range(4) if dy or dx]

    loads = []
    for i, (src, dst) in enumerate(
        ((k_hbm, kbuf), (v_hbm, vbuf), (og_hbm, cot), (wu_hbm, wubuf), (q_hbm, qbuf), (wd_hbm, wdbuf))
    ):
        copy = pltpu.make_async_copy(src, dst, load_sem.at[i])
        copy.start()
        loads.append(copy)
    barrier = pltpu.get_barrier_semaphore()
    greeted = plane + peers + [twin]
    for to in greeted:
        pl.semaphore_signal(barrier, inc=1, device_id=to, device_id_type=MESH)

    first, second = pl.ds(0, 256), pl.ds(256, 256)

    def hops(h):
        return tuple(
            remote(src, dst, kv_send.at[i, h], kv_recv.at[i, h], to)
            for i, (src, dst, to) in enumerate((
                (kv.at[0, h], kv.at[1, h], right),
                (kv.at[0, h], kv.at[2, h], left),
                (kv.at[0, h], kv.at[3, h], cross),
                (kv.at[1, h, first], kv.at[4, h, first], right),
                (kv.at[2, h, second], kv.at[4, h, second], left),
                (kv.at[3, h], kv.at[5, h], right),
                (kv.at[3, h], kv.at[6, h], left),
                (kv.at[4, h], kv.at[7, h], cross),
            ))
        )

    links = [hops(h) for h in range(KVH)]

    def start(h, *steps):
        for i in steps:
            links[h][i].start()

    def arrived(h, *steps):
        for i in steps:
            links[h][i].wait_recv()

    loads[0].wait()
    loads[1].wait()
    for h in range(KVH):
        kv[0, h, 0:256, :] = kbuf[:, h * D:(h + 1) * D]
        for part in range(2):
            piece = vbuf[part * 128:(part + 1) * 128, h * D:(h + 1) * D]
            kv[0, h, 256 + part * 128:384 + part * 128, :] = piece.astype(F32).T.astype(BF16)
    pl.semaphore_wait(barrier, len(greeted))
    for h in range(3):
        start(h, 0, 1, 2)

    scale = adv_ref[...].astype(F32) * (1.0 / (128.0 * 256.0))
    column = jnp.broadcast_to(scale, (128, T)).T
    wide = FEATURES // 8

    def cotangent(part):
        cols = slice(part * wide, (part + 1) * wide)
        for at in range(part * wide, (part + 1) * wide, 128):
            cot[:, at:at + 128] = (column * cot[:, at:at + 128].astype(F32)).astype(BF16)
        term = lax.dot_general(
            cot[:, cols], wubuf[:, cols], (((1,), (1,)), ((), ())), preferred_element_type=F32
        )
        if part == 0:
            acc[...] = term
        else:
            acc[...] += term

    loads[2].wait()
    loads[3].wait()
    for part in range(4):
        cotangent(part)
    arrived(0, 0, 1, 2)
    start(0, 3, 4, 5, 6)
    start(3, 0, 1, 2)
    for part in range(4, 8):
        cotangent(part)
    for half in range(2):
        blh[half] = acc[:, half * 128:(half + 1) * 128].astype(BF16)
    cot_copy = remote(cot, cot2, core_send.at[0], core_recv.at[0], twin)
    cot_copy.start()
    bl_copy = remote(blh.at[1 - core], bl2, core_send.at[1], core_recv.at[1], twin)
    bl_copy.start()
    arrived(1, 0, 1, 2)
    start(1, 3, 4)

    loads[4].wait()

    @pl.loop(0, ATTN // D)
    def _(i):
        at = pl.multiple_of(i * D, D)
        qt[pl.ds(at, D), :] = qbuf[:, pl.ds(at, D)].astype(F32).T.astype(BF16)

    arrived(2, 0, 1, 2)
    start(2, 3, 4)
    start(1, 5, 6)
    arrived(0, 3, 4)
    start(0, 7)

    loads[5].wait()
    for h in range(KVH):

        @pl.loop(0, GROUP)
        def _(i):
            at = pl.multiple_of(i * D, D)
            wdt[h, :, pl.ds(at, D)] = wdbuf[
                pl.ds(pl.multiple_of(h * GROUP * D + i * D, D), D), :
            ].astype(F32).T.astype(BF16)

    ctx = yh * 4 + x
    marked = [jnp.int32(0)] * BLOCKS
    cur = ctx
    for _ in range(BLOCKS):
        cur = parents[0, cur]
        marked = [jnp.where(cur == b, 1, marked[b]) for b in range(BLOCKS)]
    for s in range(1, BLOCKS):
        block = (yh if SLOT_ROW[s] == 0 else 1 - yh) * 4 + (x + SLOT_STEP[s]) % 4
        seen = jnp.int32(0)
        for b in range(BLOCKS):
            seen = jnp.where(block == b, marked[b], seen)
        offs[s] = jnp.where(seen > 0, 0.0, MASKED)
    key_pos = lax.broadcasted_iota(jnp.int32, (T, T), 0)
    query_pos = lax.broadcasted_iota(jnp.int32, (T, T), 1)
    of_query = jnp.broadcast_to(branch_ref[...].astype(F32), (T, T))
    of_key = of_query.T
    local = (key_pos <= query_pos) & ((of_key == of_query) | (of_key == 0.0))
    bias[...] = jnp.where(local, 0.0, MASKED)

    def score(h, *slots):
        for s in slots:
            for g in range(GROUP):
                at = (h * GROUP + g) * D
                value = jnp.dot(kv[s, h, 0:256, :], qt[at:at + D, :], preferred_element_type=F32)
                if s == 0:
                    value = value + bias[...]
                scores[h % 2, s, g] = value
                peak = jnp.max(value.reshape(T // 8, 8, T), axis=0)
                top[h % 2, g] = peak if s == 0 else jnp.maximum(top[h % 2, g], peak + offs[s])

    def weigh(h):
        for s in range(BLOCKS):
            vt[:, s * T:s * T + 128] = kv[s, h, 256:384, :]
            vt[:, s * T + 128:(s + 1) * T] = kv[s, h, 384:512, :]
        for g in range(GROUP):
            peak = jnp.max(top[h % 2, g], axis=0, keepdims=True) * FACTOR
            total = jnp.zeros((8, T), F32)
            out = jnp.zeros((D, T), F32)
            for s in range(BLOCKS):
                shift = peak if s == 0 else peak - offs[s]
                weight = jnp.exp2(scores[h % 2, s, g] * FACTOR - shift)
                total = total + jnp.sum(weight.reshape(T // 8, 8, T), axis=0)
                out = out + jnp.dot(vt[:, s * T:(s + 1) * T], weight.astype(BF16), preferred_element_type=F32)
            bottom = jnp.sum(total, axis=0, keepdims=True)
            ctx_t[h, g * D:(g + 1) * D, :] = (out / bottom).astype(BF16)

    ctx_copies = [
        remote(ctx_t.at[h], ctx2.at[h], core_send.at[2 + h], core_recv.at[2 + h], twin) for h in range(KVH)
    ]

    def after(h):
        ctx_copies[h].start()
        term = jnp.dot(wdt[h], ctx_t[h], preferred_element_type=F32)
        if h == 0:
            low[...] = term
        else:
            low[...] += term

    def band(at):
        return rows16(at * 80, 80)

    z1 = [
        [
            remote(
                downb.at[h, band((z + d) % 8)], zin.at[h, d - 1], z1_send.at[h, d - 1], z1_recv.at[h, d - 1], peers[d - 1]
            )
            for d in range(1, 8)
        ]
        for h in range(KVH)
    ]

    def down_terms(h):
        ctx_copies[h].wait_recv()
        term = jnp.dot(ctx_t[h], blh[core], preferred_element_type=F32)
        term = term + jnp.dot(ctx2[h], bl2[...], preferred_element_type=F32)
        downb[h] = term.astype(BF16)
        for copy in z1[h]:
            copy.start()

    me = y * 4 + x
    z2 = []
    for h in range(KVH):
        for to_yl in range(2):
            to_y = (h // 2) * 2 + to_yl
            to_x = 2 * (h % 2) + z // 4
            z2.append((
                to_y * 4 + to_x != me,
                remote(zs.at[h], zin2.at[me], z2_send.at[h, to_yl], z2_recv.at[me], in_plane(to_y, to_x)),
            ))

    def band_sum(h):
        total = downb[h, band(z), :].astype(F32)
        for d in range(1, 8):
            z1[h][d - 1].wait_recv()
            total = total + zin[h, d - 1].astype(F32)
        zs[h] = total.astype(BF16)
        for elsewhere, copy in z2[2 * h:2 * h + 2]:
            pl.when(elsewhere)(copy.start)

    score(0, 0, 1, 2, 3)
    arrived(3, 0, 1, 2)
    start(3, 3, 4)
    start(2, 5, 6)
    start(3, 5, 6)
    arrived(1, 3, 4)
    start(1, 7)
    score(0, 4)
    arrived(0, 5, 6)
    score(0, 5, 6)
    score(1, 0, 1, 2, 3, 4)
    arrived(2, 3, 4)
    start(2, 7)
    arrived(0, 7)
    score(0, 7)
    weigh(0)
    after(0)
    arrived(3, 3, 4)
    start(3, 7)
    arrived(1, 5, 6)
    score(1, 5, 6)
    arrived(1, 7)
    score(1, 7)
    score(2, 0, 1, 2, 3, 4)
    weigh(1)
    after(1)
    bl_copy.wait_recv()
    down_terms(0)
    arrived(2, 5, 6)
    score(2, 5, 6)
    arrived(2, 7)
    score(2, 7)
    score(3, 0, 1, 2, 3, 4)
    weigh(2)
    after(2)
    down_terms(1)
    band_sum(0)
    arrived(3, 5, 6)
    score(3, 5, 6)
    arrived(3, 7)
    score(3, 7)
    down_terms(2)
    band_sum(1)
    weigh(3)
    after(3)

    for half in range(2):
        lowh[half] = low[half * 128:(half + 1) * 128, :].astype(BF16)
    low_copy = remote(lowh.at[1 - core], low2, core_send.at[6], core_recv.at[6], twin)
    low_copy.start()
    down_terms(3)
    cot_copy.wait_recv()
    low_copy.wait_recv()

    def up_terms(row, col):
        cols = pl.ds(pl.multiple_of((row * 4 + col) * 640, 128), 640)
        term = jnp.dot(lowh[core], cot[:, cols], preferred_element_type=F32)
        term = term + jnp.dot(low2[...], cot2[:, cols], preferred_element_type=F32)
        for j in range(5):
            terms[row, col, j * 128:(j + 1) * 128, :] = term[:, j * 128:(j + 1) * 128].astype(BF16)

    def by_x(col):
        return terms.at[:, col, pl.ds(0, 160)], terms.at[:, col, pl.ds(160, 160)]

    def by_y(at):
        part = rows16(320 + (at % 2) * 160, 160)
        return terms.at[at // 2, pl.ds(0, 2), part], terms.at[at // 2, pl.ds(2, 2), part]

    ring_x = Ring(
        right, left, (by_x(xo), by_x(xp), by_x(xm), by_x(x)),
        [x1.at[i] for i in range(8)], ring_send.at[0], ring_recv.at[0],
    )
    ring_y = Ring(
        plus_y, minus_y, (by_y(yo), by_y(yp), by_y(ym), by_y(y)),
        [y1.at[i] for i in range(8)], ring_send.at[1], ring_recv.at[1],
    )
    up_terms(yh, xo)
    up_terms(1 - yh, xo)
    ring_x.start(0, 1)
    up_terms(1 - yh, x)
    up_terms(1 - yh, xp)
    up_terms(1 - yh, xm)
    ring_y.start(0, 1)
    up_terms(yh, xp)
    up_terms(yh, xm)
    ring_x.start(2, 3)
    up_terms(yh, x)
    ring_y.start(2, 3)
    band_sum(2)
    ring_x.middle()
    ring_y.middle()
    band_sum(3)

    def x_by_y(at):
        return left_x.at[at // 2, rows16((at % 2) * 160, 160)]

    direct_xy = Direct(
        cross, plus_y, minus_y, (x_by_y(yo), x_by_y(yp), x_by_y(ym), x_by_y(y)), x2, dir_send.at[0], dir_recv.at[0]
    )
    direct_yx = Direct(
        in_plane(y, xo), right, left, (left_y.at[xo], left_y.at[xp], left_y.at[xm], left_y.at[x]),
        y2, dir_send.at[1], dir_recv.at[1],
    )
    a, b = ring_x.end()
    left_x[:, 0:160, :] = a.astype(BF16)
    left_x[:, 160:320, :] = b.astype(BF16)
    direct_xy.begin()
    a, b = ring_y.end()
    left_y[0:2] = a.astype(BF16)
    left_y[2:4] = b.astype(BF16)
    direct_yx.begin()

    owner = x % 2 == z // 4
    mine = 2 * yh + x // 2
    spot = rows16((z % 4) * 80, 80)
    z4 = [
        remote(fdown.at[core, spot], fdown.at[core, spot], z4_send.at[d - 1], z4_recv.at[z % 4], peers[d - 1])
        for d in range(1, 8)
    ]

    @pl.when(owner)
    def _():
        for i in range(16):

            @pl.when(i != me)
            def _():
                remote(zs.at[0], zin2.at[i], z2_send.at[0, 0], z2_recv.at[i], twin).wait_recv()

            @pl.when(i == me)
            def _():
                zin2[i] = zs[mine]

        total = zin2[0].astype(F32)
        for i in range(1, 16):
            total = total + zin2[i].astype(F32)
        fdown[core, spot, :] = total.astype(BF16)
        for copy in z4:
            copy.start()

    quarter[0:160] = direct_xy.end().astype(BF16)
    quarter[160:320] = direct_yx.end().astype(BF16)
    quarter[320:384] = jnp.zeros((64, 128), BF16)

    def chunk(at):
        return rows16(at * 48, 48)

    z_copies = []
    for d in range(1, 8):
        copy = remote(
            quarter.at[chunk((z + d) % 8)], pieces.at[d - 1], z_send.at[0, d - 1], z_recv.at[0, d - 1], peers[d - 1]
        )
        copy.start()
        z_copies.append(copy)

    for i in range(4):
        at = pl.ds(i * 80, 80)
        part = fdown.at[core, at]

        @pl.when(jnp.logical_not(owner) | (z % 4 != i))
        def _():
            remote(part, part, z4_send.at[0], z4_recv.at[i], twin).wait_recv()

    down_out = remote(fdown.at[core], fdown.at[core], out_send.at[3], out_recv.at[3], twin)
    down_out.start()

    piece = quarter[chunk(z), :].astype(F32)
    for d in range(1, 8):
        z_copies[d - 1].wait_recv()
        piece = piece + pieces[d - 1].astype(F32)
    final[core, yl, chunk(z), :] = piece.astype(BF16)

    def to_near(d):
        here = final.at[core, yl, chunk((z + 8 - d) % 8)]
        return remote(here, here, near_send.at[d], near_recv.at[d], near)

    near_copies = [to_near(d) for d in range(8)]
    near_copies[0].start()
    for d in range(1, 8):
        here = final.at[core, yl, chunk(z)]
        copy = remote(here, here, z_send.at[1, d - 1], z_recv.at[1, d - 1], peers[d - 1])
        copy.start()
        z_copies.append(copy)

    for d in (1, 7, 2, 6, 3, 5, 4):
        z_copies[6 + d].wait_recv()
        near_copies[d].start()
    here = final.at[core, yl]
    to_twin = remote(here, here, out_send.at[1], out_recv.at[1], twin)
    to_twin.start()
    there = final.at[core, 1 - yl]
    for copy in near_copies:
        copy.wait_recv()
    on_twin = remote(there, there, out_send.at[2], out_recv.at[2], twin)
    on_twin.start()
    to_twin.wait_recv()
    on_twin.wait_recv()
    down_out.wait_recv()

    for h in range(KVH):
        for copy in links[h] + tuple(z1[h]):
            copy.wait_send()
    for elsewhere, copy in z2:
        pl.when(elsewhere)(copy.wait_send)

    @pl.when(owner)
    def _():
        for copy in z4:
            copy.wait_send()

    for copy in ctx_copies + z_copies + near_copies + [cot_copy, bl_copy, low_copy, down_out, to_twin, on_twin]:
        copy.wait_send()
    for ring in (ring_x, ring_y, direct_xy, direct_yx):
        ring.finish()


def lay_out(fdown, final, down_ref, up_ref, rows):
    for k in range(2):
        down_ref[:, k * 128:(k + 1) * 128] = fdown[k].astype(F32)
        for part in range(2):
            rows[k, part * 160:part * 160 + 160, :] = final[k, part, 0:160, :].astype(F32)
            rows[k, 320 + part * 160:480 + part * 160, :] = final[k, part, 160:320, :].astype(F32)
    for k in range(2):
        for j in range(5):
            up_ref[k * 128:(k + 1) * 128, j * 128:(j + 1) * 128] = rows[k, j * 128:(j + 1) * 128, :]


def on_device(q, k, v, og, adv, branch, parents, wd, wu):
    hbm = pl.BlockSpec(memory_space=pl.ANY)
    vmem = pl.BlockSpec(memory_space=pltpu.VMEM)
    dma = pltpu.SemaphoreType.DMA
    sums = pl.pallas_call(
        kernel,
        name="adapter_gradients",
        out_shape=(
            jax.ShapeDtypeStruct((2, 320, 128), BF16),
            jax.ShapeDtypeStruct((2, 2, 384, 128), BF16),
        ),
        in_specs=[pl.BlockSpec(memory_space=pltpu.SMEM), vmem, vmem] + [hbm] * 6,
        out_specs=(vmem, vmem),
        scratch_shapes=[
            pltpu.VMEM((T, KVH * D), BF16),
            pltpu.VMEM((T, KVH * D), BF16),
            pltpu.VMEM((BLOCKS, KVH, 512, D), BF16),
            pltpu.VMEM((T, ATTN), BF16),
            pltpu.VMEM((ATTN, T), BF16),
                pltpu.VMEM((RANK, FEATURES), BF16),
            pltpu.VMEM((ATTN, RANK), BF16),
            pltpu.VMEM((KVH, RANK, GROUP * D), BF16),
            pltpu.VMEM((T, FEATURES), BF16),
            pltpu.VMEM((T, FEATURES), BF16),
            pltpu.VMEM((T, RANK), F32),
            pltpu.VMEM((2, T, 128), BF16),
            pltpu.VMEM((T, 128), BF16),
            pltpu.VMEM((KVH, GROUP * D, T), BF16),
            pltpu.VMEM((KVH, GROUP * D, T), BF16),
            pltpu.VMEM((RANK, T), F32),
            pltpu.VMEM((2, 128, T), BF16),
            pltpu.VMEM((128, T), BF16),
            pltpu.VMEM((2, BLOCKS, GROUP, T, T), F32),
            pltpu.VMEM((2, GROUP, 8, T), F32),
            pltpu.VMEM((T, T), F32),
            pltpu.VMEM((D, BLOCKS * T), BF16),
            pltpu.SMEM((BLOCKS,), F32),
            pltpu.VMEM((KVH, GROUP * D, 128), BF16),
            pltpu.VMEM((KVH, 7, 80, 128), BF16),
            pltpu.VMEM((KVH, 80, 128), BF16),
            pltpu.VMEM((16, 80, 128), BF16),
            pltpu.VMEM((2, 4, 640, 128), BF16),
            pltpu.VMEM((8, 2, 160, 128), BF16),
            pltpu.VMEM((8, 2, 160, 128), BF16),
            pltpu.VMEM((2, 320, 128), BF16),
            pltpu.VMEM((4, 160, 128), BF16),
            pltpu.VMEM((3, 160, 128), BF16),
            pltpu.VMEM((3, 160, 128), BF16),
            pltpu.VMEM((384, 128), BF16),
            pltpu.VMEM((7, 48, 128), BF16),
            dma((6,)),
            dma((8, KVH)), dma((8, KVH)),
            dma((7,)), dma((7,)),
            dma((KVH, 7)), dma((KVH, 7)),
            dma((KVH, 2)), dma((16,)),
            dma((7,)), dma((4,)),
            dma((2, 6)), dma((2, 6)),
            dma((2, 3)), dma((2, 3)),
            dma((2, 7)), dma((2, 7)),
            dma((8,)), dma((8,)),
            dma((4,)), dma((4,)),
        ],
        compiler_params=pltpu.CompilerParams(
            collective_id=0, has_side_effects=True, vmem_limit_bytes=60 * MIB
        ),
    )(parents, adv, branch[0], q[0], k[0], v[0], og[0], wu, wd)
    return pl.pallas_call(
        lay_out,
        name="lay_out",
        out_shape=(
            jax.ShapeDtypeStruct((320, RANK), F32),
            jax.ShapeDtypeStruct((RANK, 640), F32),
        ),
        in_specs=[vmem, vmem],
        out_specs=(vmem, vmem),
        scratch_shapes=[pltpu.VMEM((2, 640, 128), F32)],
    )(*sums)


def solution(mesh):
    return jax.shard_map(
        on_device,
        mesh=mesh,
        in_specs=(
            P("dp", "ctx", None),
            P("dp", "ctx", None),
            P("dp", "ctx", None),
            P("dp", "ctx", None),
            P("dp", "ctx"),
            P("dp", "ctx", None),
            P("dp", None),
            P(),
            P(),
        ),
        out_specs=(P("ctx", None), P(None, "ctx")),
        check_vma=False,
    )
```

```python
import math

import jax
import jax.numpy as jnp
from jax import lax
from jax.experimental import pallas as pl
from jax.experimental.pallas import tpu as pltpu
from jax.sharding import PartitionSpec as P

MESH = pl.DeviceIdType.MESH
BF16 = jnp.bfloat16
F32 = jnp.float32
D = 128
T = 256
KVH = 4
GROUP = 5
BLOCKS = 8
FEATURES = 5120
ATTN = 2560
RANK = 256
MASKED = -1e30
MIB = 1 << 20
FACTOR = math.log2(math.e) / math.sqrt(D)


def place():
    dp = lax.axis_index("dp")
    ctx = lax.axis_index("ctx")
    return dp // 16, (dp // 2) % 8, dp % 2, ctx // 4, ctx % 4


def device(yl, z, core, yh, x):
    return ((yl * 8 + z) * 2 + core, yh * 4 + x)


def remote(src, dst, send, recv, to):
    return pltpu.make_async_remote_copy(
        src_ref=src, dst_ref=dst, send_sem=send, recv_sem=recv, device_id=to, device_id_type=MESH
    )


def rows16(start, size):
    return pl.ds(pl.multiple_of(start, 16), size)


class Ring:
    def __init__(self, plus, minus, parts, bufs, send, recv):
        self.opposite, self.plus_part, self.minus_part, self.own = parts
        self.bufs = bufs
        opp_a, opp_b, dir_a, dir_b, sum_a, sum_b, out_a, out_b = bufs
        self.copies = tuple(
            remote(src, dst, send.at[i], recv.at[i], to)
            for i, (src, dst, to) in enumerate((
                (self.opposite[0], opp_a, plus),
                (self.opposite[1], opp_b, minus),
                (self.plus_part[1], dir_b, plus),
                (self.minus_part[0], dir_a, minus),
                (out_a, sum_a, plus),
                (out_b, sum_b, minus),
            ))
        )

    def start(self, *which):
        for i in which:
            self.copies[i].start()

    def middle(self):
        opp_a, opp_b, _, _, _, _, out_a, out_b = self.bufs
        self.copies[0].wait_recv()
        out_a[...] = (self.plus_part[0][...].astype(F32) + opp_a[...].astype(F32)).astype(BF16)
        self.copies[4].start()
        self.copies[1].wait_recv()
        out_b[...] = (self.minus_part[1][...].astype(F32) + opp_b[...].astype(F32)).astype(BF16)
        self.copies[5].start()

    def end(self):
        _, _, dir_a, dir_b, sum_a, sum_b, _, _ = self.bufs
        for i in (2, 3, 4, 5):
            self.copies[i].wait_recv()
        a = self.own[0][...].astype(F32) + dir_a[...].astype(F32) + sum_a[...].astype(F32)
        b = self.own[1][...].astype(F32) + dir_b[...].astype(F32) + sum_b[...].astype(F32)
        return a, b

    def finish(self):
        for copy in self.copies:
            copy.wait_send()


class Direct:
    def __init__(self, opposite, plus, minus, parts, bufs, send, recv):
        self.own = parts[3]
        self.bufs = bufs
        self.copies = tuple(
            remote(parts[i], bufs.at[i], send.at[i], recv.at[i], to)
            for i, to in enumerate((opposite, plus, minus))
        )

    def begin(self):
        for copy in self.copies:
            copy.start()

    def end(self):
        total = self.own[...].astype(F32)
        for i in (1, 2, 0):
            self.copies[i].wait_recv()
            total = total + self.bufs[i].astype(F32)
        return total

    def finish(self):
        for copy in self.copies:
            copy.wait_send()


SLOT_ROW = (0, 0, 0, 1, 0, 1, 1, 1)
SLOT_STEP = (0, 3, 1, 0, 2, 3, 1, 2)


def kernel(
    parents, adv_ref, branch_ref, q_hbm, k_hbm, v_hbm, og_hbm, wu_hbm, wd_hbm,
    fdown, final,
    kbuf, vbuf, kv, qbuf, wubuf, wdbuf, wdt, cot, cot2, acc, blh, bl2, ctx_t, ctx2, low, lowh, low2,
    scores, top, bias, vt, offs,
    downb, zin, zs, zin2,
    terms, x1, y1, left_x, left_y, x2, y2, quarter, pieces,
    load_sem, kv_send, kv_recv, core_send, core_recv, z1_send, z1_recv, z2_send, z2_recv, z4_send, z4_recv,
    ring_send, ring_recv, dir_send, dir_recv, z_send, z_recv, near_send, near_recv, out_send, out_recv, met,
):
    yl, z, core, yh, x = place()
    y = yh * 2 + yl
    xp, xm, xo = (x + 1) % 4, (x + 3) % 4, (x + 2) % 4
    yp, ym, yo = (y + 1) % 4, (y + 3) % 4, (y + 2) % 4

    def in_plane(to_y, to_x):
        return device(to_y % 2, z, core, to_y // 2, to_x)

    right, left = in_plane(y, xp), in_plane(y, xm)
    plus_y, minus_y, cross = in_plane(yp, x), in_plane(ym, x), in_plane(yo, x)
    near = device(1 - yl, z, core, yh, x)
    twin = device(yl, z, 1 - core, yh, x)
    peers = [device(yl, (z + d) % 8, core, yh, x) for d in range(1, 8)]

    loads = []
    for i, (src, dst) in enumerate(
        ((k_hbm, kbuf), (v_hbm, vbuf), (og_hbm, cot), (wu_hbm, wubuf), (q_hbm, qbuf), (wd_hbm, wdbuf))
    ):
        copy = pltpu.make_async_copy(src, dst, load_sem.at[i])
        copy.start()
        loads.append(copy)
    barrier = pltpu.get_barrier_semaphore()
    beside = [right, left, plus_y, minus_y, peers[0], peers[6]]
    greeted = beside + [cross, twin]
    for to in greeted:
        pl.semaphore_signal(barrier, inc=1, device_id=to, device_id_type=MESH)

    def tell(k):
        for to in beside:
            pl.semaphore_signal(met.at[k], inc=1, device_id=to, device_id_type=MESH)

    def hear(k):
        pl.semaphore_wait(met.at[k], len(beside))

    first, second = pl.ds(0, 256), pl.ds(256, 256)
    most, rest = pl.ds(0, 448), pl.ds(448, 64)

    def hops(h):
        return tuple(
            remote(src, dst, kv_send.at[i, h], kv_recv.at[i, h], to)
            for i, (src, dst, to) in enumerate((
                (kv.at[0, h], kv.at[1, h], right),
                (kv.at[0, h], kv.at[2, h], left),
                (kv.at[0, h], kv.at[3, h], cross),
                (kv.at[1, h, first], kv.at[4, h, first], right),
                (kv.at[2, h, second], kv.at[4, h, second], left),
                (kv.at[3, h, most], kv.at[5, h, most], right),
                (kv.at[3, h, most], kv.at[6, h, most], left),
                (kv.at[4, h], kv.at[7, h], cross),
                (kv.at[1, h, rest], kv.at[5, h, rest], cross),
                (kv.at[2, h, rest], kv.at[6, h, rest], cross),
            ))
        )

    links = [hops(h) for h in range(KVH)]

    def start(h, *steps):
        for i in steps:
            links[h][i].start()

    def arrived(h, *steps):
        for i in steps:
            links[h][i].wait_recv()

    loads[0].wait()
    loads[1].wait()
    for h in range(KVH):
        kv[0, h, 0:256, :] = kbuf[:, h * D:(h + 1) * D]
        for part in range(2):
            piece = vbuf[part * 128:(part + 1) * 128, h * D:(h + 1) * D]
            kv[0, h, 256 + part * 128:384 + part * 128, :] = piece.astype(F32).T.astype(BF16)
    pl.semaphore_wait(barrier, len(greeted))
    start(0, 0, 1, 2)
    start(1, 0, 1, 2)
    tell(0)

    scale = adv_ref[...].astype(F32) * (1.0 / (128.0 * 256.0))
    column = jnp.broadcast_to(scale, (128, T)).T
    wide = FEATURES // 8

    def cotangent(part):
        cols = slice(part * wide, (part + 1) * wide)
        for at in range(part * wide, (part + 1) * wide, 128):
            cot[:, at:at + 128] = (column * cot[:, at:at + 128].astype(F32)).astype(BF16)
        term = lax.dot_general(
            cot[:, cols], wubuf[:, cols], (((1,), (1,)), ((), ())), preferred_element_type=F32
        )
        if part == 0:
            acc[...] = term
        else:
            acc[...] += term

    loads[2].wait()
    loads[3].wait()
    for part in range(4):
        cotangent(part)
    arrived(0, 0, 1, 2)
    start(0, 3, 4, 5, 6, 8, 9)
    start(2, 0, 1, 2)
    hear(0)
    tell(1)
    for part in range(4, 8):
        cotangent(part)
    for half in range(2):
        blh[half] = acc[:, half * 128:(half + 1) * 128].astype(BF16)
    cot_copy = remote(cot, cot2, core_send.at[0], core_recv.at[0], twin)
    cot_copy.start()
    bl_copy = remote(blh.at[1 - core], bl2, core_send.at[1], core_recv.at[1], twin)
    bl_copy.start()
    arrived(1, 0, 1, 2)
    start(1, 3, 4, 8, 9)
    start(3, 0, 1, 2)
    hear(1)
    tell(2)

    loads[5].wait()
    for i in range(KVH * GROUP):
        wdt[i // GROUP, :, i % GROUP * D:(i % GROUP + 1) * D] = wdbuf[i * D:(i + 1) * D, :].astype(F32).T.astype(BF16)

    ctx = yh * 4 + x
    marked = [jnp.int32(0)] * BLOCKS
    cur = ctx
    for _ in range(BLOCKS):
        cur = parents[0, cur]
        marked = [jnp.where(cur == b, 1, marked[b]) for b in range(BLOCKS)]
    for s in range(1, BLOCKS):
        block = (yh if SLOT_ROW[s] == 0 else 1 - yh) * 4 + (x + SLOT_STEP[s]) % 4
        seen = jnp.int32(0)
        for b in range(BLOCKS):
            seen = jnp.where(block == b, marked[b], seen)
        offs[s] = jnp.where(seen > 0, 0.0, MASKED)
    key_pos = lax.broadcasted_iota(jnp.int32, (T, T), 0)
    query_pos = lax.broadcasted_iota(jnp.int32, (T, T), 1)
    of_query = jnp.broadcast_to(branch_ref[...].astype(F32), (T, T))
    of_key = of_query.T
    local = (key_pos <= query_pos) & ((of_key == of_query) | (of_key == 0.0))
    bias[...] = jnp.where(local, 0.0, MASKED)

    def score(h, *slots):
        for s in slots:
            for g in range(GROUP):
                at = (h * GROUP + g) * D
                value = lax.dot_general(
                    kv[s, h, 0:256, :], qbuf[:, at:at + D], (((1,), (1,)), ((), ())), preferred_element_type=F32
                )
                if s == 0:
                    value = value + bias[...]
                scores[h % 2, s, g] = value
                peak = jnp.max(value.reshape(T // 8, 8, T), axis=0)
                top[h % 2, g] = peak if s == 0 else jnp.maximum(top[h % 2, g], peak + offs[s])

    def weigh(h):
        for s in range(BLOCKS):
            vt[:, s * T:s * T + 128] = kv[s, h, 256:384, :]
            vt[:, s * T + 128:(s + 1) * T] = kv[s, h, 384:512, :]
        for g in range(GROUP):
            peak = jnp.max(top[h % 2, g], axis=0, keepdims=True) * FACTOR
            total = jnp.zeros((8, T), F32)
            out = jnp.zeros((D, T), F32)
            for s in range(BLOCKS):
                shift = peak if s == 0 else peak - offs[s]
                weight = jnp.exp2(scores[h % 2, s, g] * FACTOR - shift)
                total = total + jnp.sum(weight.reshape(T // 8, 8, T), axis=0)
                out = out + jnp.dot(vt[:, s * T:(s + 1) * T], weight.astype(BF16), preferred_element_type=F32)
            bottom = jnp.sum(total, axis=0, keepdims=True)
            ctx_t[h, g * D:(g + 1) * D, :] = (out / bottom).astype(BF16)

    ctx_copies = [
        remote(ctx_t.at[h], ctx2.at[h], core_send.at[2 + h], core_recv.at[2 + h], twin) for h in range(KVH)
    ]

    def after(h):
        ctx_copies[h].start()
        term = jnp.dot(wdt[h], ctx_t[h], preferred_element_type=F32)
        if h == 0:
            low[...] = term
        else:
            low[...] += term

    def band(at):
        return rows16(at * 80, 80)

    z1 = [
        [
            remote(
                downb.at[h, band((z + d) % 8)], zin.at[h, d - 1], z1_send.at[h, d - 1], z1_recv.at[h, d - 1], peers[d - 1]
            )
            for d in range(1, 8)
        ]
        for h in range(KVH)
    ]

    def down_terms(h):
        ctx_copies[h].wait_recv()
        term = jnp.dot(ctx_t[h], blh[core], preferred_element_type=F32)
        term = term + jnp.dot(ctx2[h], bl2[...], preferred_element_type=F32)
        downb[h] = term.astype(BF16)
        for copy in z1[h]:
            copy.start()

    me = y * 4 + x
    z2 = []
    for h in range(KVH):
        for to_yl in range(2):
            to_y = (h // 2) * 2 + to_yl
            to_x = 2 * (h % 2) + z // 4
            z2.append((
                to_y * 4 + to_x != me,
                remote(zs.at[h], zin2.at[me], z2_send.at[h, to_yl], z2_recv.at[me], in_plane(to_y, to_x)),
            ))

    def band_sum(h):
        total = downb[h, band(z), :].astype(F32)
        for d in range(1, 8):
            z1[h][d - 1].wait_recv()
            total = total + zin[h, d - 1].astype(F32)
        zs[h] = total.astype(BF16)
        for elsewhere, copy in z2[2 * h:2 * h + 2]:
            pl.when(elsewhere)(copy.start)

    loads[4].wait()
    hear(2)
    arrived(0, 3, 4)
    start(0, 7)
    score(0, 0, 1, 2, 3, 4)
    score(1, 0, 1, 2, 3)
    arrived(0, 5, 6)
    score(0, 5, 6)
    arrived(0, 7)
    score(0, 7)
    arrived(2, 0, 1, 2)
    start(2, 3, 4, 8, 9)
    start(1, 5, 6)
    arrived(0, 8, 9)
    weigh(0)
    after(0)
    arrived(1, 3, 4)
    start(1, 7)
    score(1, 4)
    score(2, 0, 1, 2, 3)
    arrived(3, 0, 1, 2)
    start(3, 3, 4, 8, 9)
    start(2, 5, 6)
    start(3, 5, 6)
    arrived(1, 5, 6)
    score(1, 5, 6)
    arrived(1, 7)
    score(1, 7)
    arrived(2, 3, 4)
    start(2, 7)
    arrived(1, 8, 9)
    weigh(1)
    after(1)
    bl_copy.wait_recv()
    down_terms(0)
    arrived(3, 3, 4)
    start(3, 7)
    score(2, 4)
    score(3, 0, 1, 2, 3, 4)
    arrived(2, 5, 6)
    score(2, 5, 6)
    arrived(2, 7)
    score(2, 7)
    arrived(2, 8, 9)
    weigh(2)
    after(2)
    down_terms(1)
    band_sum(0)
    arrived(3, 5, 6)
    score(3, 5, 6)
    arrived(3, 7)
    score(3, 7)
    arrived(3, 8, 9)
    down_terms(2)
    weigh(3)
    after(3)

    for half in range(2):
        lowh[half] = low[half * 128:(half + 1) * 128, :].astype(BF16)
    low_copy = remote(lowh.at[1 - core], low2, core_send.at[6], core_recv.at[6], twin)
    low_copy.start()
    down_terms(3)
    band_sum(1)
    cot_copy.wait_recv()
    low_copy.wait_recv()

    def up_terms(row, col):
        cols = pl.ds(pl.multiple_of((row * 4 + col) * 640, 128), 640)
        term = jnp.dot(lowh[core], cot[:, cols], preferred_element_type=F32)
        term = term + jnp.dot(low2[...], cot2[:, cols], preferred_element_type=F32)
        for j in range(5):
            terms[row, col, j * 128:(j + 1) * 128, :] = term[:, j * 128:(j + 1) * 128].astype(BF16)

    def by_x(col):
        return terms.at[:, col, pl.ds(0, 160)], terms.at[:, col, pl.ds(160, 160)]

    def by_y(at):
        part = rows16(320 + (at % 2) * 160, 160)
        return terms.at[at // 2, pl.ds(0, 2), part], terms.at[at // 2, pl.ds(2, 2), part]

    ring_x = Ring(
        right, left, (by_x(xo), by_x(xp), by_x(xm), by_x(x)),
        [x1.at[i] for i in range(8)], ring_send.at[0], ring_recv.at[0],
    )
    ring_y = Ring(
        plus_y, minus_y, (by_y(yo), by_y(yp), by_y(ym), by_y(y)),
        [y1.at[i] for i in range(8)], ring_send.at[1], ring_recv.at[1],
    )
    up_terms(yh, xo)
    up_terms(1 - yh, xo)
    ring_x.start(0, 1)
    up_terms(1 - yh, x)
    up_terms(1 - yh, xp)
    up_terms(1 - yh, xm)
    ring_y.start(0, 1)
    up_terms(yh, xp)
    up_terms(yh, xm)
    ring_x.start(2, 3)
    up_terms(yh, x)
    ring_y.start(2, 3)
    band_sum(2)
    ring_x.middle()
    ring_y.middle()
    band_sum(3)

    def x_by_y(at):
        return left_x.at[at // 2, rows16((at % 2) * 160, 160)]

    direct_xy = Direct(
        cross, plus_y, minus_y, (x_by_y(yo), x_by_y(yp), x_by_y(ym), x_by_y(y)), x2, dir_send.at[0], dir_recv.at[0]
    )
    direct_yx = Direct(
        in_plane(y, xo), right, left, (left_y.at[xo], left_y.at[xp], left_y.at[xm], left_y.at[x]),
        y2, dir_send.at[1], dir_recv.at[1],
    )
    a, b = ring_x.end()
    left_x[:, 0:160, :] = a.astype(BF16)
    left_x[:, 160:320, :] = b.astype(BF16)
    direct_xy.begin()
    a, b = ring_y.end()
    left_y[0:2] = a.astype(BF16)
    left_y[2:4] = b.astype(BF16)
    direct_yx.begin()

    owner = x % 2 == z // 4
    mine = 2 * yh + x // 2
    spot = rows16((z % 4) * 80, 80)
    z4 = [
        remote(fdown.at[core, spot], fdown.at[core, spot], z4_send.at[d - 1], z4_recv.at[z % 4], peers[d - 1])
        for d in range(1, 8)
    ]

    @pl.when(owner)
    def _():
        for i in range(16):

            @pl.when(i != me)
            def _():
                remote(zs.at[0], zin2.at[i], z2_send.at[0, 0], z2_recv.at[i], twin).wait_recv()

            @pl.when(i == me)
            def _():
                zin2[i] = zs[mine]

        total = zin2[0].astype(F32)
        for i in range(1, 16):
            total = total + zin2[i].astype(F32)
        fdown[core, spot, :] = total.astype(BF16)
        for copy in z4:
            copy.start()

    quarter[0:160] = direct_xy.end().astype(BF16)
    quarter[160:320] = direct_yx.end().astype(BF16)
    quarter[320:384] = jnp.zeros((64, 128), BF16)

    def chunk(at):
        return rows16(at * 48, 48)

    z_copies = []
    for d in range(1, 8):
        copy = remote(
            quarter.at[chunk((z + d) % 8)], pieces.at[d - 1], z_send.at[0, d - 1], z_recv.at[0, d - 1], peers[d - 1]
        )
        copy.start()
        z_copies.append(copy)

    for i in range(4):
        at = pl.ds(i * 80, 80)
        part = fdown.at[core, at]

        @pl.when(jnp.logical_not(owner) | (z % 4 != i))
        def _():
            remote(part, part, z4_send.at[0], z4_recv.at[i], twin).wait_recv()

    down_out = remote(fdown.at[core], fdown.at[core], out_send.at[3], out_recv.at[3], twin)
    down_out.start()

    piece = quarter[chunk(z), :].astype(F32)
    for d in range(1, 8):
        z_copies[d - 1].wait_recv()
        piece = piece + pieces[d - 1].astype(F32)
    final[core, yl, chunk(z), :] = piece.astype(BF16)

    def to_near(d):
        here = final.at[core, yl, chunk((z + 8 - d) % 8)]
        return remote(here, here, near_send.at[d], near_recv.at[d], near)

    near_copies = [to_near(d) for d in range(8)]
    near_copies[0].start()
    for d in range(1, 8):
        here = final.at[core, yl, chunk(z)]
        copy = remote(here, here, z_send.at[1, d - 1], z_recv.at[1, d - 1], peers[d - 1])
        copy.start()
        z_copies.append(copy)

    for d in (1, 7, 2, 6, 3, 5, 4):
        z_copies[6 + d].wait_recv()
        near_copies[d].start()
    here = final.at[core, yl]
    to_twin = remote(here, here, out_send.at[1], out_recv.at[1], twin)
    to_twin.start()
    there = final.at[core, 1 - yl]
    for copy in near_copies:
        copy.wait_recv()
    on_twin = remote(there, there, out_send.at[2], out_recv.at[2], twin)
    on_twin.start()
    to_twin.wait_recv()
    on_twin.wait_recv()
    down_out.wait_recv()

    for h in range(KVH):
        for copy in links[h] + tuple(z1[h]):
            copy.wait_send()
    for elsewhere, copy in z2:
        pl.when(elsewhere)(copy.wait_send)

    @pl.when(owner)
    def _():
        for copy in z4:
            copy.wait_send()

    for copy in ctx_copies + z_copies + near_copies + [cot_copy, bl_copy, low_copy, down_out, to_twin, on_twin]:
        copy.wait_send()
    for ring in (ring_x, ring_y, direct_xy, direct_yx):
        ring.finish()


def lay_out(fdown, final, down_ref, up_ref, rows):
    for k in range(2):
        down_ref[:, k * 128:(k + 1) * 128] = fdown[k].astype(F32)
        for part in range(2):
            rows[k, part * 160:part * 160 + 160, :] = final[k, part, 0:160, :].astype(F32)
            rows[k, 320 + part * 160:480 + part * 160, :] = final[k, part, 160:320, :].astype(F32)
    for k in range(2):
        for j in range(5):
            up_ref[k * 128:(k + 1) * 128, j * 128:(j + 1) * 128] = rows[k, j * 128:(j + 1) * 128, :]


def on_device(q, k, v, og, adv, branch, parents, wd, wu):
    hbm = pl.BlockSpec(memory_space=pl.ANY)
    vmem = pl.BlockSpec(memory_space=pltpu.VMEM)
    dma = pltpu.SemaphoreType.DMA
    sums = pl.pallas_call(
        kernel,
        name="adapter_gradients",
        out_shape=(
            jax.ShapeDtypeStruct((2, 320, 128), BF16),
            jax.ShapeDtypeStruct((2, 2, 384, 128), BF16),
        ),
        in_specs=[pl.BlockSpec(memory_space=pltpu.SMEM), vmem, vmem] + [hbm] * 6,
        out_specs=(vmem, vmem),
        scratch_shapes=[
            pltpu.VMEM((T, KVH * D), BF16),
            pltpu.VMEM((T, KVH * D), BF16),
            pltpu.VMEM((BLOCKS, KVH, 512, D), BF16),
            pltpu.VMEM((T, ATTN), BF16),
                pltpu.VMEM((RANK, FEATURES), BF16),
            pltpu.VMEM((ATTN, RANK), BF16),
            pltpu.VMEM((KVH, RANK, GROUP * D), BF16),
            pltpu.VMEM((T, FEATURES), BF16),
            pltpu.VMEM((T, FEATURES), BF16),
            pltpu.VMEM((T, RANK), F32),
            pltpu.VMEM((2, T, 128), BF16),
            pltpu.VMEM((T, 128), BF16),
            pltpu.VMEM((KVH, GROUP * D, T), BF16),
            pltpu.VMEM((KVH, GROUP * D, T), BF16),
            pltpu.VMEM((RANK, T), F32),
            pltpu.VMEM((2, 128, T), BF16),
            pltpu.VMEM((128, T), BF16),
            pltpu.VMEM((2, BLOCKS, GROUP, T, T), F32),
            pltpu.VMEM((2, GROUP, 8, T), F32),
            pltpu.VMEM((T, T), F32),
            pltpu.VMEM((D, BLOCKS * T), BF16),
            pltpu.SMEM((BLOCKS,), F32),
            pltpu.VMEM((KVH, GROUP * D, 128), BF16),
            pltpu.VMEM((KVH, 7, 80, 128), BF16),
            pltpu.VMEM((KVH, 80, 128), BF16),
            pltpu.VMEM((16, 80, 128), BF16),
            pltpu.VMEM((2, 4, 640, 128), BF16),
            pltpu.VMEM((8, 2, 160, 128), BF16),
            pltpu.VMEM((8, 2, 160, 128), BF16),
            pltpu.VMEM((2, 320, 128), BF16),
            pltpu.VMEM((4, 160, 128), BF16),
            pltpu.VMEM((3, 160, 128), BF16),
            pltpu.VMEM((3, 160, 128), BF16),
            pltpu.VMEM((384, 128), BF16),
            pltpu.VMEM((7, 48, 128), BF16),
            dma((6,)),
            dma((10, KVH)), dma((10, KVH)),
            dma((7,)), dma((7,)),
            dma((KVH, 7)), dma((KVH, 7)),
            dma((KVH, 2)), dma((16,)),
            dma((7,)), dma((4,)),
            dma((2, 6)), dma((2, 6)),
            dma((2, 3)), dma((2, 3)),
            dma((2, 7)), dma((2, 7)),
            dma((8,)), dma((8,)),
            dma((4,)), dma((4,)),
            pltpu.SemaphoreType.REGULAR((3,)),
        ],
        compiler_params=pltpu.CompilerParams(
            collective_id=0, has_side_effects=True, vmem_limit_bytes=60 * MIB
        ),
    )(parents, adv, branch[0], q[0], k[0], v[0], og[0], wu, wd)
    return pl.pallas_call(
        lay_out,
        name="lay_out",
        out_shape=(
            jax.ShapeDtypeStruct((320, RANK), F32),
            jax.ShapeDtypeStruct((RANK, 640), F32),
        ),
        in_specs=[vmem, vmem],
        out_specs=(vmem, vmem),
        scratch_shapes=[pltpu.VMEM((2, 640, 128), F32)],
    )(*sums)


def solution(mesh):
    return jax.shard_map(
        on_device,
        mesh=mesh,
        in_specs=(
            P("dp", "ctx", None),
            P("dp", "ctx", None),
            P("dp", "ctx", None),
            P("dp", "ctx", None),
            P("dp", "ctx"),
            P("dp", "ctx", None),
            P("dp", None),
            P(),
            P(),
        ),
        out_specs=(P("ctx", None), P(None, "ctx")),
        check_vma=False,
    )
```

```python
import math

import jax
import jax.numpy as jnp
from jax import lax
from jax.experimental import pallas as pl
from jax.experimental.pallas import tpu as pltpu
from jax.sharding import PartitionSpec as P

MESH = pl.DeviceIdType.MESH
BF16 = jnp.bfloat16
F32 = jnp.float32
D = 128
T = 256
KVH = 4
GROUP = 5
BLOCKS = 8
FEATURES = 5120
ATTN = 2560
RANK = 256
MASKED = -1e30
MIB = 1 << 20
FACTOR = math.log2(math.e) / math.sqrt(D)


def place():
    dp = lax.axis_index("dp")
    ctx = lax.axis_index("ctx")
    return dp // 16, (dp // 2) % 8, dp % 2, ctx // 4, ctx % 4


def device(yl, z, core, yh, x):
    return ((yl * 8 + z) * 2 + core, yh * 4 + x)


def remote(src, dst, send, recv, to):
    return pltpu.make_async_remote_copy(
        src_ref=src, dst_ref=dst, send_sem=send, recv_sem=recv, device_id=to, device_id_type=MESH
    )


def rows16(start, size):
    return pl.ds(pl.multiple_of(start, 16), size)


class Ring:
    def __init__(self, plus, minus, parts, bufs, send, recv):
        self.opposite, self.plus_part, self.minus_part, self.own = parts
        self.bufs = bufs
        opp_a, opp_b, dir_a, dir_b, sum_a, sum_b, out_a, out_b = bufs
        self.copies = tuple(
            remote(src, dst, send.at[i], recv.at[i], to)
            for i, (src, dst, to) in enumerate((
                (self.opposite[0], opp_a, plus),
                (self.opposite[1], opp_b, minus),
                (self.plus_part[1], dir_b, plus),
                (self.minus_part[0], dir_a, minus),
                (out_a, sum_a, plus),
                (out_b, sum_b, minus),
            ))
        )

    def start(self, *which):
        for i in which:
            self.copies[i].start()

    def middle(self):
        opp_a, opp_b, _, _, _, _, out_a, out_b = self.bufs
        self.copies[0].wait_recv()
        out_a[...] = (self.plus_part[0][...].astype(F32) + opp_a[...].astype(F32)).astype(BF16)
        self.copies[4].start()
        self.copies[1].wait_recv()
        out_b[...] = (self.minus_part[1][...].astype(F32) + opp_b[...].astype(F32)).astype(BF16)
        self.copies[5].start()

    def end(self):
        _, _, dir_a, dir_b, sum_a, sum_b, _, _ = self.bufs
        for i in (2, 3, 4, 5):
            self.copies[i].wait_recv()
        a = self.own[0][...].astype(F32) + dir_a[...].astype(F32) + sum_a[...].astype(F32)
        b = self.own[1][...].astype(F32) + dir_b[...].astype(F32) + sum_b[...].astype(F32)
        return a, b

    def finish(self):
        for copy in self.copies:
            copy.wait_send()


class Direct:
    def __init__(self, opposite, plus, minus, parts, bufs, send, recv):
        self.own = parts[3]
        self.bufs = bufs
        self.copies = tuple(
            remote(parts[i], bufs.at[i], send.at[i], recv.at[i], to)
            for i, to in enumerate((opposite, plus, minus))
        )

    def begin(self):
        for copy in self.copies:
            copy.start()

    def end(self):
        total = self.own[...].astype(F32)
        for i in (1, 2, 0):
            self.copies[i].wait_recv()
            total = total + self.bufs[i].astype(F32)
        return total

    def finish(self):
        for copy in self.copies:
            copy.wait_send()


SLOT_ROW = (0, 0, 0, 1, 0, 1, 1, 1)
SLOT_STEP = (0, 3, 1, 0, 2, 3, 1, 2)


def kernel(
    parents, adv_ref, branch_ref, q_hbm, k_hbm, v_hbm, og_hbm, wu_hbm, wd_hbm,
    fdown, final,
    kv, qbuf, wubuf, wdbuf, wdt, cot, cot2, acc, blh, bl2, ctx_t, ctx2, low, lowh, low2,
    scores, top, bias, vt, peaks, totals, outs, offs,
    downb, zin, zs, zin2,
    terms, x1, y1, left_x, left_y, x2, y2, quarter, pieces,
    own_sem, load_sem, kv_send, kv_recv, core_send, core_recv, z1_send, z1_recv, z2_send, z2_recv, z4_send, z4_recv,
    ring_send, ring_recv, dir_send, dir_recv, z_send, z_recv, near_send, near_recv, out_send, out_recv, met,
):
    yl, z, core, yh, x = place()
    y = yh * 2 + yl
    xp, xm, xo = (x + 1) % 4, (x + 3) % 4, (x + 2) % 4
    yp, ym, yo = (y + 1) % 4, (y + 3) % 4, (y + 2) % 4

    def in_plane(to_y, to_x):
        return device(to_y % 2, z, core, to_y // 2, to_x)

    right, left = in_plane(y, xp), in_plane(y, xm)
    plus_y, minus_y, cross = in_plane(yp, x), in_plane(ym, x), in_plane(yo, x)
    near = device(1 - yl, z, core, yh, x)
    twin = device(yl, z, 1 - core, yh, x)
    peers = [device(yl, (z + d) % 8, core, yh, x) for d in range(1, 8)]

    own = []
    for h in range(KVH):
        for i, src in enumerate((k_hbm, v_hbm)):
            own.append(
                pltpu.make_async_copy(
                    src.at[:, pl.ds(h * D, D)], kv.at[0, h, pl.ds(i * 256, 256)], own_sem.at[h, i]
                )
            )
            own[-1].start()
    loads = []
    for i, (src, dst) in enumerate(((og_hbm, cot), (wu_hbm, wubuf), (q_hbm, qbuf), (wd_hbm, wdbuf))):
        copy = pltpu.make_async_copy(src, dst, load_sem.at[i])
        copy.start()
        loads.append(copy)
    barrier = pltpu.get_barrier_semaphore()
    beside = [right, left, plus_y, minus_y, peers[0], peers[6]]
    greeted = beside + [cross, twin]
    for to in greeted:
        pl.semaphore_signal(barrier, inc=1, device_id=to, device_id_type=MESH)

    def tell(k):
        for to in beside:
            pl.semaphore_signal(met.at[k], inc=1, device_id=to, device_id_type=MESH)

    def hear(k):
        pl.semaphore_wait(met.at[k], len(beside))

    first, second = pl.ds(0, 256), pl.ds(256, 256)
    most, rest = pl.ds(0, 448), pl.ds(448, 64)

    def hops(h):
        return tuple(
            remote(src, dst, kv_send.at[i, h], kv_recv.at[i, h], to)
            for i, (src, dst, to) in enumerate((
                (kv.at[0, h], kv.at[1, h], right),
                (kv.at[0, h], kv.at[2, h], left),
                (kv.at[0, h], kv.at[3, h], cross),
                (kv.at[1, h, first], kv.at[4, h, first], right),
                (kv.at[2, h, second], kv.at[4, h, second], left),
                (kv.at[3, h, most], kv.at[5, h, most], right),
                (kv.at[3, h, most], kv.at[6, h, most], left),
                (kv.at[4, h], kv.at[7, h], cross),
                (kv.at[1, h, rest], kv.at[5, h, rest], cross),
                (kv.at[2, h, rest], kv.at[6, h, rest], cross),
            ))
        )

    links = [hops(h) for h in range(KVH)]

    def start(h, *steps):
        for i in steps:
            links[h][i].start()

    def arrived(h, *steps):
        for i in steps:
            links[h][i].wait_recv()

    def send_own(h):
        own[2 * h].wait()
        own[2 * h + 1].wait()
        start(h, 0, 1, 2)

    own[0].wait()
    own[1].wait()
    pl.semaphore_wait(barrier, len(greeted))
    start(0, 0, 1, 2)
    send_own(1)
    tell(0)

    scale = adv_ref[...].astype(F32) * (1.0 / (128.0 * 256.0))
    column = jnp.broadcast_to(scale, (128, T)).T
    wide = FEATURES // 8

    def cotangent(part):
        cols = slice(part * wide, (part + 1) * wide)
        for at in range(part * wide, (part + 1) * wide, 128):
            cot[:, at:at + 128] = (column * cot[:, at:at + 128].astype(F32)).astype(BF16)
        term = lax.dot_general(
            cot[:, cols], wubuf[:, cols], (((1,), (1,)), ((), ())), preferred_element_type=F32
        )
        if part == 0:
            acc[...] = term
        else:
            acc[...] += term

    loads[0].wait()
    loads[1].wait()
    for part in range(4):
        cotangent(part)
    arrived(0, 0, 1, 2)
    send_own(2)
    hear(0)
    tell(1)
    for part in range(4, 8):
        cotangent(part)
    for half in range(2):
        blh[half] = acc[:, half * 128:(half + 1) * 128].astype(BF16)
    cot_copy = remote(cot, cot2, core_send.at[0], core_recv.at[0], twin)
    cot_copy.start()
    bl_copy = remote(blh.at[1 - core], bl2, core_send.at[1], core_recv.at[1], twin)
    bl_copy.start()
    arrived(1, 0, 1, 2)
    send_own(3)
    start(0, 3, 4, 8, 9)
    start(1, 3, 4, 8, 9)
    hear(1)
    tell(2)

    ctx = yh * 4 + x
    marked = [jnp.int32(0)] * BLOCKS
    cur = ctx
    for _ in range(BLOCKS):
        cur = parents[0, cur]
        marked = [jnp.where(cur == b, 1, marked[b]) for b in range(BLOCKS)]
    for s in range(1, BLOCKS):
        block = (yh if SLOT_ROW[s] == 0 else 1 - yh) * 4 + (x + SLOT_STEP[s]) % 4
        seen = jnp.int32(0)
        for b in range(BLOCKS):
            seen = jnp.where(block == b, marked[b], seen)
        offs[s] = jnp.where(seen > 0, 0.0, MASKED)
    key_pos = lax.broadcasted_iota(jnp.int32, (T, T), 0)
    query_pos = lax.broadcasted_iota(jnp.int32, (T, T), 1)
    of_query = jnp.broadcast_to(branch_ref[...].astype(F32), (T, T))
    of_key = of_query.T
    local = (key_pos <= query_pos) & ((of_key == of_query) | (of_key == 0.0))
    bias[...] = jnp.where(local, 0.0, MASKED)

    def score(h, *slots):
        for s in slots:
            for g in range(GROUP):
                at = (h * GROUP + g) * D
                value = lax.dot_general(
                    kv[s, h, 0:256, :], qbuf[:, at:at + D], (((1,), (1,)), ((), ())), preferred_element_type=F32
                )
                if s == 0:
                    value = value + bias[...]
                scores[h % 2, s % 4, g] = value
                peak = jnp.max(value.reshape(T // 8, 8, T), axis=0)
                if s > 0:
                    peak = peak + offs[s]
                top[h % 2, g] = peak if s % 4 == 0 else jnp.maximum(top[h % 2, g], peak)

    def weigh(h, slots, peak, total, out, g):
        for s in slots:
            shift = peak if s == 0 else peak - offs[s]
            weight = jnp.exp2(scores[h % 2, s % 4, g] * FACTOR - shift)
            total = total + jnp.sum(weight.reshape(T // 8, 8, T), axis=0)
            out = out + jnp.dot(
                vt[h % 2, :, s % 4 * T:(s % 4 + 1) * T], weight.astype(BF16), preferred_element_type=F32
            )
        return total, out

    def turn_values(h, slots):
        for s in slots:
            vt[h % 2, :, s % 4 * T:(s % 4 + 1) * T] = kv[s, h, 256:512, :].astype(F32).T.astype(BF16)

    def early(h):
        score(h, 0, 1, 2, 3)
        turn_values(h, range(4))
        for g in range(GROUP):
            i = h * GROUP + g
            peak = jnp.max(top[h % 2, g], axis=0, keepdims=True) * FACTOR
            peaks[i] = jnp.broadcast_to(peak, (8, T))
            totals[i], outs[i] = weigh(h, range(4), peak, jnp.zeros((8, T), F32), jnp.zeros((D, T), F32), g)

    def late(h):
        turn_values(h, range(4, 8))
        for g in range(GROUP):
            i = h * GROUP + g
            before = peaks[i][0:1]
            peak = jnp.maximum(before, jnp.max(top[h % 2, g], axis=0, keepdims=True) * FACTOR)
            fade = jnp.exp2(before - peak)
            total, out = weigh(h, range(4, 8), peak, totals[i] * fade, outs[i] * fade, g)
            bottom = jnp.sum(total, axis=0, keepdims=True)
            ctx_t[h, g * D:(g + 1) * D, :] = (out / bottom).astype(BF16)

    ctx_copies = [
        remote(ctx_t.at[h], ctx2.at[h], core_send.at[2 + h], core_recv.at[2 + h], twin) for h in range(KVH)
    ]

    def after(h):
        ctx_copies[h].start()
        term = jnp.dot(wdt[h], ctx_t[h], preferred_element_type=F32)
        if h == 0:
            low[...] = term
        else:
            low[...] += term

    def band(at):
        return rows16(at * 80, 80)

    z1 = [
        [
            remote(
                downb.at[h, band((z + d) % 8)], zin.at[h, d - 1], z1_send.at[h, d - 1], z1_recv.at[h, d - 1], peers[d - 1]
            )
            for d in range(1, 8)
        ]
        for h in range(KVH)
    ]

    def down_terms(h):
        ctx_copies[h].wait_recv()
        term = jnp.dot(ctx_t[h], blh[core], preferred_element_type=F32)
        term = term + jnp.dot(ctx2[h], bl2[...], preferred_element_type=F32)
        downb[h] = term.astype(BF16)
        for copy in z1[h]:
            copy.start()

    me = y * 4 + x
    z2 = []
    for h in range(KVH):
        for to_yl in range(2):
            to_y = (h // 2) * 2 + to_yl
            to_x = 2 * (h % 2) + z // 4
            z2.append((
                to_y * 4 + to_x != me,
                remote(zs.at[h], zin2.at[me], z2_send.at[h, to_yl], z2_recv.at[me], in_plane(to_y, to_x)),
            ))

    def band_sum(h):
        total = downb[h, band(z), :].astype(F32)
        for d in range(1, 8):
            z1[h][d - 1].wait_recv()
            total = total + zin[h, d - 1].astype(F32)
        zs[h] = total.astype(BF16)
        for elsewhere, copy in z2[2 * h:2 * h + 2]:
            pl.when(elsewhere)(copy.start)

    loads[2].wait()
    early(0)
    loads[3].wait()
    for i in range(KVH * GROUP):
        wdt[i // GROUP, :, i % GROUP * D:(i % GROUP + 1) * D] = wdbuf[i * D:(i + 1) * D, :].astype(F32).T.astype(BF16)

    early(1)
    arrived(2, 0, 1, 2)
    start(2, 3, 4, 8, 9)
    hear(2)
    early(2)
    arrived(3, 0, 1, 2)
    start(3, 3, 4, 8, 9)
    for h in range(KVH):
        start(h, 5, 6)
    early(3)
    for h in range(KVH):
        arrived(h, 3, 4)
        start(h, 7)
        if h < 2:
            score(h, 4)
    bl_copy.wait_recv()
    for h in range(KVH):
        if h >= 2:
            score(h, 4)
        arrived(h, 5, 6)
        score(h, 5, 6)
        arrived(h, 7)
        score(h, 7)
        arrived(h, 8, 9)
        late(h)
        after(h)
        if h >= 1:
            down_terms(h - 1)
        if h >= 2:
            band_sum(h - 2)

    for half in range(2):
        lowh[half] = low[half * 128:(half + 1) * 128, :].astype(BF16)
    low_copy = remote(lowh.at[1 - core], low2, core_send.at[6], core_recv.at[6], twin)
    low_copy.start()
    down_terms(3)
    cot_copy.wait_recv()
    low_copy.wait_recv()

    def up_terms(row, col):
        cols = pl.ds(pl.multiple_of((row * 4 + col) * 640, 128), 640)
        term = jnp.dot(lowh[core], cot[:, cols], preferred_element_type=F32)
        term = term + jnp.dot(low2[...], cot2[:, cols], preferred_element_type=F32)
        for j in range(5):
            terms[row, col, j * 128:(j + 1) * 128, :] = term[:, j * 128:(j + 1) * 128].astype(BF16)

    def by_x(col):
        return terms.at[:, col, pl.ds(0, 160)], terms.at[:, col, pl.ds(160, 160)]

    def by_y(at):
        part = rows16(320 + (at % 2) * 160, 160)
        return terms.at[at // 2, pl.ds(0, 2), part], terms.at[at // 2, pl.ds(2, 2), part]

    ring_x = Ring(
        right, left, (by_x(xo), by_x(xp), by_x(xm), by_x(x)),
        [x1.at[i] for i in range(8)], ring_send.at[0], ring_recv.at[0],
    )
    ring_y = Ring(
        plus_y, minus_y, (by_y(yo), by_y(yp), by_y(ym), by_y(y)),
        [y1.at[i] for i in range(8)], ring_send.at[1], ring_recv.at[1],
    )
    up_terms(yh, xo)
    up_terms(1 - yh, xo)
    ring_x.start(0, 1)
    up_terms(1 - yh, x)
    up_terms(1 - yh, xp)
    up_terms(1 - yh, xm)
    ring_y.start(0, 1)
    up_terms(yh, xp)
    up_terms(yh, xm)
    ring_x.start(2, 3)
    up_terms(yh, x)
    ring_y.start(2, 3)
    ring_x.middle()
    ring_y.middle()
    band_sum(2)

    def x_by_y(at):
        return left_x.at[at // 2, rows16((at % 2) * 160, 160)]

    direct_xy = Direct(
        cross, plus_y, minus_y, (x_by_y(yo), x_by_y(yp), x_by_y(ym), x_by_y(y)), x2, dir_send.at[0], dir_recv.at[0]
    )
    direct_yx = Direct(
        in_plane(y, xo), right, left, (left_y.at[xo], left_y.at[xp], left_y.at[xm], left_y.at[x]),
        y2, dir_send.at[1], dir_recv.at[1],
    )
    a, b = ring_x.end()
    left_x[:, 0:160, :] = a.astype(BF16)
    left_x[:, 160:320, :] = b.astype(BF16)
    direct_xy.begin()
    a, b = ring_y.end()
    left_y[0:2] = a.astype(BF16)
    left_y[2:4] = b.astype(BF16)
    direct_yx.begin()
    band_sum(3)

    quarter[0:160] = direct_xy.end().astype(BF16)
    quarter[160:320] = direct_yx.end().astype(BF16)
    quarter[320:384] = jnp.zeros((64, 128), BF16)

    def chunk(at):
        return rows16(at * 48, 48)

    z_copies = []
    for d in range(1, 8):
        copy = remote(
            quarter.at[chunk((z + d) % 8)], pieces.at[d - 1], z_send.at[0, d - 1], z_recv.at[0, d - 1], peers[d - 1]
        )
        copy.start()
        z_copies.append(copy)

    owner = x % 2 == z // 4
    mine = 2 * yh + x // 2
    spot = rows16((z % 4) * 80, 80)
    z4 = [
        remote(fdown.at[core, spot], fdown.at[core, spot], z4_send.at[d - 1], z4_recv.at[z % 4], peers[d - 1])
        for d in range(1, 8)
    ]

    @pl.when(owner)
    def _():
        for i in range(16):

            @pl.when(i != me)
            def _():
                remote(zs.at[0], zin2.at[i], z2_send.at[0, 0], z2_recv.at[i], twin).wait_recv()

            @pl.when(i == me)
            def _():
                zin2[i] = zs[mine]

        total = zin2[0].astype(F32)
        for i in range(1, 16):
            total = total + zin2[i].astype(F32)
        fdown[core, spot, :] = total.astype(BF16)
        for copy in z4:
            copy.start()

    piece = quarter[chunk(z), :].astype(F32)
    for d in range(1, 8):
        z_copies[d - 1].wait_recv()
        piece = piece + pieces[d - 1].astype(F32)
    final[core, yl, chunk(z), :] = piece.astype(BF16)

    def to_near(d):
        here = final.at[core, yl, chunk((z + 8 - d) % 8)]
        return remote(here, here, near_send.at[d], near_recv.at[d], near)

    near_copies = [to_near(d) for d in range(8)]
    near_copies[0].start()
    for d in range(1, 8):
        here = final.at[core, yl, chunk(z)]
        copy = remote(here, here, z_send.at[1, d - 1], z_recv.at[1, d - 1], peers[d - 1])
        copy.start()
        z_copies.append(copy)

    for i in range(4):
        at = pl.ds(i * 80, 80)
        part = fdown.at[core, at]

        @pl.when(jnp.logical_not(owner) | (z % 4 != i))
        def _():
            remote(part, part, z4_send.at[0], z4_recv.at[i], twin).wait_recv()

    down_out = remote(fdown.at[core], fdown.at[core], out_send.at[3], out_recv.at[3], twin)
    down_out.start()

    for d in (1, 7, 2, 6, 3, 5, 4):
        z_copies[6 + d].wait_recv()
        near_copies[d].start()
    here = final.at[core, yl]
    to_twin = remote(here, here, out_send.at[1], out_recv.at[1], twin)
    to_twin.start()
    there = final.at[core, 1 - yl]
    for copy in near_copies:
        copy.wait_recv()
    on_twin = remote(there, there, out_send.at[2], out_recv.at[2], twin)
    on_twin.start()
    to_twin.wait_recv()
    on_twin.wait_recv()
    down_out.wait_recv()

    for h in range(KVH):
        for copy in links[h] + tuple(z1[h]):
            copy.wait_send()
    for elsewhere, copy in z2:
        pl.when(elsewhere)(copy.wait_send)

    @pl.when(owner)
    def _():
        for copy in z4:
            copy.wait_send()

    for copy in ctx_copies + z_copies + near_copies + [cot_copy, bl_copy, low_copy, down_out, to_twin, on_twin]:
        copy.wait_send()
    for ring in (ring_x, ring_y, direct_xy, direct_yx):
        ring.finish()


def lay_out(fdown, final, down_ref, up_ref, rows):
    for k in range(2):
        down_ref[:, k * 128:(k + 1) * 128] = fdown[k].astype(F32)
        for part in range(2):
            rows[k, part * 160:part * 160 + 160, :] = final[k, part, 0:160, :].astype(F32)
            rows[k, 320 + part * 160:480 + part * 160, :] = final[k, part, 160:320, :].astype(F32)
    for k in range(2):
        for j in range(5):
            up_ref[k * 128:(k + 1) * 128, j * 128:(j + 1) * 128] = rows[k, j * 128:(j + 1) * 128, :]


def on_device(q, k, v, og, adv, branch, parents, wd, wu):
    hbm = pl.BlockSpec(memory_space=pl.ANY)
    vmem = pl.BlockSpec(memory_space=pltpu.VMEM)
    dma = pltpu.SemaphoreType.DMA
    sums = pl.pallas_call(
        kernel,
        name="adapter_gradients",
        out_shape=(
            jax.ShapeDtypeStruct((2, 320, 128), BF16),
            jax.ShapeDtypeStruct((2, 2, 384, 128), BF16),
        ),
        in_specs=[pl.BlockSpec(memory_space=pltpu.SMEM), vmem, vmem] + [hbm] * 6,
        out_specs=(vmem, vmem),
        scratch_shapes=[
            pltpu.VMEM((BLOCKS, KVH, 512, D), BF16),
            pltpu.VMEM((T, ATTN), BF16),
                pltpu.VMEM((RANK, FEATURES), BF16),
            pltpu.VMEM((ATTN, RANK), BF16),
            pltpu.VMEM((KVH, RANK, GROUP * D), BF16),
            pltpu.VMEM((T, FEATURES), BF16),
            pltpu.VMEM((T, FEATURES), BF16),
            pltpu.VMEM((T, RANK), F32),
            pltpu.VMEM((2, T, 128), BF16),
            pltpu.VMEM((T, 128), BF16),
            pltpu.VMEM((KVH, GROUP * D, T), BF16),
            pltpu.VMEM((KVH, GROUP * D, T), BF16),
            pltpu.VMEM((RANK, T), F32),
            pltpu.VMEM((2, 128, T), BF16),
            pltpu.VMEM((128, T), BF16),
            pltpu.VMEM((2, 4, GROUP, T, T), F32),
            pltpu.VMEM((2, GROUP, 8, T), F32),
            pltpu.VMEM((T, T), F32),
            pltpu.VMEM((2, D, 4 * T), BF16),
            pltpu.VMEM((KVH * GROUP, 8, T), F32),
            pltpu.VMEM((KVH * GROUP, 8, T), F32),
            pltpu.VMEM((KVH * GROUP, D, T), F32),
            pltpu.SMEM((BLOCKS,), F32),
            pltpu.VMEM((KVH, GROUP * D, 128), BF16),
            pltpu.VMEM((KVH, 7, 80, 128), BF16),
            pltpu.VMEM((KVH, 80, 128), BF16),
            pltpu.VMEM((16, 80, 128), BF16),
            pltpu.VMEM((2, 4, 640, 128), BF16),
            pltpu.VMEM((8, 2, 160, 128), BF16),
            pltpu.VMEM((8, 2, 160, 128), BF16),
            pltpu.VMEM((2, 320, 128), BF16),
            pltpu.VMEM((4, 160, 128), BF16),
            pltpu.VMEM((3, 160, 128), BF16),
            pltpu.VMEM((3, 160, 128), BF16),
            pltpu.VMEM((384, 128), BF16),
            pltpu.VMEM((7, 48, 128), BF16),
            dma((KVH, 2)),
            dma((4,)),
            dma((10, KVH)), dma((10, KVH)),
            dma((7,)), dma((7,)),
            dma((KVH, 7)), dma((KVH, 7)),
            dma((KVH, 2)), dma((16,)),
            dma((7,)), dma((4,)),
            dma((2, 6)), dma((2, 6)),
            dma((2, 3)), dma((2, 3)),
            dma((2, 7)), dma((2, 7)),
            dma((8,)), dma((8,)),
            dma((4,)), dma((4,)),
            pltpu.SemaphoreType.REGULAR((3,)),
        ],
        compiler_params=pltpu.CompilerParams(
            collective_id=0, has_side_effects=True, vmem_limit_bytes=60 * MIB
        ),
    )(parents, adv, branch[0], q[0], k[0], v[0], og[0], wu, wd)
    return pl.pallas_call(
        lay_out,
        name="lay_out",
        out_shape=(
            jax.ShapeDtypeStruct((320, RANK), F32),
            jax.ShapeDtypeStruct((RANK, 640), F32),
        ),
        in_specs=[vmem, vmem],
        out_specs=(vmem, vmem),
        scratch_shapes=[pltpu.VMEM((2, 640, 128), F32)],
    )(*sums)


def solution(mesh):
    return jax.shard_map(
        on_device,
        mesh=mesh,
        in_specs=(
            P("dp", "ctx", None),
            P("dp", "ctx", None),
            P("dp", "ctx", None),
            P("dp", "ctx", None),
            P("dp", "ctx"),
            P("dp", "ctx", None),
            P("dp", None),
            P(),
            P(),
        ),
        out_specs=(P("ctx", None), P(None, "ctx")),
        check_vma=False,
    )
```

```python
import math

import jax
import jax.numpy as jnp
from jax import lax
from jax.experimental import pallas as pl
from jax.experimental.pallas import tpu as pltpu
from jax.sharding import PartitionSpec as P

MESH = pl.DeviceIdType.MESH
BF16 = jnp.bfloat16
F32 = jnp.float32
D = 128
T = 256
KVH = 4
GROUP = 5
BLOCKS = 8
FEATURES = 5120
ATTN = 2560
RANK = 256
MASKED = -1e30
MIB = 1 << 20
FACTOR = math.log2(math.e) / math.sqrt(D)


def place():
    dp = lax.axis_index("dp")
    ctx = lax.axis_index("ctx")
    return dp // 16, (dp // 2) % 8, dp % 2, ctx // 4, ctx % 4


def device(yl, z, core, yh, x):
    return ((yl * 8 + z) * 2 + core, yh * 4 + x)


def remote(src, dst, send, recv, to):
    return pltpu.make_async_remote_copy(
        src_ref=src, dst_ref=dst, send_sem=send, recv_sem=recv, device_id=to, device_id_type=MESH
    )


def rows16(start, size):
    return pl.ds(pl.multiple_of(start, 16), size)


class Ring:
    def __init__(self, plus, minus, parts, bufs, send, recv):
        self.opposite, self.plus_part, self.minus_part, self.own = parts
        self.bufs = bufs
        opp_a, opp_b, dir_a, dir_b, sum_a, sum_b, out_a, out_b = bufs
        self.copies = tuple(
            remote(src, dst, send.at[i], recv.at[i], to)
            for i, (src, dst, to) in enumerate((
                (self.opposite[0], opp_a, plus),
                (self.opposite[1], opp_b, minus),
                (self.plus_part[1], dir_b, plus),
                (self.minus_part[0], dir_a, minus),
                (out_a, sum_a, plus),
                (out_b, sum_b, minus),
            ))
        )

    def start(self, *which):
        for i in which:
            self.copies[i].start()

    def middle(self):
        opp_a, opp_b, _, _, _, _, out_a, out_b = self.bufs
        self.copies[0].wait_recv()
        out_a[...] = (self.plus_part[0][...].astype(F32) + opp_a[...].astype(F32)).astype(BF16)
        self.copies[4].start()
        self.copies[1].wait_recv()
        out_b[...] = (self.minus_part[1][...].astype(F32) + opp_b[...].astype(F32)).astype(BF16)
        self.copies[5].start()

    def end(self):
        _, _, dir_a, dir_b, sum_a, sum_b, _, _ = self.bufs
        for i in (2, 3, 4, 5):
            self.copies[i].wait_recv()
        a = self.own[0][...].astype(F32) + dir_a[...].astype(F32) + sum_a[...].astype(F32)
        b = self.own[1][...].astype(F32) + dir_b[...].astype(F32) + sum_b[...].astype(F32)
        return a, b

    def finish(self):
        for copy in self.copies:
            copy.wait_send()


class Direct:
    def __init__(self, opposite, plus, minus, parts, bufs, send, recv):
        self.own = parts[3]
        self.bufs = bufs
        self.copies = tuple(
            remote(parts[i], bufs.at[i], send.at[i], recv.at[i], to)
            for i, to in enumerate((opposite, plus, minus))
        )

    def begin(self):
        for copy in self.copies:
            copy.start()

    def end(self):
        total = self.own[...].astype(F32)
        for i in (1, 2, 0):
            self.copies[i].wait_recv()
            total = total + self.bufs[i].astype(F32)
        return total

    def finish(self):
        for copy in self.copies:
            copy.wait_send()


SLOT_ROW = (0, 0, 0, 1, 0, 1, 1, 1)
SLOT_STEP = (0, 3, 1, 0, 2, 3, 1, 2)


def kernel(
    parents, adv_ref, branch_ref, q_hbm, k_hbm, v_hbm, og_hbm, wu_hbm, wd_hbm,
    fdown, final,
    kv, qbuf, wubuf, wdbuf, wdt, cot, cot2, acc, blh, bl2, ctx_t, ctx2, low, lowh, low2,
    scores, top, bias, vt, peaks, totals, outs, offs,
    downb, zin, zs, zin2,
    terms, x1, y1, left_x, left_y, x2, y2, quarter, pieces,
    own_sem, load_sem, kv_send, kv_recv, core_send, core_recv, z1_send, z1_recv, z2_send, z2_recv, z4_send, z4_recv,
    ring_send, ring_recv, dir_send, dir_recv, z_send, z_recv, near_send, near_recv, out_send, out_recv, met,
):
    yl, z, core, yh, x = place()
    y = yh * 2 + yl
    xp, xm, xo = (x + 1) % 4, (x + 3) % 4, (x + 2) % 4
    yp, ym, yo = (y + 1) % 4, (y + 3) % 4, (y + 2) % 4

    def in_plane(to_y, to_x):
        return device(to_y % 2, z, core, to_y // 2, to_x)

    right, left = in_plane(y, xp), in_plane(y, xm)
    plus_y, minus_y, cross = in_plane(yp, x), in_plane(ym, x), in_plane(yo, x)
    near = device(1 - yl, z, core, yh, x)
    twin = device(yl, z, 1 - core, yh, x)
    peers = [device(yl, (z + d) % 8, core, yh, x) for d in range(1, 8)]

    own = []
    for h in range(KVH):
        for i, src in enumerate((k_hbm, v_hbm)):
            own.append(
                pltpu.make_async_copy(
                    src.at[:, pl.ds(h * D, D)], kv.at[0, h, pl.ds(i * 256, 256)], own_sem.at[h, i]
                )
            )
            own[-1].start()
    loads = []
    for i, (src, dst) in enumerate(((og_hbm, cot), (wu_hbm, wubuf), (q_hbm, qbuf), (wd_hbm, wdbuf))):
        copy = pltpu.make_async_copy(src, dst, load_sem.at[i])
        copy.start()
        loads.append(copy)
    barrier = pltpu.get_barrier_semaphore()
    beside = [right, left, plus_y, minus_y, peers[0], peers[6]]
    greeted = beside + [cross, twin]
    for to in greeted:
        pl.semaphore_signal(barrier, inc=1, device_id=to, device_id_type=MESH)

    def tell(k):
        for to in beside:
            pl.semaphore_signal(met.at[k], inc=1, device_id=to, device_id_type=MESH)

    def hear(k):
        pl.semaphore_wait(met.at[k], len(beside))

    first, second = pl.ds(0, 256), pl.ds(256, 256)
    most, rest = pl.ds(0, 448), pl.ds(448, 64)

    def hops(h):
        return tuple(
            remote(src, dst, kv_send.at[i, h], kv_recv.at[i, h], to)
            for i, (src, dst, to) in enumerate((
                (kv.at[0, h], kv.at[1, h], right),
                (kv.at[0, h], kv.at[2, h], left),
                (kv.at[0, h], kv.at[3, h], cross),
                (kv.at[1, h, first], kv.at[4, h, first], right),
                (kv.at[2, h, second], kv.at[4, h, second], left),
                (kv.at[3, h, most], kv.at[5, h, most], right),
                (kv.at[3, h, most], kv.at[6, h, most], left),
                (kv.at[4, h], kv.at[7, h], cross),
                (kv.at[1, h, rest], kv.at[5, h, rest], cross),
                (kv.at[2, h, rest], kv.at[6, h, rest], cross),
            ))
        )

    links = [hops(h) for h in range(KVH)]

    def start(h, *steps):
        for i in steps:
            links[h][i].start()

    def arrived(h, *steps):
        for i in steps:
            links[h][i].wait_recv()

    def send_own(h):
        own[2 * h].wait()
        own[2 * h + 1].wait()
        start(h, 0, 1, 2)

    own[0].wait()
    own[1].wait()
    pl.semaphore_wait(barrier, len(greeted))
    start(0, 0, 1, 2)
    send_own(1)
    tell(0)

    scale = adv_ref[...].astype(F32) * (1.0 / (128.0 * 256.0))
    column = jnp.broadcast_to(scale, (128, T)).T
    wide = FEATURES // 8

    def cotangent(part):
        cols = slice(part * wide, (part + 1) * wide)
        for at in range(part * wide, (part + 1) * wide, 128):
            cot[:, at:at + 128] = (column * cot[:, at:at + 128].astype(F32)).astype(BF16)
        term = lax.dot_general(
            cot[:, cols], wubuf[:, cols], (((1,), (1,)), ((), ())), preferred_element_type=F32
        )
        if part == 0:
            acc[...] = term
        else:
            acc[...] += term

    loads[0].wait()
    loads[1].wait()
    for part in range(4):
        cotangent(part)
    arrived(0, 0, 1, 2)
    send_own(2)
    hear(0)
    tell(1)
    for part in range(4, 8):
        cotangent(part)
    for half in range(2):
        blh[half] = acc[:, half * 128:(half + 1) * 128].astype(BF16)
    cot_copy = remote(cot, cot2, core_send.at[0], core_recv.at[0], twin)
    cot_copy.start()
    bl_copy = remote(blh.at[1 - core], bl2, core_send.at[1], core_recv.at[1], twin)
    bl_copy.start()
    arrived(1, 0, 1, 2)
    send_own(3)
    start(0, 3, 4, 8, 9)
    start(1, 3, 4, 8, 9)
    hear(1)
    tell(2)

    ctx = yh * 4 + x
    marked = [jnp.int32(0)] * BLOCKS
    cur = ctx
    for _ in range(BLOCKS):
        cur = parents[0, cur]
        marked = [jnp.where(cur == b, 1, marked[b]) for b in range(BLOCKS)]
    for s in range(1, BLOCKS):
        block = (yh if SLOT_ROW[s] == 0 else 1 - yh) * 4 + (x + SLOT_STEP[s]) % 4
        seen = jnp.int32(0)
        for b in range(BLOCKS):
            seen = jnp.where(block == b, marked[b], seen)
        offs[s] = jnp.where(seen > 0, 0.0, MASKED)
    key_pos = lax.broadcasted_iota(jnp.int32, (T, T), 0)
    query_pos = lax.broadcasted_iota(jnp.int32, (T, T), 1)
    of_query = jnp.broadcast_to(branch_ref[...].astype(F32), (T, T))
    of_key = of_query.T
    local = (key_pos <= query_pos) & ((of_key == of_query) | (of_key == 0.0))
    bias[...] = jnp.where(local, 0.0, MASKED)

    def score(h, *slots):
        for s in slots:
            for g in range(GROUP):
                at = (h * GROUP + g) * D
                value = lax.dot_general(
                    kv[s, h, 0:256, :], qbuf[:, at:at + D], (((1,), (1,)), ((), ())), preferred_element_type=F32
                )
                if s == 0:
                    value = value + bias[...]
                scores[h % 2, s % 4, g] = value
                peak = jnp.max(value.reshape(T // 8, 8, T), axis=0)
                if s > 0:
                    peak = peak + offs[s]
                top[h % 2, g] = peak if s % 4 == 0 else jnp.maximum(top[h % 2, g], peak)

    def weigh(h, slots, peak, total, out, g):
        for s in slots:
            shift = peak if s == 0 else peak - offs[s]
            weight = jnp.exp2(scores[h % 2, s % 4, g] * FACTOR - shift)
            total = total + jnp.sum(weight.reshape(T // 8, 8, T), axis=0)
            out = out + jnp.dot(
                vt[h % 2, :, s % 4 * T:(s % 4 + 1) * T], weight.astype(BF16), preferred_element_type=F32
            )
        return total, out

    def turn_values(h, slots):
        for s in slots:
            vt[h % 2, :, s % 4 * T:(s % 4 + 1) * T] = kv[s, h, 256:512, :].astype(F32).T.astype(BF16)

    def early(h):
        score(h, 0, 1, 2, 3)
        turn_values(h, range(4))
        for g in range(GROUP):
            i = h * GROUP + g
            peak = jnp.max(top[h % 2, g], axis=0, keepdims=True) * FACTOR
            peaks[i] = jnp.broadcast_to(peak, (8, T))
            totals[i], outs[i] = weigh(h, range(4), peak, jnp.zeros((8, T), F32), jnp.zeros((D, T), F32), g)

    def late(h):
        turn_values(h, range(4, 8))
        for g in range(GROUP):
            i = h * GROUP + g
            before = peaks[i][0:1]
            peak = jnp.maximum(before, jnp.max(top[h % 2, g], axis=0, keepdims=True) * FACTOR)
            fade = jnp.exp2(before - peak)
            total, out = weigh(h, range(4, 8), peak, totals[i] * fade, outs[i] * fade, g)
            bottom = jnp.sum(total, axis=0, keepdims=True)
            ctx_t[h, g * D:(g + 1) * D, :] = (out / bottom).astype(BF16)

    ctx_copies = [
        remote(ctx_t.at[h], ctx2.at[h], core_send.at[2 + h], core_recv.at[2 + h], twin) for h in range(KVH)
    ]

    def after(h):
        if h < KVH - 1:
            ctx_copies[h].start()
        term = jnp.dot(wdt[h], ctx_t[h], preferred_element_type=F32)
        if h == 0:
            low[...] = term
        else:
            low[...] += term

    def band(at):
        return rows16(at * 80, 80)

    z1 = [
        [
            remote(
                downb.at[h, band((z + d) % 8)], zin.at[h, d - 1], z1_send.at[h, d - 1], z1_recv.at[h, d - 1], peers[d - 1]
            )
            for d in range(1, 8)
        ]
        for h in range(KVH)
    ]

    def down_terms(h):
        ctx_copies[h].wait_recv()
        term = jnp.dot(ctx_t[h], blh[core], preferred_element_type=F32)
        term = term + jnp.dot(ctx2[h], bl2[...], preferred_element_type=F32)
        downb[h] = term.astype(BF16)
        for copy in z1[h]:
            copy.start()

    me = y * 4 + x
    z2 = []
    for h in range(KVH):
        for to_yl in range(2):
            to_y = (h // 2) * 2 + to_yl
            to_x = 2 * (h % 2) + z // 4
            z2.append((
                to_y * 4 + to_x != me,
                remote(zs.at[h], zin2.at[me], z2_send.at[h, to_yl], z2_recv.at[me], in_plane(to_y, to_x)),
            ))

    def band_sum(h):
        total = downb[h, band(z), :].astype(F32)
        for d in range(1, 8):
            z1[h][d - 1].wait_recv()
            total = total + zin[h, d - 1].astype(F32)
        zs[h] = total.astype(BF16)
        for elsewhere, copy in z2[2 * h:2 * h + 2]:
            pl.when(elsewhere)(copy.start)

    loads[2].wait()
    early(0)
    loads[3].wait()
    for i in range(KVH * GROUP):
        wdt[i // GROUP, :, i % GROUP * D:(i % GROUP + 1) * D] = wdbuf[i * D:(i + 1) * D, :].astype(F32).T.astype(BF16)

    early(1)
    arrived(2, 0, 1, 2)
    start(2, 3, 4, 8, 9)
    hear(2)
    early(2)
    arrived(3, 0, 1, 2)
    start(3, 3, 4, 8, 9)
    for h in range(KVH):
        start(h, 5, 6)
    early(3)
    for h in range(KVH):
        arrived(h, 3, 4)
        start(h, 7)
        if h < 2:
            score(h, 4)
    bl_copy.wait_recv()
    for h in range(KVH):
        if h >= 2:
            score(h, 4)
        arrived(h, 5, 6)
        score(h, 5, 6)
        arrived(h, 7)
        score(h, 7)
        arrived(h, 8, 9)
        late(h)
        after(h)
        if 1 <= h < KVH - 1:
            down_terms(h - 1)
        if h == KVH - 1:
            break
        if h >= 2:
            band_sum(h - 2)

    for half in range(2):
        lowh[half] = low[half * 128:(half + 1) * 128, :].astype(BF16)
    low_copy = remote(lowh.at[1 - core], low2, core_send.at[6], core_recv.at[6], twin)
    low_copy.start()
    ctx_copies[KVH - 1].start()
    down_terms(2)
    cot_copy.wait_recv()
    low_copy.wait_recv()

    def up_terms(row, col):
        cols = pl.ds(pl.multiple_of((row * 4 + col) * 640, 128), 640)
        term = jnp.dot(lowh[core], cot[:, cols], preferred_element_type=F32)
        term = term + jnp.dot(low2[...], cot2[:, cols], preferred_element_type=F32)
        for j in range(5):
            terms[row, col, j * 128:(j + 1) * 128, :] = term[:, j * 128:(j + 1) * 128].astype(BF16)

    def by_x(col):
        return terms.at[:, col, pl.ds(0, 160)], terms.at[:, col, pl.ds(160, 160)]

    def by_y(at):
        part = rows16(320 + (at % 2) * 160, 160)
        return terms.at[at // 2, pl.ds(0, 2), part], terms.at[at // 2, pl.ds(2, 2), part]

    ring_x = Ring(
        right, left, (by_x(xo), by_x(xp), by_x(xm), by_x(x)),
        [x1.at[i] for i in range(8)], ring_send.at[0], ring_recv.at[0],
    )
    ring_y = Ring(
        plus_y, minus_y, (by_y(yo), by_y(yp), by_y(ym), by_y(y)),
        [y1.at[i] for i in range(8)], ring_send.at[1], ring_recv.at[1],
    )
    up_terms(yh, xo)
    up_terms(1 - yh, xo)
    ring_x.start(0, 1)
    up_terms(1 - yh, x)
    up_terms(1 - yh, xp)
    up_terms(1 - yh, xm)
    ring_y.start(0, 1)
    up_terms(yh, xp)
    up_terms(yh, xm)
    ring_x.start(2, 3)
    up_terms(yh, x)
    ring_y.start(2, 3)
    down_terms(3)
    band_sum(1)
    ring_x.middle()
    ring_y.middle()
    band_sum(2)

    def x_by_y(at):
        return left_x.at[at // 2, rows16((at % 2) * 160, 160)]

    direct_xy = Direct(
        cross, plus_y, minus_y, (x_by_y(yo), x_by_y(yp), x_by_y(ym), x_by_y(y)), x2, dir_send.at[0], dir_recv.at[0]
    )
    direct_yx = Direct(
        in_plane(y, xo), right, left, (left_y.at[xo], left_y.at[xp], left_y.at[xm], left_y.at[x]),
        y2, dir_send.at[1], dir_recv.at[1],
    )
    a, b = ring_x.end()
    left_x[:, 0:160, :] = a.astype(BF16)
    left_x[:, 160:320, :] = b.astype(BF16)
    direct_xy.begin()
    a, b = ring_y.end()
    left_y[0:2] = a.astype(BF16)
    left_y[2:4] = b.astype(BF16)
    direct_yx.begin()

    quarter[0:160] = direct_xy.end().astype(BF16)
    quarter[160:320] = direct_yx.end().astype(BF16)
    quarter[320:384] = jnp.zeros((64, 128), BF16)

    def chunk(at):
        return rows16(at * 48, 48)

    z_copies = []
    for d in range(1, 8):
        copy = remote(
            quarter.at[chunk((z + d) % 8)], pieces.at[d - 1], z_send.at[0, d - 1], z_recv.at[0, d - 1], peers[d - 1]
        )
        copy.start()
        z_copies.append(copy)

    band_sum(3)
    for h in range(KVH):
        for copy in links[h]:
            copy.wait_send()
    for copy in ctx_copies + [cot_copy, bl_copy, low_copy]:
        copy.wait_send()
    ring_x.finish()
    ring_y.finish()
    piece = quarter[chunk(z), :].astype(F32)
    for d in range(1, 8):
        z_copies[d - 1].wait_recv()
        piece = piece + pieces[d - 1].astype(F32)
    final[core, yl, chunk(z), :] = piece.astype(BF16)

    def to_near(d):
        here = final.at[core, yl, chunk((z + 8 - d) % 8)]
        return remote(here, here, near_send.at[d], near_recv.at[d], near)

    near_copies = [to_near(d) for d in range(8)]
    near_copies[0].start()
    for d in range(1, 8):
        here = final.at[core, yl, chunk(z)]
        copy = remote(here, here, z_send.at[1, d - 1], z_recv.at[1, d - 1], peers[d - 1])
        copy.start()
        z_copies.append(copy)

    owner = x % 2 == z // 4
    mine = 2 * yh + x // 2
    spot = rows16((z % 4) * 80, 80)
    z4 = [
        remote(fdown.at[core, spot], fdown.at[core, spot], z4_send.at[d - 1], z4_recv.at[z % 4], peers[d - 1])
        for d in range(1, 8)
    ]

    @pl.when(owner)
    def _():
        for i in range(16):

            @pl.when(i != me)
            def _():
                remote(zs.at[0], zin2.at[i], z2_send.at[0, 0], z2_recv.at[i], twin).wait_recv()

            @pl.when(i == me)
            def _():
                zin2[i] = zs[mine]

        total = zin2[0].astype(F32)
        for i in range(1, 16):
            total = total + zin2[i].astype(F32)
        fdown[core, spot, :] = total.astype(BF16)
        for copy in z4:
            copy.start()

    for h in range(KVH):
        for copy in z1[h]:
            copy.wait_send()
    for elsewhere, copy in z2:
        pl.when(elsewhere)(copy.wait_send)
    for copy in z_copies[:7]:
        copy.wait_send()
    direct_xy.finish()
    direct_yx.finish()
    for d in (1, 7, 2, 6, 3, 5, 4):
        z_copies[6 + d].wait_recv()
        near_copies[d].start()
    here = final.at[core, yl]
    to_twin = remote(here, here, out_send.at[1], out_recv.at[1], twin)
    to_twin.start()
    for i in range(4):
        at = pl.ds(i * 80, 80)
        part = fdown.at[core, at]

        @pl.when(jnp.logical_not(owner) | (z % 4 != i))
        def _():
            remote(part, part, z4_send.at[0], z4_recv.at[i], twin).wait_recv()

    down_out = remote(fdown.at[core], fdown.at[core], out_send.at[3], out_recv.at[3], twin)
    down_out.start()

    there = final.at[core, 1 - yl]
    for copy in near_copies:
        copy.wait_recv()
    on_twin = remote(there, there, out_send.at[2], out_recv.at[2], twin)
    on_twin.start()
    to_twin.wait_recv()
    on_twin.wait_recv()
    down_out.wait_recv()

    @pl.when(owner)
    def _():
        for copy in z4:
            copy.wait_send()

    for copy in z_copies[7:] + near_copies + [down_out, to_twin, on_twin]:
        copy.wait_send()


def lay_out(fdown, final, down_ref, up_ref, rows):
    for k in range(2):
        down_ref[:, k * 128:(k + 1) * 128] = fdown[k].astype(F32)
        for part in range(2):
            rows[k, part * 160:part * 160 + 160, :] = final[k, part, 0:160, :].astype(F32)
            rows[k, 320 + part * 160:480 + part * 160, :] = final[k, part, 160:320, :].astype(F32)
    for k in range(2):
        for j in range(5):
            up_ref[k * 128:(k + 1) * 128, j * 128:(j + 1) * 128] = rows[k, j * 128:(j + 1) * 128, :]


def on_device(q, k, v, og, adv, branch, parents, wd, wu):
    hbm = pl.BlockSpec(memory_space=pl.ANY)
    vmem = pl.BlockSpec(memory_space=pltpu.VMEM)
    dma = pltpu.SemaphoreType.DMA
    sums = pl.pallas_call(
        kernel,
        name="adapter_gradients",
        out_shape=(
            jax.ShapeDtypeStruct((2, 320, 128), BF16),
            jax.ShapeDtypeStruct((2, 2, 384, 128), BF16),
        ),
        in_specs=[pl.BlockSpec(memory_space=pltpu.SMEM), vmem, vmem] + [hbm] * 6,
        out_specs=(vmem, vmem),
        scratch_shapes=[
            pltpu.VMEM((BLOCKS, KVH, 512, D), BF16),
            pltpu.VMEM((T, ATTN), BF16),
                pltpu.VMEM((RANK, FEATURES), BF16),
            pltpu.VMEM((ATTN, RANK), BF16),
            pltpu.VMEM((KVH, RANK, GROUP * D), BF16),
            pltpu.VMEM((T, FEATURES), BF16),
            pltpu.VMEM((T, FEATURES), BF16),
            pltpu.VMEM((T, RANK), F32),
            pltpu.VMEM((2, T, 128), BF16),
            pltpu.VMEM((T, 128), BF16),
            pltpu.VMEM((KVH, GROUP * D, T), BF16),
            pltpu.VMEM((KVH, GROUP * D, T), BF16),
            pltpu.VMEM((RANK, T), F32),
            pltpu.VMEM((2, 128, T), BF16),
            pltpu.VMEM((128, T), BF16),
            pltpu.VMEM((2, 4, GROUP, T, T), F32),
            pltpu.VMEM((2, GROUP, 8, T), F32),
            pltpu.VMEM((T, T), F32),
            pltpu.VMEM((2, D, 4 * T), BF16),
            pltpu.VMEM((KVH * GROUP, 8, T), F32),
            pltpu.VMEM((KVH * GROUP, 8, T), F32),
            pltpu.VMEM((KVH * GROUP, D, T), F32),
            pltpu.SMEM((BLOCKS,), F32),
            pltpu.VMEM((KVH, GROUP * D, 128), BF16),
            pltpu.VMEM((KVH, 7, 80, 128), BF16),
            pltpu.VMEM((KVH, 80, 128), BF16),
            pltpu.VMEM((16, 80, 128), BF16),
            pltpu.VMEM((2, 4, 640, 128), BF16),
            pltpu.VMEM((8, 2, 160, 128), BF16),
            pltpu.VMEM((8, 2, 160, 128), BF16),
            pltpu.VMEM((2, 320, 128), BF16),
            pltpu.VMEM((4, 160, 128), BF16),
            pltpu.VMEM((3, 160, 128), BF16),
            pltpu.VMEM((3, 160, 128), BF16),
            pltpu.VMEM((384, 128), BF16),
            pltpu.VMEM((7, 48, 128), BF16),
            dma((KVH, 2)),
            dma((4,)),
            dma((10, KVH)), dma((10, KVH)),
            dma((7,)), dma((7,)),
            dma((KVH, 7)), dma((KVH, 7)),
            dma((KVH, 2)), dma((16,)),
            dma((7,)), dma((4,)),
            dma((2, 6)), dma((2, 6)),
            dma((2, 3)), dma((2, 3)),
            dma((2, 7)), dma((2, 7)),
            dma((8,)), dma((8,)),
            dma((4,)), dma((4,)),
            pltpu.SemaphoreType.REGULAR((3,)),
        ],
        compiler_params=pltpu.CompilerParams(
            collective_id=0, has_side_effects=True, vmem_limit_bytes=60 * MIB
        ),
    )(parents, adv, branch[0], q[0], k[0], v[0], og[0], wu, wd)
    return pl.pallas_call(
        lay_out,
        name="lay_out",
        out_shape=(
            jax.ShapeDtypeStruct((320, RANK), F32),
            jax.ShapeDtypeStruct((RANK, 640), F32),
        ),
        in_specs=[vmem, vmem],
        out_specs=(vmem, vmem),
        scratch_shapes=[pltpu.VMEM((2, 640, 128), F32)],
    )(*sums)


def solution(mesh):
    return jax.shard_map(
        on_device,
        mesh=mesh,
        in_specs=(
            P("dp", "ctx", None),
            P("dp", "ctx", None),
            P("dp", "ctx", None),
            P("dp", "ctx", None),
            P("dp", "ctx"),
            P("dp", "ctx", None),
            P("dp", None),
            P(),
            P(),
        ),
        out_specs=(P("ctx", None), P(None, "ctx")),
        check_vma=False,
    )
```

```python
import math

import jax
import jax.numpy as jnp
from jax import lax
from jax.experimental import pallas as pl
from jax.experimental.pallas import tpu as pltpu
from jax.sharding import PartitionSpec as P

MESH = pl.DeviceIdType.MESH
BF16 = jnp.bfloat16
F32 = jnp.float32
D = 128
T = 256
KVH = 4
GROUP = 5
BLOCKS = 8
FEATURES = 5120
ATTN = 2560
RANK = 256
MASKED = -1e30
MIB = 1 << 20
FAR_FIRST = (4, 3, 5, 2, 6, 1, 7)
FACTOR = math.log2(math.e) / math.sqrt(D)


def place():
    dp = lax.axis_index("dp")
    ctx = lax.axis_index("ctx")
    return dp // 16, (dp // 2) % 8, dp % 2, ctx // 4, ctx % 4


def device(yl, z, core, yh, x):
    return ((yl * 8 + z) * 2 + core, yh * 4 + x)


def remote(src, dst, send, recv, to):
    return pltpu.make_async_remote_copy(
        src_ref=src, dst_ref=dst, send_sem=send, recv_sem=recv, device_id=to, device_id_type=MESH
    )


def rows16(start, size):
    return pl.ds(pl.multiple_of(start, 16), size)


class Ring:
    def __init__(self, plus, minus, parts, bufs, send, recv):
        self.opposite, self.plus_part, self.minus_part, self.own = parts
        self.bufs = bufs
        opp_a, opp_b, dir_a, dir_b, sum_a, sum_b, out_a, out_b = bufs
        self.copies = tuple(
            remote(src, dst, send.at[i], recv.at[i], to)
            for i, (src, dst, to) in enumerate((
                (self.opposite[0], opp_a, plus),
                (self.opposite[1], opp_b, minus),
                (self.plus_part[1], dir_b, plus),
                (self.minus_part[0], dir_a, minus),
                (out_a, sum_a, plus),
                (out_b, sum_b, minus),
            ))
        )

    def start(self, *which):
        for i in which:
            self.copies[i].start()

    def middle(self):
        opp_a, opp_b, _, _, _, _, out_a, out_b = self.bufs
        self.copies[0].wait_recv()
        out_a[...] = (self.plus_part[0][...].astype(F32) + opp_a[...].astype(F32)).astype(BF16)
        self.copies[4].start()
        self.copies[1].wait_recv()
        out_b[...] = (self.minus_part[1][...].astype(F32) + opp_b[...].astype(F32)).astype(BF16)
        self.copies[5].start()

    def end(self):
        _, _, dir_a, dir_b, sum_a, sum_b, _, _ = self.bufs
        for i in (2, 3, 4, 5):
            self.copies[i].wait_recv()
        a = self.own[0][...].astype(F32) + dir_a[...].astype(F32) + sum_a[...].astype(F32)
        b = self.own[1][...].astype(F32) + dir_b[...].astype(F32) + sum_b[...].astype(F32)
        return a, b

    def finish(self):
        for copy in self.copies:
            copy.wait_send()


class Direct:
    def __init__(self, opposite, plus, minus, parts, bufs, send, recv):
        self.own = parts[3]
        self.bufs = bufs
        self.copies = tuple(
            remote(parts[i], bufs.at[i], send.at[i], recv.at[i], to)
            for i, to in enumerate((opposite, plus, minus))
        )

    def begin(self):
        for copy in self.copies:
            copy.start()

    def end(self):
        total = self.own[...].astype(F32)
        for i in (1, 2, 0):
            self.copies[i].wait_recv()
            total = total + self.bufs[i].astype(F32)
        return total

    def finish(self):
        for copy in self.copies:
            copy.wait_send()


SLOT_ROW = (0, 0, 0, 1, 0, 1, 1, 1)
SLOT_STEP = (0, 3, 1, 0, 2, 3, 1, 2)


def kernel(
    parents, adv_ref, branch_ref, q_hbm, k_hbm, v_hbm, og_hbm, wu_hbm, wd_hbm,
    fdown, final,
    kv, qbuf, wubuf, wdbuf, wdt, cot, cot2, acc, blh, bl2, ctx_t, ctx2, low, lowh, low2,
    scores, top, bias, vt, peaks, totals, outs, offs,
    downb, zin, zs, zin2,
    terms, x1, y1, left_x, left_y, x2, y2, quarter, pieces,
    own_sem, load_sem, kv_send, kv_recv, core_send, core_recv, z1_send, z1_recv, z2_send, z2_recv, z4_send, z4_recv,
    ring_send, ring_recv, dir_send, dir_recv, z_send, z_recv, near_send, near_recv, out_send, out_recv, met,
):
    yl, z, core, yh, x = place()
    y = yh * 2 + yl
    xp, xm, xo = (x + 1) % 4, (x + 3) % 4, (x + 2) % 4
    yp, ym, yo = (y + 1) % 4, (y + 3) % 4, (y + 2) % 4

    def in_plane(to_y, to_x):
        return device(to_y % 2, z, core, to_y // 2, to_x)

    right, left = in_plane(y, xp), in_plane(y, xm)
    plus_y, minus_y, cross = in_plane(yp, x), in_plane(ym, x), in_plane(yo, x)
    near = device(1 - yl, z, core, yh, x)
    twin = device(yl, z, 1 - core, yh, x)
    peers = [device(yl, (z + d) % 8, core, yh, x) for d in range(1, 8)]

    barrier = pltpu.get_barrier_semaphore()
    beside = [right, left, plus_y, minus_y, peers[0], peers[6]]
    greeted = beside + [cross, twin]
    for to in greeted:
        pl.semaphore_signal(barrier, inc=1, device_id=to, device_id_type=MESH)

    own = []
    for h in range(KVH):
        for i, src in enumerate((k_hbm, v_hbm)):
            own.append(
                pltpu.make_async_copy(
                    src.at[:, pl.ds(h * D, D)], kv.at[0, h, pl.ds(i * 256, 256)], own_sem.at[h, i]
                )
            )
            own[-1].start()
    loads = []
    for i, (src, dst) in enumerate(((og_hbm, cot), (wu_hbm, wubuf), (q_hbm, qbuf), (wd_hbm, wdbuf))):
        copy = pltpu.make_async_copy(src, dst, load_sem.at[i])
        copy.start()
        loads.append(copy)

    def tell(k):
        for to in beside:
            pl.semaphore_signal(met.at[k], inc=1, device_id=to, device_id_type=MESH)

    def hear(k):
        pl.semaphore_wait(met.at[k], len(beside))

    first, second = pl.ds(0, 256), pl.ds(256, 256)
    most, rest = pl.ds(0, 448), pl.ds(448, 64)

    def hops(h):
        return tuple(
            remote(src, dst, kv_send.at[i, h], kv_recv.at[i, h], to)
            for i, (src, dst, to) in enumerate((
                (kv.at[0, h], kv.at[1, h], right),
                (kv.at[0, h], kv.at[2, h], left),
                (kv.at[0, h], kv.at[3, h], cross),
                (kv.at[1, h, first], kv.at[4, h, first], right),
                (kv.at[2, h, second], kv.at[4, h, second], left),
                (kv.at[3, h, most], kv.at[5, h, most], right),
                (kv.at[3, h, most], kv.at[6, h, most], left),
                (kv.at[4, h], kv.at[7, h], cross),
                (kv.at[1, h, rest], kv.at[5, h, rest], cross),
                (kv.at[2, h, rest], kv.at[6, h, rest], cross),
            ))
        )

    links = [hops(h) for h in range(KVH)]

    def start(h, *steps):
        for i in steps:
            links[h][i].start()

    def arrived(h, *steps):
        for i in steps:
            links[h][i].wait_recv()

    def send_own(h):
        own[2 * h].wait()
        own[2 * h + 1].wait()
        start(h, 0, 1, 2)

    own[0].wait()
    own[1].wait()
    pl.semaphore_wait(barrier, len(greeted))
    start(0, 0, 1, 2)
    send_own(1)
    tell(0)

    scale = adv_ref[...].astype(F32) * (1.0 / (128.0 * 256.0))
    column = jnp.broadcast_to(scale, (128, T)).T
    wide = FEATURES // 8

    def cotangent(part):
        cols = slice(part * wide, (part + 1) * wide)
        for at in range(part * wide, (part + 1) * wide, 128):
            cot[:, at:at + 128] = (column * cot[:, at:at + 128].astype(F32)).astype(BF16)
        term = lax.dot_general(
            cot[:, cols], wubuf[:, cols], (((1,), (1,)), ((), ())), preferred_element_type=F32
        )
        if part == 0:
            acc[...] = term
        else:
            acc[...] += term

    loads[0].wait()
    loads[1].wait()
    for part in range(4):
        cotangent(part)
    arrived(0, 0, 1, 2)
    send_own(2)
    hear(0)
    tell(1)
    for part in range(4, 8):
        cotangent(part)
    for half in range(2):
        blh[half] = acc[:, half * 128:(half + 1) * 128].astype(BF16)
    cot_copy = remote(cot, cot2, core_send.at[0], core_recv.at[0], twin)
    cot_copy.start()
    bl_copy = remote(blh.at[1 - core], bl2, core_send.at[1], core_recv.at[1], twin)
    bl_copy.start()
    arrived(1, 0, 1, 2)
    send_own(3)
    start(0, 3, 4, 8, 9)
    start(1, 3, 4, 8, 9)
    hear(1)
    tell(2)

    ctx = yh * 4 + x
    marked = [jnp.int32(0)] * BLOCKS
    cur = ctx
    for _ in range(BLOCKS):
        cur = parents[0, cur]
        marked = [jnp.where(cur == b, 1, marked[b]) for b in range(BLOCKS)]
    for s in range(1, BLOCKS):
        block = (yh if SLOT_ROW[s] == 0 else 1 - yh) * 4 + (x + SLOT_STEP[s]) % 4
        seen = jnp.int32(0)
        for b in range(BLOCKS):
            seen = jnp.where(block == b, marked[b], seen)
        offs[s] = jnp.where(seen > 0, 0.0, MASKED)
    key_pos = lax.broadcasted_iota(jnp.int32, (T, T), 0)
    query_pos = lax.broadcasted_iota(jnp.int32, (T, T), 1)
    of_query = jnp.broadcast_to(branch_ref[...].astype(F32), (T, T))
    of_key = of_query.T
    local = (key_pos <= query_pos) & ((of_key == of_query) | (of_key == 0.0))
    bias[...] = jnp.where(local, 0.0, MASKED)

    def score(h, *slots):
        for s in slots:
            for g in range(GROUP):
                at = (h * GROUP + g) * D
                value = lax.dot_general(
                    kv[s, h, 0:256, :], qbuf[:, at:at + D], (((1,), (1,)), ((), ())), preferred_element_type=F32
                )
                if s == 0:
                    value = value + bias[...]
                scores[h % 2, s % 4, g] = value
                peak = jnp.max(value.reshape(T // 8, 8, T), axis=0)
                if s > 0:
                    peak = peak + offs[s]
                top[h % 2, g] = peak if s % 4 == 0 else jnp.maximum(top[h % 2, g], peak)

    def weigh(h, slots, peak, total, out, g):
        for s in slots:
            shift = peak if s == 0 else peak - offs[s]
            weight = jnp.exp2(scores[h % 2, s % 4, g] * FACTOR - shift)
            total = total + jnp.sum(weight.reshape(T // 8, 8, T), axis=0)
            out = out + jnp.dot(
                vt[h % 2, :, s % 4 * T:(s % 4 + 1) * T], weight.astype(BF16), preferred_element_type=F32
            )
        return total, out

    def turn_values(h, slots):
        for s in slots:
            vt[h % 2, :, s % 4 * T:(s % 4 + 1) * T] = kv[s, h, 256:512, :].astype(F32).T.astype(BF16)

    def early(h):
        score(h, 0, 1, 2, 3)
        turn_values(h, range(4))
        for g in range(GROUP):
            i = h * GROUP + g
            peak = jnp.max(top[h % 2, g], axis=0, keepdims=True) * FACTOR
            peaks[i] = jnp.broadcast_to(peak, (8, T))
            totals[i], outs[i] = weigh(h, range(4), peak, jnp.zeros((8, T), F32), jnp.zeros((D, T), F32), g)

    def late(h):
        turn_values(h, range(4, 8))
        for g in range(GROUP):
            i = h * GROUP + g
            before = peaks[i][0:1]
            peak = jnp.maximum(before, jnp.max(top[h % 2, g], axis=0, keepdims=True) * FACTOR)
            fade = jnp.exp2(before - peak)
            total, out = weigh(h, range(4, 8), peak, totals[i] * fade, outs[i] * fade, g)
            bottom = jnp.sum(total, axis=0, keepdims=True)
            ctx_t[h, g * D:(g + 1) * D, :] = (out / bottom).astype(BF16)

    ctx_copies = [
        remote(ctx_t.at[h], ctx2.at[h], core_send.at[2 + h], core_recv.at[2 + h], twin) for h in range(KVH)
    ]

    def after(h):
        if h < KVH - 1:
            ctx_copies[h].start()
        term = jnp.dot(wdt[h], ctx_t[h], preferred_element_type=F32)
        if h == 0:
            low[...] = term
        else:
            low[...] += term

    def band(at):
        return rows16(at * 80, 80)

    z1 = [
        [
            remote(
                downb.at[h, band((z + d) % 8)], zin.at[h, d - 1], z1_send.at[h, d - 1], z1_recv.at[h, d - 1], peers[d - 1]
            )
            for d in range(1, 8)
        ]
        for h in range(KVH)
    ]

    def down_terms(h):
        ctx_copies[h].wait_recv()
        term = jnp.dot(ctx_t[h], blh[core], preferred_element_type=F32)
        term = term + jnp.dot(ctx2[h], bl2[...], preferred_element_type=F32)
        downb[h] = term.astype(BF16)
        for d in FAR_FIRST:
            z1[h][d - 1].start()

    me = y * 4 + x
    z2 = []
    for h in range(KVH):
        for to_yl in range(2):
            to_y = (h // 2) * 2 + to_yl
            to_x = 2 * (h % 2) + z // 4
            z2.append((
                to_y * 4 + to_x != me,
                remote(zs.at[h], zin2.at[me], z2_send.at[h, to_yl], z2_recv.at[me], in_plane(to_y, to_x)),
            ))

    def band_sum(h):
        total = downb[h, band(z), :].astype(F32)
        for d in range(1, 8):
            z1[h][d - 1].wait_recv()
            total = total + zin[h, d - 1].astype(F32)
        zs[h] = total.astype(BF16)
        for elsewhere, copy in z2[2 * h:2 * h + 2]:
            pl.when(elsewhere)(copy.start)

    loads[2].wait()
    early(0)
    loads[3].wait()
    for i in range(KVH * GROUP):
        wdt[i // GROUP, :, i % GROUP * D:(i % GROUP + 1) * D] = wdbuf[i * D:(i + 1) * D, :].astype(F32).T.astype(BF16)

    early(1)
    arrived(2, 0, 1, 2)
    start(2, 3, 4, 8, 9)
    hear(2)
    early(2)
    arrived(3, 0, 1, 2)
    start(3, 3, 4, 8, 9)
    for h in range(KVH):
        start(h, 5, 6)
    early(3)
    for h in range(KVH):
        arrived(h, 3, 4)
        start(h, 7)
        if h < 2:
            score(h, 4)
    bl_copy.wait_recv()
    for h in range(KVH):
        if h >= 2:
            score(h, 4)
        arrived(h, 5, 6)
        score(h, 5, 6)
        arrived(h, 7)
        score(h, 7)
        arrived(h, 8, 9)
        late(h)
        after(h)
        if 1 <= h < KVH - 1:
            down_terms(h - 1)
        if h == KVH - 1:
            break
        if h >= 2:
            band_sum(h - 2)

    for half in range(2):
        lowh[half] = low[half * 128:(half + 1) * 128, :].astype(BF16)
    low_copy = remote(lowh.at[1 - core], low2, core_send.at[6], core_recv.at[6], twin)
    low_copy.start()
    ctx_copies[KVH - 1].start()
    down_terms(2)
    cot_copy.wait_recv()
    low_copy.wait_recv()

    def up_terms(row, col):
        cols = pl.ds(pl.multiple_of((row * 4 + col) * 640, 128), 640)
        term = jnp.dot(lowh[core], cot[:, cols], preferred_element_type=F32)
        term = term + jnp.dot(low2[...], cot2[:, cols], preferred_element_type=F32)
        for j in range(5):
            terms[row, col, j * 128:(j + 1) * 128, :] = term[:, j * 128:(j + 1) * 128].astype(BF16)

    def by_x(col):
        return terms.at[:, col, pl.ds(0, 160)], terms.at[:, col, pl.ds(160, 160)]

    def by_y(at):
        part = rows16(320 + (at % 2) * 160, 160)
        return terms.at[at // 2, pl.ds(0, 2), part], terms.at[at // 2, pl.ds(2, 2), part]

    ring_x = Ring(
        right, left, (by_x(xo), by_x(xp), by_x(xm), by_x(x)),
        [x1.at[i] for i in range(8)], ring_send.at[0], ring_recv.at[0],
    )
    ring_y = Ring(
        plus_y, minus_y, (by_y(yo), by_y(yp), by_y(ym), by_y(y)),
        [y1.at[i] for i in range(8)], ring_send.at[1], ring_recv.at[1],
    )
    up_terms(yh, xo)
    up_terms(1 - yh, xo)
    ring_x.start(0, 1)
    up_terms(1 - yh, x)
    up_terms(1 - yh, xp)
    up_terms(1 - yh, xm)
    ring_y.start(0, 1)
    up_terms(yh, xp)
    up_terms(yh, xm)
    ring_x.start(2, 3)
    up_terms(yh, x)
    ring_y.start(2, 3)
    down_terms(3)
    band_sum(1)
    ring_x.middle()
    ring_y.middle()
    band_sum(2)

    def x_by_y(at):
        return left_x.at[at // 2, rows16((at % 2) * 160, 160)]

    direct_xy = Direct(
        cross, plus_y, minus_y, (x_by_y(yo), x_by_y(yp), x_by_y(ym), x_by_y(y)), x2, dir_send.at[0], dir_recv.at[0]
    )
    direct_yx = Direct(
        in_plane(y, xo), right, left, (left_y.at[xo], left_y.at[xp], left_y.at[xm], left_y.at[x]),
        y2, dir_send.at[1], dir_recv.at[1],
    )
    a, b = ring_x.end()
    left_x[:, 0:160, :] = a.astype(BF16)
    left_x[:, 160:320, :] = b.astype(BF16)
    direct_xy.begin()
    a, b = ring_y.end()
    left_y[0:2] = a.astype(BF16)
    left_y[2:4] = b.astype(BF16)
    direct_yx.begin()

    quarter[0:160] = direct_xy.end().astype(BF16)
    quarter[160:320] = direct_yx.end().astype(BF16)
    quarter[320:384] = jnp.zeros((64, 128), BF16)

    def chunk(at):
        return rows16(at * 48, 48)

    z_copies = [
        remote(
            quarter.at[chunk((z + d) % 8)], pieces.at[d - 1], z_send.at[0, d - 1], z_recv.at[0, d - 1], peers[d - 1]
        )
        for d in range(1, 8)
    ]
    for d in FAR_FIRST:
        z_copies[d - 1].start()

    band_sum(3)
    for h in range(KVH):
        for copy in links[h]:
            copy.wait_send()
    for copy in ctx_copies + [cot_copy, bl_copy, low_copy]:
        copy.wait_send()
    ring_x.finish()
    ring_y.finish()
    piece = quarter[chunk(z), :].astype(F32)
    for d in range(1, 8):
        z_copies[d - 1].wait_recv()
        piece = piece + pieces[d - 1].astype(F32)
    final[core, yl, chunk(z), :] = piece.astype(BF16)

    def to_near(d):
        here = final.at[core, yl, chunk((z + 8 - d) % 8)]
        return remote(here, here, near_send.at[d], near_recv.at[d], near)

    near_copies = [to_near(d) for d in range(8)]
    here = final.at[core, yl, chunk(z)]
    z_copies += [
        remote(here, here, z_send.at[1, d - 1], z_recv.at[1, d - 1], peers[d - 1]) for d in range(1, 8)
    ]
    for d in FAR_FIRST:
        z_copies[6 + d].start()
    near_copies[0].start()

    owner = x % 2 == z // 4
    mine = 2 * yh + x // 2
    spot = rows16((z % 4) * 80, 80)
    z4 = [
        remote(fdown.at[core, spot], fdown.at[core, spot], z4_send.at[d - 1], z4_recv.at[z % 4], peers[d - 1])
        for d in range(1, 8)
    ]

    @pl.when(owner)
    def _():
        for i in range(16):

            @pl.when(i != me)
            def _():
                remote(zs.at[0], zin2.at[i], z2_send.at[0, 0], z2_recv.at[i], twin).wait_recv()

            @pl.when(i == me)
            def _():
                zin2[i] = zs[mine]

        total = zin2[0].astype(F32)
        for i in range(1, 16):
            total = total + zin2[i].astype(F32)
        fdown[core, spot, :] = total.astype(BF16)
        for d in FAR_FIRST:
            z4[d - 1].start()

    for h in range(KVH):
        for copy in z1[h]:
            copy.wait_send()
    for elsewhere, copy in z2:
        pl.when(elsewhere)(copy.wait_send)
    for copy in z_copies[:7]:
        copy.wait_send()
    direct_xy.finish()
    direct_yx.finish()
    for d in (1, 7, 2, 6, 3, 5, 4):
        z_copies[6 + d].wait_recv()
        near_copies[d].start()
    here = final.at[core, yl]
    to_twin = remote(here, here, out_send.at[1], out_recv.at[1], twin)
    to_twin.start()
    for i in range(4):
        at = pl.ds(i * 80, 80)
        part = fdown.at[core, at]

        @pl.when(jnp.logical_not(owner) | (z % 4 != i))
        def _():
            remote(part, part, z4_send.at[0], z4_recv.at[i], twin).wait_recv()

    down_out = remote(fdown.at[core], fdown.at[core], out_send.at[3], out_recv.at[3], twin)
    down_out.start()

    there = final.at[core, 1 - yl]
    for copy in near_copies:
        copy.wait_recv()
    on_twin = remote(there, there, out_send.at[2], out_recv.at[2], twin)
    on_twin.start()
    to_twin.wait_recv()
    on_twin.wait_recv()
    down_out.wait_recv()

    @pl.when(owner)
    def _():
        for copy in z4:
            copy.wait_send()

    for copy in z_copies[7:] + near_copies + [down_out, to_twin, on_twin]:
        copy.wait_send()


def lay_out(fdown, final, down_ref, up_ref, rows):
    for k in range(2):
        down_ref[:, k * 128:(k + 1) * 128] = fdown[k].astype(F32)
        for part in range(2):
            rows[k, part * 160:part * 160 + 160, :] = final[k, part, 0:160, :].astype(F32)
            rows[k, 320 + part * 160:480 + part * 160, :] = final[k, part, 160:320, :].astype(F32)
    for k in range(2):
        for j in range(5):
            up_ref[k * 128:(k + 1) * 128, j * 128:(j + 1) * 128] = rows[k, j * 128:(j + 1) * 128, :]


def on_device(q, k, v, og, adv, branch, parents, wd, wu):
    hbm = pl.BlockSpec(memory_space=pl.ANY)
    vmem = pl.BlockSpec(memory_space=pltpu.VMEM)
    dma = pltpu.SemaphoreType.DMA
    sums = pl.pallas_call(
        kernel,
        name="adapter_gradients",
        out_shape=(
            jax.ShapeDtypeStruct((2, 320, 128), BF16),
            jax.ShapeDtypeStruct((2, 2, 384, 128), BF16),
        ),
        in_specs=[pl.BlockSpec(memory_space=pltpu.SMEM), vmem, vmem] + [hbm] * 6,
        out_specs=(vmem, vmem),
        scratch_shapes=[
            pltpu.VMEM((BLOCKS, KVH, 512, D), BF16),
            pltpu.VMEM((T, ATTN), BF16),
                pltpu.VMEM((RANK, FEATURES), BF16),
            pltpu.VMEM((ATTN, RANK), BF16),
            pltpu.VMEM((KVH, RANK, GROUP * D), BF16),
            pltpu.VMEM((T, FEATURES), BF16),
            pltpu.VMEM((T, FEATURES), BF16),
            pltpu.VMEM((T, RANK), F32),
            pltpu.VMEM((2, T, 128), BF16),
            pltpu.VMEM((T, 128), BF16),
            pltpu.VMEM((KVH, GROUP * D, T), BF16),
            pltpu.VMEM((KVH, GROUP * D, T), BF16),
            pltpu.VMEM((RANK, T), F32),
            pltpu.VMEM((2, 128, T), BF16),
            pltpu.VMEM((128, T), BF16),
            pltpu.VMEM((2, 4, GROUP, T, T), F32),
            pltpu.VMEM((2, GROUP, 8, T), F32),
            pltpu.VMEM((T, T), F32),
            pltpu.VMEM((2, D, 4 * T), BF16),
            pltpu.VMEM((KVH * GROUP, 8, T), F32),
            pltpu.VMEM((KVH * GROUP, 8, T), F32),
            pltpu.VMEM((KVH * GROUP, D, T), F32),
            pltpu.SMEM((BLOCKS,), F32),
            pltpu.VMEM((KVH, GROUP * D, 128), BF16),
            pltpu.VMEM((KVH, 7, 80, 128), BF16),
            pltpu.VMEM((KVH, 80, 128), BF16),
            pltpu.VMEM((16, 80, 128), BF16),
            pltpu.VMEM((2, 4, 640, 128), BF16),
            pltpu.VMEM((8, 2, 160, 128), BF16),
            pltpu.VMEM((8, 2, 160, 128), BF16),
            pltpu.VMEM((2, 320, 128), BF16),
            pltpu.VMEM((4, 160, 128), BF16),
            pltpu.VMEM((3, 160, 128), BF16),
            pltpu.VMEM((3, 160, 128), BF16),
            pltpu.VMEM((384, 128), BF16),
            pltpu.VMEM((7, 48, 128), BF16),
            dma((KVH, 2)),
            dma((4,)),
            dma((10, KVH)), dma((10, KVH)),
            dma((7,)), dma((7,)),
            dma((KVH, 7)), dma((KVH, 7)),
            dma((KVH, 2)), dma((16,)),
            dma((7,)), dma((4,)),
            dma((2, 6)), dma((2, 6)),
            dma((2, 3)), dma((2, 3)),
            dma((2, 7)), dma((2, 7)),
            dma((8,)), dma((8,)),
            dma((4,)), dma((4,)),
            pltpu.SemaphoreType.REGULAR((3,)),
        ],
        compiler_params=pltpu.CompilerParams(
            collective_id=0, has_side_effects=True, vmem_limit_bytes=60 * MIB
        ),
    )(parents, adv, branch[0], q[0], k[0], v[0], og[0], wu, wd)
    return pl.pallas_call(
        lay_out,
        name="lay_out",
        out_shape=(
            jax.ShapeDtypeStruct((320, RANK), F32),
            jax.ShapeDtypeStruct((RANK, 640), F32),
        ),
        in_specs=[vmem, vmem],
        out_specs=(vmem, vmem),
        scratch_shapes=[pltpu.VMEM((2, 640, 128), F32)],
    )(*sums)


def solution(mesh):
    return jax.shard_map(
        on_device,
        mesh=mesh,
        in_specs=(
            P("dp", "ctx", None),
            P("dp", "ctx", None),
            P("dp", "ctx", None),
            P("dp", "ctx", None),
            P("dp", "ctx"),
            P("dp", "ctx", None),
            P("dp", None),
            P(),
            P(),
        ),
        out_specs=(P("ctx", None), P(None, "ctx")),
        check_vma=False,
    )
```

```python
import math

import jax
import jax.numpy as jnp
from jax import lax
from jax.experimental import pallas as pl
from jax.experimental.pallas import tpu as pltpu
from jax.sharding import PartitionSpec as P

MESH = pl.DeviceIdType.MESH
BF16 = jnp.bfloat16
F32 = jnp.float32
D = 128
T = 256
KVH = 4
GROUP = 5
BLOCKS = 8
FEATURES = 5120
ATTN = 2560
RANK = 256
MASKED = -1e30
MIB = 1 << 20
FAR_FIRST = (4, 3, 5, 2, 6, 1, 7)
FACTOR = math.log2(math.e) / math.sqrt(D)


def place():
    dp = lax.axis_index("dp")
    ctx = lax.axis_index("ctx")
    return dp // 16, (dp // 2) % 8, dp % 2, ctx // 4, ctx % 4


def device(yl, z, core, yh, x):
    return ((yl * 8 + z) * 2 + core, yh * 4 + x)


def remote(src, dst, send, recv, to):
    return pltpu.make_async_remote_copy(
        src_ref=src, dst_ref=dst, send_sem=send, recv_sem=recv, device_id=to, device_id_type=MESH
    )


def rows16(start, size):
    return pl.ds(pl.multiple_of(start, 16), size)


class Ring:
    def __init__(self, plus, minus, parts, bufs, send, recv):
        self.opposite, self.plus_part, self.minus_part, self.own = parts
        self.bufs = bufs
        opp_a, opp_b, dir_a, dir_b, sum_a, sum_b, out_a, out_b = bufs
        self.copies = tuple(
            remote(src, dst, send.at[i], recv.at[i], to)
            for i, (src, dst, to) in enumerate((
                (self.opposite[0], opp_a, plus),
                (self.opposite[1], opp_b, minus),
                (self.plus_part[1], dir_b, plus),
                (self.minus_part[0], dir_a, minus),
                (out_a, sum_a, plus),
                (out_b, sum_b, minus),
            ))
        )

    def start(self, *which):
        for i in which:
            self.copies[i].start()

    def middle(self):
        opp_a, opp_b, _, _, _, _, out_a, out_b = self.bufs
        self.copies[0].wait_recv()
        out_a[...] = (self.plus_part[0][...].astype(F32) + opp_a[...].astype(F32)).astype(BF16)
        self.copies[4].start()
        self.copies[1].wait_recv()
        out_b[...] = (self.minus_part[1][...].astype(F32) + opp_b[...].astype(F32)).astype(BF16)
        self.copies[5].start()

    def end(self):
        _, _, dir_a, dir_b, sum_a, sum_b, _, _ = self.bufs
        for i in (2, 3, 4, 5):
            self.copies[i].wait_recv()
        a = self.own[0][...].astype(F32) + dir_a[...].astype(F32) + sum_a[...].astype(F32)
        b = self.own[1][...].astype(F32) + dir_b[...].astype(F32) + sum_b[...].astype(F32)
        return a, b

    def finish(self):
        for copy in self.copies:
            copy.wait_send()


class Direct:
    def __init__(self, opposite, plus, minus, parts, bufs, send, recv):
        self.own = parts[3]
        self.bufs = bufs
        self.copies = tuple(
            remote(parts[i], bufs.at[i], send.at[i], recv.at[i], to)
            for i, to in enumerate((opposite, plus, minus))
        )

    def begin(self):
        for copy in self.copies:
            copy.start()

    def end(self):
        total = self.own[...].astype(F32)
        for i in (1, 2, 0):
            self.copies[i].wait_recv()
            total = total + self.bufs[i].astype(F32)
        return total

    def finish(self):
        for copy in self.copies:
            copy.wait_send()


SLOT_ROW = (0, 0, 0, 1, 0, 1, 1, 1)
SLOT_STEP = (0, 3, 1, 0, 2, 3, 1, 2)


def kernel(
    parents, adv_ref, branch_ref, q_hbm, k_hbm, v_hbm, og_hbm, wu_hbm, wd_hbm,
    fdown, final,
    kv, qbuf, wubuf, wdbuf, wdt, cot, cot2, acc, blh, bl2, ctx_t, ctx2, low, lowh, low2,
    scores, top, bias, vt, peaks, totals, outs, offs,
    downb, zin, zs, zin2,
    terms, x1, y1, left_x, left_y, x2, y2, quarter, pieces,
    own_sem, load_sem, kv_send, kv_recv, core_send, core_recv, z1_send, z1_recv, z2_send, z2_recv, z4_send, z4_recv,
    ring_send, ring_recv, dir_send, dir_recv, z_send, z_recv, near_send, near_recv, diag_send, diag_recv, out_send, out_recv, met,
):
    yl, z, core, yh, x = place()
    y = yh * 2 + yl
    xp, xm, xo = (x + 1) % 4, (x + 3) % 4, (x + 2) % 4
    yp, ym, yo = (y + 1) % 4, (y + 3) % 4, (y + 2) % 4

    def in_plane(to_y, to_x):
        return device(to_y % 2, z, core, to_y // 2, to_x)

    right, left = in_plane(y, xp), in_plane(y, xm)
    plus_y, minus_y, cross = in_plane(yp, x), in_plane(ym, x), in_plane(yo, x)
    near = device(1 - yl, z, core, yh, x)
    twin = device(yl, z, 1 - core, yh, x)
    diag = device(1 - yl, z, 1 - core, yh, x)
    peers = [device(yl, (z + d) % 8, core, yh, x) for d in range(1, 8)]

    barrier = pltpu.get_barrier_semaphore()
    beside = [right, left, plus_y, minus_y, peers[0], peers[6]]
    greeted = beside + [cross, twin]
    for to in greeted:
        pl.semaphore_signal(barrier, inc=1, device_id=to, device_id_type=MESH)

    own = []
    for h in range(KVH):
        for i, src in enumerate((k_hbm, v_hbm)):
            own.append(
                pltpu.make_async_copy(
                    src.at[:, pl.ds(h * D, D)], kv.at[0, h, pl.ds(i * 256, 256)], own_sem.at[h, i]
                )
            )
            own[-1].start()
    loads = []
    for i, (src, dst) in enumerate(((og_hbm, cot), (wu_hbm, wubuf), (q_hbm, qbuf), (wd_hbm, wdbuf))):
        copy = pltpu.make_async_copy(src, dst, load_sem.at[i])
        copy.start()
        loads.append(copy)

    def tell(k):
        for to in beside:
            pl.semaphore_signal(met.at[k], inc=1, device_id=to, device_id_type=MESH)

    def hear(k):
        pl.semaphore_wait(met.at[k], len(beside))

    first, second = pl.ds(0, 256), pl.ds(256, 256)
    most, rest = pl.ds(0, 448), pl.ds(448, 64)

    def hops(h):
        return tuple(
            remote(src, dst, kv_send.at[i, h], kv_recv.at[i, h], to)
            for i, (src, dst, to) in enumerate((
                (kv.at[0, h], kv.at[1, h], right),
                (kv.at[0, h], kv.at[2, h], left),
                (kv.at[0, h], kv.at[3, h], cross),
                (kv.at[1, h, first], kv.at[4, h, first], right),
                (kv.at[2, h, second], kv.at[4, h, second], left),
                (kv.at[3, h, most], kv.at[5, h, most], right),
                (kv.at[3, h, most], kv.at[6, h, most], left),
                (kv.at[4, h], kv.at[7, h], cross),
                (kv.at[1, h, rest], kv.at[5, h, rest], cross),
                (kv.at[2, h, rest], kv.at[6, h, rest], cross),
            ))
        )

    links = [hops(h) for h in range(KVH)]

    def start(h, *steps):
        for i in steps:
            links[h][i].start()

    def arrived(h, *steps):
        for i in steps:
            links[h][i].wait_recv()

    def send_own(h):
        own[2 * h].wait()
        own[2 * h + 1].wait()
        start(h, 0, 1, 2)

    own[0].wait()
    own[1].wait()
    pl.semaphore_wait(barrier, len(greeted))
    start(0, 0, 1, 2)
    send_own(1)
    tell(0)

    scale = adv_ref[...].astype(F32) * (1.0 / (128.0 * 256.0))
    column = jnp.broadcast_to(scale, (128, T)).T
    wide = FEATURES // 8

    def cotangent(part):
        cols = slice(part * wide, (part + 1) * wide)
        for at in range(part * wide, (part + 1) * wide, 128):
            cot[:, at:at + 128] = (column * cot[:, at:at + 128].astype(F32)).astype(BF16)
        term = lax.dot_general(
            cot[:, cols], wubuf[:, cols], (((1,), (1,)), ((), ())), preferred_element_type=F32
        )
        if part == 0:
            acc[...] = term
        else:
            acc[...] += term

    loads[0].wait()
    loads[1].wait()
    for part in range(4):
        cotangent(part)
    arrived(0, 0, 1, 2)
    send_own(2)
    hear(0)
    tell(1)
    for part in range(4, 8):
        cotangent(part)
    for half in range(2):
        blh[half] = acc[:, half * 128:(half + 1) * 128].astype(BF16)
    cot_copy = remote(cot, cot2, core_send.at[0], core_recv.at[0], twin)
    cot_copy.start()
    bl_copy = remote(blh.at[1 - core], bl2, core_send.at[1], core_recv.at[1], twin)
    bl_copy.start()
    arrived(1, 0, 1, 2)
    send_own(3)
    start(0, 3, 4, 8, 9)
    start(1, 3, 4, 8, 9)
    hear(1)
    tell(2)

    ctx = yh * 4 + x
    marked = [jnp.int32(0)] * BLOCKS
    cur = ctx
    for _ in range(BLOCKS):
        cur = parents[0, cur]
        marked = [jnp.where(cur == b, 1, marked[b]) for b in range(BLOCKS)]
    for s in range(1, BLOCKS):
        block = (yh if SLOT_ROW[s] == 0 else 1 - yh) * 4 + (x + SLOT_STEP[s]) % 4
        seen = jnp.int32(0)
        for b in range(BLOCKS):
            seen = jnp.where(block == b, marked[b], seen)
        offs[s] = jnp.where(seen > 0, 0.0, MASKED)
    key_pos = lax.broadcasted_iota(jnp.int32, (T, T), 0)
    query_pos = lax.broadcasted_iota(jnp.int32, (T, T), 1)
    of_query = jnp.broadcast_to(branch_ref[...].astype(F32), (T, T))
    of_key = of_query.T
    local = (key_pos <= query_pos) & ((of_key == of_query) | (of_key == 0.0))
    bias[...] = jnp.where(local, 0.0, MASKED)

    def score(h, *slots):
        for s in slots:
            for g in range(GROUP):
                at = (h * GROUP + g) * D
                value = lax.dot_general(
                    kv[s, h, 0:256, :], qbuf[:, at:at + D], (((1,), (1,)), ((), ())), preferred_element_type=F32
                )
                if s == 0:
                    value = value + bias[...]
                scores[h % 2, s % 4, g] = value
                peak = jnp.max(value.reshape(T // 8, 8, T), axis=0)
                if s > 0:
                    peak = peak + offs[s]
                top[h % 2, g] = peak if s % 4 == 0 else jnp.maximum(top[h % 2, g], peak)

    def weigh(h, slots, peak, total, out, g):
        for s in slots:
            shift = peak if s == 0 else peak - offs[s]
            weight = jnp.exp2(scores[h % 2, s % 4, g] * FACTOR - shift)
            total = total + jnp.sum(weight.reshape(T // 8, 8, T), axis=0)
            out = out + jnp.dot(
                vt[h % 2, :, s % 4 * T:(s % 4 + 1) * T], weight.astype(BF16), preferred_element_type=F32
            )
        return total, out

    def turn_values(h, slots):
        for s in slots:
            vt[h % 2, :, s % 4 * T:(s % 4 + 1) * T] = kv[s, h, 256:512, :].astype(F32).T.astype(BF16)

    def early(h):
        score(h, 0, 1, 2, 3)
        turn_values(h, range(4))
        for g in range(GROUP):
            i = h * GROUP + g
            peak = jnp.max(top[h % 2, g], axis=0, keepdims=True) * FACTOR
            peaks[i] = jnp.broadcast_to(peak, (8, T))
            totals[i], outs[i] = weigh(h, range(4), peak, jnp.zeros((8, T), F32), jnp.zeros((D, T), F32), g)

    def late(h):
        turn_values(h, range(4, 8))
        for g in range(GROUP):
            i = h * GROUP + g
            before = peaks[i][0:1]
            peak = jnp.maximum(before, jnp.max(top[h % 2, g], axis=0, keepdims=True) * FACTOR)
            fade = jnp.exp2(before - peak)
            total, out = weigh(h, range(4, 8), peak, totals[i] * fade, outs[i] * fade, g)
            bottom = jnp.sum(total, axis=0, keepdims=True)
            ctx_t[h, g * D:(g + 1) * D, :] = (out / bottom).astype(BF16)

    ctx_copies = [
        remote(ctx_t.at[h], ctx2.at[h], core_send.at[2 + h], core_recv.at[2 + h], twin) for h in range(KVH)
    ]

    def after(h):
        if h < KVH - 1:
            ctx_copies[h].start()
        term = jnp.dot(wdt[h], ctx_t[h], preferred_element_type=F32)
        if h == 0:
            low[...] = term
        else:
            low[...] += term

    def band(at):
        return rows16(at * 80, 80)

    z1 = [
        [
            remote(
                downb.at[h, band((z + d) % 8)], zin.at[h, d - 1], z1_send.at[h, d - 1], z1_recv.at[h, d - 1], peers[d - 1]
            )
            for d in range(1, 8)
        ]
        for h in range(KVH)
    ]

    def down_terms(h):
        ctx_copies[h].wait_recv()
        term = jnp.dot(ctx_t[h], blh[core], preferred_element_type=F32)
        term = term + jnp.dot(ctx2[h], bl2[...], preferred_element_type=F32)
        downb[h] = term.astype(BF16)
        for d in FAR_FIRST:
            z1[h][d - 1].start()

    me = y * 4 + x
    z2 = []
    for h in range(KVH):
        for to_yl in range(2):
            to_y = (h // 2) * 2 + to_yl
            to_x = 2 * (h % 2) + z // 4
            z2.append((
                to_y * 4 + to_x != me,
                remote(zs.at[h], zin2.at[me], z2_send.at[h, to_yl], z2_recv.at[me], in_plane(to_y, to_x)),
            ))

    def band_sum(h):
        total = downb[h, band(z), :].astype(F32)
        for d in range(1, 8):
            z1[h][d - 1].wait_recv()
            total = total + zin[h, d - 1].astype(F32)
        zs[h] = total.astype(BF16)
        for elsewhere, copy in z2[2 * h:2 * h + 2]:
            pl.when(elsewhere)(copy.start)

    loads[2].wait()
    early(0)
    loads[3].wait()
    for i in range(KVH * GROUP):
        wdt[i // GROUP, :, i % GROUP * D:(i % GROUP + 1) * D] = wdbuf[i * D:(i + 1) * D, :].astype(F32).T.astype(BF16)

    early(1)
    arrived(2, 0, 1, 2)
    start(2, 3, 4, 8, 9)
    hear(2)
    early(2)
    arrived(3, 0, 1, 2)
    start(3, 3, 4, 8, 9)
    for h in range(KVH):
        start(h, 5, 6)
    early(3)
    for h in range(KVH):
        arrived(h, 3, 4)
        start(h, 7)
        if h < 2:
            score(h, 4)
    bl_copy.wait_recv()
    for h in range(KVH):
        if h >= 2:
            score(h, 4)
        arrived(h, 5, 6)
        score(h, 5, 6)
        arrived(h, 7)
        score(h, 7)
        arrived(h, 8, 9)
        late(h)
        after(h)
        if 1 <= h < KVH - 1:
            down_terms(h - 1)
        if h == KVH - 1:
            break
        if h >= 2:
            band_sum(h - 2)

    for half in range(2):
        lowh[half] = low[half * 128:(half + 1) * 128, :].astype(BF16)
    low_copy = remote(lowh.at[1 - core], low2, core_send.at[6], core_recv.at[6], twin)
    low_copy.start()
    ctx_copies[KVH - 1].start()
    down_terms(2)
    cot_copy.wait_recv()
    low_copy.wait_recv()

    def up_terms(row, col):
        cols = pl.ds(pl.multiple_of((row * 4 + col) * 640, 128), 640)
        term = jnp.dot(lowh[core], cot[:, cols], preferred_element_type=F32)
        term = term + jnp.dot(low2[...], cot2[:, cols], preferred_element_type=F32)
        for j in range(5):
            terms[row, col, j * 128:(j + 1) * 128, :] = term[:, j * 128:(j + 1) * 128].astype(BF16)

    def by_x(col):
        return terms.at[:, col, pl.ds(0, 160)], terms.at[:, col, pl.ds(160, 160)]

    def by_y(at):
        part = rows16(320 + (at % 2) * 160, 160)
        return terms.at[at // 2, pl.ds(0, 2), part], terms.at[at // 2, pl.ds(2, 2), part]

    ring_x = Ring(
        right, left, (by_x(xo), by_x(xp), by_x(xm), by_x(x)),
        [x1.at[i] for i in range(8)], ring_send.at[0], ring_recv.at[0],
    )
    ring_y = Ring(
        plus_y, minus_y, (by_y(yo), by_y(yp), by_y(ym), by_y(y)),
        [y1.at[i] for i in range(8)], ring_send.at[1], ring_recv.at[1],
    )
    up_terms(yh, xo)
    up_terms(1 - yh, xo)
    ring_x.start(0, 1)
    up_terms(1 - yh, x)
    up_terms(1 - yh, xp)
    up_terms(1 - yh, xm)
    ring_y.start(0, 1)
    up_terms(yh, xp)
    up_terms(yh, xm)
    ring_x.start(2, 3)
    up_terms(yh, x)
    ring_y.start(2, 3)
    down_terms(3)
    band_sum(1)
    ring_x.middle()
    ring_y.middle()
    band_sum(2)

    def x_by_y(at):
        return left_x.at[at // 2, rows16((at % 2) * 160, 160)]

    direct_xy = Direct(
        cross, plus_y, minus_y, (x_by_y(yo), x_by_y(yp), x_by_y(ym), x_by_y(y)), x2, dir_send.at[0], dir_recv.at[0]
    )
    direct_yx = Direct(
        in_plane(y, xo), right, left, (left_y.at[xo], left_y.at[xp], left_y.at[xm], left_y.at[x]),
        y2, dir_send.at[1], dir_recv.at[1],
    )
    a, b = ring_x.end()
    left_x[:, 0:160, :] = a.astype(BF16)
    left_x[:, 160:320, :] = b.astype(BF16)
    direct_xy.begin()
    a, b = ring_y.end()
    left_y[0:2] = a.astype(BF16)
    left_y[2:4] = b.astype(BF16)
    direct_yx.begin()

    quarter[0:160] = direct_xy.end().astype(BF16)
    quarter[160:320] = direct_yx.end().astype(BF16)
    quarter[320:336] = jnp.zeros((16, 128), BF16)

    def chunk(at):
        return rows16(at * 48, 48)

    z_copies = [
        remote(
            quarter.at[chunk((z + d) % 8)], pieces.at[d - 1], z_send.at[0, d - 1], z_recv.at[0, d - 1], peers[d - 1]
        )
        for d in range(1, 8)
    ]
    filled = [(z + 8 - d) % 8 != 7 for d in range(8)]
    wanted = [(z + d) % 8 != 7 for d in range(8)]
    for d in FAR_FIRST:
        pl.when(wanted[d])(z_copies[d - 1].start)

    band_sum(3)
    for h in range(KVH):
        for copy in links[h]:
            copy.wait_send()
    for copy in ctx_copies + [cot_copy, bl_copy, low_copy]:
        copy.wait_send()
    ring_x.finish()
    ring_y.finish()

    def hand_on(d, sems, to):
        here = final.at[core, yl, chunk((z + 8 - d) % 8)]
        return remote(here, here, sems[0].at[d], sems[1].at[d], to)

    near_copies = [hand_on(d, (near_send, near_recv), near) for d in range(8)]
    diag_copies = [hand_on(d, (diag_send, diag_recv), diag) for d in range(8)]
    here = final.at[core, yl, chunk(z)]
    z_copies += [
        remote(here, here, z_send.at[1, d - 1], z_recv.at[1, d - 1], peers[d - 1]) for d in range(1, 8)
    ]

    @pl.when(filled[0])
    def _():
        piece = quarter[chunk(z), :].astype(F32)
        for d in range(1, 8):
            z_copies[d - 1].wait_recv()
            piece = piece + pieces[d - 1].astype(F32)
        final[core, yl, chunk(z), :] = piece.astype(BF16)
        for d in FAR_FIRST:
            z_copies[6 + d].start()
        near_copies[0].start()
        diag_copies[0].start()

    owner = x % 2 == z // 4
    mine = 2 * yh + x // 2
    spot = rows16((z % 4) * 80, 80)
    z4 = [
        remote(fdown.at[core, spot], fdown.at[core, spot], z4_send.at[d - 1], z4_recv.at[z % 4], peers[d - 1])
        for d in range(1, 8)
    ]

    @pl.when(owner)
    def _():
        for i in range(16):

            @pl.when(i != me)
            def _():
                remote(zs.at[0], zin2.at[i], z2_send.at[0, 0], z2_recv.at[i], twin).wait_recv()

            @pl.when(i == me)
            def _():
                zin2[i] = zs[mine]

        total = zin2[0].astype(F32)
        for i in range(1, 16):
            total = total + zin2[i].astype(F32)
        fdown[core, spot, :] = total.astype(BF16)
        for d in FAR_FIRST:
            z4[d - 1].start()

    for h in range(KVH):
        for copy in z1[h]:
            copy.wait_send()
    for elsewhere, copy in z2:
        pl.when(elsewhere)(copy.wait_send)
    for d in range(1, 8):
        pl.when(wanted[d])(z_copies[d - 1].wait_send)
    direct_xy.finish()
    direct_yx.finish()
    for d in (1, 7, 2, 6, 3, 5, 4):

        @pl.when(filled[d])
        def _():
            z_copies[6 + d].wait_recv()
            near_copies[d].start()
            diag_copies[d].start()

    here = final.at[core, yl, pl.ds(0, 320)]
    to_twin = remote(here, here, out_send.at[1], out_recv.at[1], twin)
    to_twin.start()
    for i in range(4):
        at = pl.ds(i * 80, 80)
        part = fdown.at[core, at]

        @pl.when(jnp.logical_not(owner) | (z % 4 != i))
        def _():
            remote(part, part, z4_send.at[0], z4_recv.at[i], twin).wait_recv()

    down_out = remote(fdown.at[core], fdown.at[core], out_send.at[3], out_recv.at[3], twin)
    down_out.start()

    for d in range(8):
        pl.when(filled[d])(near_copies[d].wait_recv)
        pl.when(filled[d])(diag_copies[d].wait_recv)
    to_twin.wait_recv()
    down_out.wait_recv()

    @pl.when(owner)
    def _():
        for copy in z4:
            copy.wait_send()

    @pl.when(filled[0])
    def _():
        for copy in z_copies[7:]:
            copy.wait_send()

    for d in range(8):
        pl.when(filled[d])(near_copies[d].wait_send)
        pl.when(filled[d])(diag_copies[d].wait_send)
    down_out.wait_send()
    to_twin.wait_send()


def lay_out(fdown, final, down_ref, up_ref, rows):
    for k in range(2):
        down_ref[:, k * 128:(k + 1) * 128] = fdown[k].astype(F32)
        for part in range(2):
            rows[k, part * 160:part * 160 + 160, :] = final[k, part, 0:160, :].astype(F32)
            rows[k, 320 + part * 160:480 + part * 160, :] = final[k, part, 160:320, :].astype(F32)
    for k in range(2):
        for j in range(5):
            up_ref[k * 128:(k + 1) * 128, j * 128:(j + 1) * 128] = rows[k, j * 128:(j + 1) * 128, :]


def on_device(q, k, v, og, adv, branch, parents, wd, wu):
    hbm = pl.BlockSpec(memory_space=pl.ANY)
    vmem = pl.BlockSpec(memory_space=pltpu.VMEM)
    dma = pltpu.SemaphoreType.DMA
    sums = pl.pallas_call(
        kernel,
        name="adapter_gradients",
        out_shape=(
            jax.ShapeDtypeStruct((2, 320, 128), BF16),
            jax.ShapeDtypeStruct((2, 2, 384, 128), BF16),
        ),
        in_specs=[pl.BlockSpec(memory_space=pltpu.SMEM), vmem, vmem] + [hbm] * 6,
        out_specs=(vmem, vmem),
        scratch_shapes=[
            pltpu.VMEM((BLOCKS, KVH, 512, D), BF16),
            pltpu.VMEM((T, ATTN), BF16),
                pltpu.VMEM((RANK, FEATURES), BF16),
            pltpu.VMEM((ATTN, RANK), BF16),
            pltpu.VMEM((KVH, RANK, GROUP * D), BF16),
            pltpu.VMEM((T, FEATURES), BF16),
            pltpu.VMEM((T, FEATURES), BF16),
            pltpu.VMEM((T, RANK), F32),
            pltpu.VMEM((2, T, 128), BF16),
            pltpu.VMEM((T, 128), BF16),
            pltpu.VMEM((KVH, GROUP * D, T), BF16),
            pltpu.VMEM((KVH, GROUP * D, T), BF16),
            pltpu.VMEM((RANK, T), F32),
            pltpu.VMEM((2, 128, T), BF16),
            pltpu.VMEM((128, T), BF16),
            pltpu.VMEM((2, 4, GROUP, T, T), F32),
            pltpu.VMEM((2, GROUP, 8, T), F32),
            pltpu.VMEM((T, T), F32),
            pltpu.VMEM((2, D, 4 * T), BF16),
            pltpu.VMEM((KVH * GROUP, 8, T), F32),
            pltpu.VMEM((KVH * GROUP, 8, T), F32),
            pltpu.VMEM((KVH * GROUP, D, T), F32),
            pltpu.SMEM((BLOCKS,), F32),
            pltpu.VMEM((KVH, GROUP * D, 128), BF16),
            pltpu.VMEM((KVH, 7, 80, 128), BF16),
            pltpu.VMEM((KVH, 80, 128), BF16),
            pltpu.VMEM((16, 80, 128), BF16),
            pltpu.VMEM((2, 4, 640, 128), BF16),
            pltpu.VMEM((8, 2, 160, 128), BF16),
            pltpu.VMEM((8, 2, 160, 128), BF16),
            pltpu.VMEM((2, 320, 128), BF16),
            pltpu.VMEM((4, 160, 128), BF16),
            pltpu.VMEM((3, 160, 128), BF16),
            pltpu.VMEM((3, 160, 128), BF16),
            pltpu.VMEM((384, 128), BF16),
            pltpu.VMEM((7, 48, 128), BF16),
            dma((KVH, 2)),
            dma((4,)),
            dma((10, KVH)), dma((10, KVH)),
            dma((7,)), dma((7,)),
            dma((KVH, 7)), dma((KVH, 7)),
            dma((KVH, 2)), dma((16,)),
            dma((7,)), dma((4,)),
            dma((2, 6)), dma((2, 6)),
            dma((2, 3)), dma((2, 3)),
            dma((2, 7)), dma((2, 7)),
            dma((8,)), dma((8,)),
            dma((8,)), dma((8,)),
            dma((4,)), dma((4,)),
            pltpu.SemaphoreType.REGULAR((3,)),
        ],
        compiler_params=pltpu.CompilerParams(
            collective_id=0, has_side_effects=True, vmem_limit_bytes=60 * MIB
        ),
    )(parents, adv, branch[0], q[0], k[0], v[0], og[0], wu, wd)
    return pl.pallas_call(
        lay_out,
        name="lay_out",
        out_shape=(
            jax.ShapeDtypeStruct((320, RANK), F32),
            jax.ShapeDtypeStruct((RANK, 640), F32),
        ),
        in_specs=[vmem, vmem],
        out_specs=(vmem, vmem),
        scratch_shapes=[pltpu.VMEM((2, 640, 128), F32)],
    )(*sums)


def solution(mesh):
    return jax.shard_map(
        on_device,
        mesh=mesh,
        in_specs=(
            P("dp", "ctx", None),
            P("dp", "ctx", None),
            P("dp", "ctx", None),
            P("dp", "ctx", None),
            P("dp", "ctx"),
            P("dp", "ctx", None),
            P("dp", None),
            P(),
            P(),
        ),
        out_specs=(P("ctx", None), P(None, "ctx")),
        check_vma=False,
    )
```

```python
import math

import jax
import jax.numpy as jnp
from jax import lax
from jax.experimental import pallas as pl
from jax.experimental.pallas import tpu as pltpu
from jax.sharding import PartitionSpec as P

MESH = pl.DeviceIdType.MESH
BF16 = jnp.bfloat16
F32 = jnp.float32
D = 128
T = 256
KVH = 4
GROUP = 5
BLOCKS = 8
FEATURES = 5120
ATTN = 2560
RANK = 256
MASKED = -1e30
MIB = 1 << 20
FAR_FIRST = (4, 3, 5, 2, 6, 1, 7)
FACTOR = math.log2(math.e) / math.sqrt(D)


def place():
    dp = lax.axis_index("dp")
    ctx = lax.axis_index("ctx")
    return dp // 16, (dp // 2) % 8, dp % 2, ctx // 4, ctx % 4


def device(yl, z, core, yh, x):
    return ((yl * 8 + z) * 2 + core, yh * 4 + x)


def remote(src, dst, send, recv, to):
    return pltpu.make_async_remote_copy(
        src_ref=src, dst_ref=dst, send_sem=send, recv_sem=recv, device_id=to, device_id_type=MESH
    )


def rows16(start, size):
    return pl.ds(pl.multiple_of(start, 16), size)


class Ring:
    def __init__(self, plus, minus, parts, bufs, send, recv):
        self.opposite, self.plus_part, self.minus_part, self.own = parts
        self.bufs = bufs
        opp_a, opp_b, dir_a, dir_b, sum_a, sum_b, out_a, out_b = bufs
        self.copies = tuple(
            remote(src, dst, send.at[i], recv.at[i], to)
            for i, (src, dst, to) in enumerate((
                (self.opposite[0], opp_a, plus),
                (self.opposite[1], opp_b, minus),
                (self.plus_part[1], dir_b, plus),
                (self.minus_part[0], dir_a, minus),
                (out_a, sum_a, plus),
                (out_b, sum_b, minus),
            ))
        )

    def start(self, *which):
        for i in which:
            self.copies[i].start()

    def middle(self):
        opp_a, opp_b, _, _, _, _, out_a, out_b = self.bufs
        self.copies[0].wait_recv()
        out_a[...] = (self.plus_part[0][...].astype(F32) + opp_a[...].astype(F32)).astype(BF16)
        self.copies[4].start()
        self.copies[1].wait_recv()
        out_b[...] = (self.minus_part[1][...].astype(F32) + opp_b[...].astype(F32)).astype(BF16)
        self.copies[5].start()

    def end(self):
        _, _, dir_a, dir_b, sum_a, sum_b, _, _ = self.bufs
        for i in (2, 3, 4, 5):
            self.copies[i].wait_recv()
        a = self.own[0][...].astype(F32) + dir_a[...].astype(F32) + sum_a[...].astype(F32)
        b = self.own[1][...].astype(F32) + dir_b[...].astype(F32) + sum_b[...].astype(F32)
        return a, b

    def finish(self):
        for copy in self.copies:
            copy.wait_send()


class Direct:
    def __init__(self, opposite, plus, minus, parts, bufs, send, recv):
        self.own = parts[3]
        self.bufs = bufs
        self.copies = tuple(
            remote(parts[i], bufs.at[i], send.at[i], recv.at[i], to)
            for i, to in enumerate((opposite, plus, minus))
        )

    def begin(self):
        for copy in self.copies:
            copy.start()

    def end(self):
        total = self.own[...].astype(F32)
        for i in (1, 2, 0):
            self.copies[i].wait_recv()
            total = total + self.bufs[i].astype(F32)
        return total

    def finish(self):
        for copy in self.copies:
            copy.wait_send()


SLOT_ROW = (0, 0, 0, 1, 0, 1, 1, 1)
SLOT_STEP = (0, 3, 1, 0, 2, 3, 1, 2)


def kernel(
    parents, adv_ref, branch_ref, q_hbm, k_hbm, v_hbm, og_hbm, wu_hbm, wd_hbm,
    fdown, final,
    kv, qbuf, wubuf, wdbuf, wdt, cot, cot2, acc, blh, bl2, ctx_t, ctx2, low, lowh, low2,
    scores, top, bias, vt, peaks, totals, outs, offs,
    downb, zin, zs, zin2,
    terms, x1, y1, left_x, left_y, x2, y2, quarter, pieces,
    own_sem, load_sem, kv_send, kv_recv, core_send, core_recv, z1_send, z1_recv, z2_send, z2_recv, z4_send, z4_recv,
    ring_send, ring_recv, dir_send, dir_recv, z_send, z_recv, near_send, near_recv, diag_send, diag_recv, out_send, out_recv, met,
):
    yl, z, core, yh, x = place()
    y = yh * 2 + yl
    xp, xm, xo = (x + 1) % 4, (x + 3) % 4, (x + 2) % 4
    yp, ym, yo = (y + 1) % 4, (y + 3) % 4, (y + 2) % 4

    def in_plane(to_y, to_x):
        return device(to_y % 2, z, core, to_y // 2, to_x)

    right, left = in_plane(y, xp), in_plane(y, xm)
    plus_y, minus_y, cross = in_plane(yp, x), in_plane(ym, x), in_plane(yo, x)
    near = device(1 - yl, z, core, yh, x)
    twin = device(yl, z, 1 - core, yh, x)
    diag = device(1 - yl, z, 1 - core, yh, x)
    peers = [device(yl, (z + d) % 8, core, yh, x) for d in range(1, 8)]

    barrier = pltpu.get_barrier_semaphore()
    beside = [right, left, plus_y, minus_y, peers[0], peers[6]]
    greeted = beside + [cross, twin]
    for to in greeted:
        pl.semaphore_signal(barrier, inc=1, device_id=to, device_id_type=MESH)

    own = []
    for h in range(KVH):
        for i, src in enumerate((k_hbm, v_hbm)):
            own.append(
                pltpu.make_async_copy(
                    src.at[:, pl.ds(h * D, D)], kv.at[0, h, pl.ds(i * 256, 256)], own_sem.at[h, i]
                )
            )
            own[-1].start()
    loads = []
    for i, (src, dst) in enumerate(((og_hbm, cot), (wu_hbm, wubuf), (q_hbm, qbuf), (wd_hbm, wdbuf))):
        copy = pltpu.make_async_copy(src, dst, load_sem.at[i])
        copy.start()
        loads.append(copy)

    def tell(k):
        for to in beside:
            pl.semaphore_signal(met.at[k], inc=1, device_id=to, device_id_type=MESH)

    def hear(k):
        pl.semaphore_wait(met.at[k], len(beside))

    first, second = pl.ds(0, 256), pl.ds(256, 256)
    most, rest = pl.ds(0, 448), pl.ds(448, 64)

    def hops(h):
        return tuple(
            remote(src, dst, kv_send.at[i, h], kv_recv.at[i, h], to)
            for i, (src, dst, to) in enumerate((
                (kv.at[0, h], kv.at[1, h], right),
                (kv.at[0, h], kv.at[2, h], left),
                (kv.at[0, h], kv.at[3, h], cross),
                (kv.at[1, h, first], kv.at[4, h, first], right),
                (kv.at[2, h, second], kv.at[4, h, second], left),
                (kv.at[3, h, most], kv.at[5, h, most], right),
                (kv.at[3, h, most], kv.at[6, h, most], left),
                (kv.at[4, h], kv.at[7, h], cross),
                (kv.at[1, h, rest], kv.at[5, h, rest], cross),
                (kv.at[2, h, rest], kv.at[6, h, rest], cross),
            ))
        )

    links = [hops(h) for h in range(KVH)]

    def start(h, *steps):
        for i in steps:
            links[h][i].start()

    def arrived(h, *steps):
        for i in steps:
            links[h][i].wait_recv()

    def send_own(h):
        own[2 * h].wait()
        own[2 * h + 1].wait()
        start(h, 0, 1, 2)

    own[0].wait()
    own[1].wait()
    pl.semaphore_wait(barrier, len(greeted))
    start(0, 0, 1, 2)
    send_own(1)
    tell(0)

    scale = adv_ref[...].astype(F32) * (1.0 / (128.0 * 256.0))
    column = jnp.broadcast_to(scale, (128, T)).T
    wide = FEATURES // 8

    def cotangent(part):
        cols = slice(part * wide, (part + 1) * wide)
        for at in range(part * wide, (part + 1) * wide, 128):
            cot[:, at:at + 128] = (column * cot[:, at:at + 128].astype(F32)).astype(BF16)
        term = lax.dot_general(
            cot[:, cols], wubuf[:, cols], (((1,), (1,)), ((), ())), preferred_element_type=F32
        )
        if part == 0:
            acc[...] = term
        else:
            acc[...] += term

    loads[0].wait()
    loads[1].wait()
    for part in range(4):
        cotangent(part)
    arrived(0, 0, 1, 2)
    send_own(2)
    hear(0)
    tell(1)
    for part in range(4, 8):
        cotangent(part)
    for half in range(2):
        blh[half] = acc[:, half * 128:(half + 1) * 128].astype(BF16)
    cot_copy = remote(cot, cot2, core_send.at[0], core_recv.at[0], twin)
    cot_copy.start()
    bl_copy = remote(blh.at[1 - core], bl2, core_send.at[1], core_recv.at[1], twin)
    bl_copy.start()
    arrived(1, 0, 1, 2)
    send_own(3)
    start(0, 3, 4, 8, 9)
    start(1, 3, 4, 8, 9)
    hear(1)
    tell(2)

    ctx = yh * 4 + x
    marked = [jnp.int32(0)] * BLOCKS
    cur = ctx
    for _ in range(BLOCKS):
        cur = parents[0, cur]
        marked = [jnp.where(cur == b, 1, marked[b]) for b in range(BLOCKS)]
    for s in range(1, BLOCKS):
        block = (yh if SLOT_ROW[s] == 0 else 1 - yh) * 4 + (x + SLOT_STEP[s]) % 4
        seen = jnp.int32(0)
        for b in range(BLOCKS):
            seen = jnp.where(block == b, marked[b], seen)
        offs[s] = jnp.where(seen > 0, 0.0, MASKED)
    key_pos = lax.broadcasted_iota(jnp.int32, (T, T), 0)
    query_pos = lax.broadcasted_iota(jnp.int32, (T, T), 1)
    of_query = jnp.broadcast_to(branch_ref[...].astype(F32), (T, T))
    of_key = of_query.T
    local = (key_pos <= query_pos) & ((of_key == of_query) | (of_key == 0.0))
    bias[...] = jnp.where(local, 0.0, MASKED)

    def score(h, *slots):
        for s in slots:
            for g in range(GROUP):
                at = (h * GROUP + g) * D
                value = lax.dot_general(
                    kv[s, h, 0:256, :], qbuf[:, at:at + D], (((1,), (1,)), ((), ())), preferred_element_type=F32
                )
                if s == 0:
                    value = value + bias[...]
                scores[h % 2, s % 4, g] = value
                peak = jnp.max(value.reshape(T // 8, 8, T), axis=0)
                if s > 0:
                    peak = peak + offs[s]
                top[h % 2, g] = peak if s % 4 == 0 else jnp.maximum(top[h % 2, g], peak)

    def weigh(h, slots, peak, total, out, g):
        for s in slots:
            shift = peak if s == 0 else peak - offs[s]
            weight = jnp.exp2(scores[h % 2, s % 4, g] * FACTOR - shift)
            total = total + jnp.sum(weight.reshape(T // 8, 8, T), axis=0)
            out = out + jnp.dot(
                vt[h % 2, :, s % 4 * T:(s % 4 + 1) * T], weight.astype(BF16), preferred_element_type=F32
            )
        return total, out

    def turn_values(h, slots):
        for s in slots:
            vt[h % 2, :, s % 4 * T:(s % 4 + 1) * T] = kv[s, h, 256:512, :].astype(F32).T.astype(BF16)

    def early(h):
        score(h, 0, 1, 2, 3)
        turn_values(h, range(4))
        for g in range(GROUP):
            i = h * GROUP + g
            peak = jnp.max(top[h % 2, g], axis=0, keepdims=True) * FACTOR
            peaks[i] = jnp.broadcast_to(peak, (8, T))
            totals[i], outs[i] = weigh(h, range(4), peak, jnp.zeros((8, T), F32), jnp.zeros((D, T), F32), g)

    def late(h):
        turn_values(h, range(4, 8))
        for g in range(GROUP):
            i = h * GROUP + g
            before = peaks[i][0:1]
            peak = jnp.maximum(before, jnp.max(top[h % 2, g], axis=0, keepdims=True) * FACTOR)
            fade = jnp.exp2(before - peak)
            total, out = weigh(h, range(4, 8), peak, totals[i] * fade, outs[i] * fade, g)
            bottom = jnp.sum(total, axis=0, keepdims=True)
            ctx_t[h, g * D:(g + 1) * D, :] = (out / bottom).astype(BF16)

    ctx_copies = [
        remote(ctx_t.at[h], ctx2.at[h], core_send.at[2 + h], core_recv.at[2 + h], twin) for h in range(KVH)
    ]

    def after(h):
        if h < KVH - 1:
            ctx_copies[h].start()
        term = jnp.dot(wdt[h], ctx_t[h], preferred_element_type=F32)
        if h == 0:
            low[...] = term
        else:
            low[...] += term

    def band(at):
        return rows16(at * 80, 80)

    z1 = [
        [
            remote(
                downb.at[h, band((z + d) % 8)], zin.at[h, d - 1], z1_send.at[h, d - 1], z1_recv.at[h, d - 1], peers[d - 1]
            )
            for d in range(1, 8)
        ]
        for h in range(KVH)
    ]

    def down_terms(h):
        ctx_copies[h].wait_recv()
        term = jnp.dot(ctx_t[h], blh[core], preferred_element_type=F32)
        term = term + jnp.dot(ctx2[h], bl2[...], preferred_element_type=F32)
        downb[h] = term.astype(BF16)
        for d in FAR_FIRST:
            z1[h][d - 1].start()

    me = y * 4 + x
    z2 = []
    for h in range(KVH):
        for to_yl in range(2):
            to_y = (h // 2) * 2 + to_yl
            to_x = 2 * (h % 2) + z // 4
            z2.append((
                to_y * 4 + to_x != me,
                remote(zs.at[h], zin2.at[me], z2_send.at[h, to_yl], z2_recv.at[me], in_plane(to_y, to_x)),
            ))

    def band_sum(h):
        total = downb[h, band(z), :].astype(F32)
        for d in range(1, 8):
            z1[h][d - 1].wait_recv()
            total = total + zin[h, d - 1].astype(F32)
        zs[h] = total.astype(BF16)
        for elsewhere, copy in z2[2 * h:2 * h + 2]:
            pl.when(elsewhere)(copy.start)

    loads[2].wait()
    early(0)
    loads[3].wait()
    for i in range(KVH * GROUP):
        wdt[i // GROUP, :, i % GROUP * D:(i % GROUP + 1) * D] = wdbuf[i * D:(i + 1) * D, :].astype(F32).T.astype(BF16)

    early(1)
    arrived(2, 0, 1, 2)
    start(2, 3, 4, 8, 9)
    hear(2)
    early(2)
    arrived(3, 0, 1, 2)
    start(3, 3, 4, 8, 9)
    for h in range(KVH):
        start(h, 5, 6)
    early(3)
    for h in range(KVH):
        arrived(h, 3, 4)
        start(h, 7)
        if h < 2:
            score(h, 4)
    bl_copy.wait_recv()
    for h in range(KVH):
        if h >= 2:
            score(h, 4)
        arrived(h, 5, 6)
        score(h, 5, 6)
        arrived(h, 7)
        score(h, 7)
        arrived(h, 8, 9)
        late(h)
        after(h)
        if 1 <= h < KVH - 1:
            down_terms(h - 1)
        if h == KVH - 1:
            break
        if h >= 2:
            band_sum(h - 2)

    for half in range(2):
        lowh[half] = low[half * 128:(half + 1) * 128, :].astype(BF16)
    low_copy = remote(lowh.at[1 - core], low2, core_send.at[6], core_recv.at[6], twin)
    low_copy.start()
    ctx_copies[KVH - 1].start()
    down_terms(2)
    cot_copy.wait_recv()
    low_copy.wait_recv()

    def up_terms(row, col):
        cols = pl.ds(pl.multiple_of((row * 4 + col) * 640, 128), 640)
        term = jnp.dot(lowh[core], cot[:, cols], preferred_element_type=F32)
        term = term + jnp.dot(low2[...], cot2[:, cols], preferred_element_type=F32)
        for j in range(5):
            terms[row, col, j * 128:(j + 1) * 128, :] = term[:, j * 128:(j + 1) * 128].astype(BF16)

    def by_x(col):
        return terms.at[:, col, pl.ds(0, 160)], terms.at[:, col, pl.ds(160, 160)]

    def by_y(at):
        part = rows16(320 + (at % 2) * 160, 160)
        return terms.at[at // 2, pl.ds(0, 2), part], terms.at[at // 2, pl.ds(2, 2), part]

    ring_x = Ring(
        right, left, (by_x(xo), by_x(xp), by_x(xm), by_x(x)),
        [x1.at[i] for i in range(8)], ring_send.at[0], ring_recv.at[0],
    )
    ring_y = Ring(
        plus_y, minus_y, (by_y(yo), by_y(yp), by_y(ym), by_y(y)),
        [y1.at[i] for i in range(8)], ring_send.at[1], ring_recv.at[1],
    )
    up_terms(yh, xo)
    up_terms(1 - yh, xo)
    ring_x.start(0, 1)
    up_terms(1 - yh, x)
    up_terms(1 - yh, xp)
    up_terms(1 - yh, xm)
    ring_y.start(0, 1)
    up_terms(yh, xp)
    up_terms(yh, xm)
    ring_x.start(2, 3)
    up_terms(yh, x)
    ring_y.start(2, 3)
    down_terms(3)
    ring_x.middle()
    ring_y.middle()

    def x_by_y(at):
        return left_x.at[at // 2, rows16((at % 2) * 160, 160)]

    direct_xy = Direct(
        cross, plus_y, minus_y, (x_by_y(yo), x_by_y(yp), x_by_y(ym), x_by_y(y)), x2, dir_send.at[0], dir_recv.at[0]
    )
    direct_yx = Direct(
        in_plane(y, xo), right, left, (left_y.at[xo], left_y.at[xp], left_y.at[xm], left_y.at[x]),
        y2, dir_send.at[1], dir_recv.at[1],
    )
    a, b = ring_x.end()
    left_x[:, 0:160, :] = a.astype(BF16)
    left_x[:, 160:320, :] = b.astype(BF16)
    direct_xy.begin()
    a, b = ring_y.end()
    left_y[0:2] = a.astype(BF16)
    left_y[2:4] = b.astype(BF16)
    direct_yx.begin()
    band_sum(1)
    band_sum(2)

    quarter[0:160] = direct_xy.end().astype(BF16)
    quarter[160:320] = direct_yx.end().astype(BF16)
    quarter[320:336] = jnp.zeros((16, 128), BF16)

    def chunk(at):
        return rows16(at * 48, 48)

    z_copies = [
        remote(
            quarter.at[chunk((z + d) % 8)], pieces.at[d - 1], z_send.at[0, d - 1], z_recv.at[0, d - 1], peers[d - 1]
        )
        for d in range(1, 8)
    ]
    filled = [(z + 8 - d) % 8 != 7 for d in range(8)]
    wanted = [(z + d) % 8 != 7 for d in range(8)]
    for d in FAR_FIRST:
        pl.when(wanted[d])(z_copies[d - 1].start)

    band_sum(3)
    for h in range(KVH):
        for copy in links[h]:
            copy.wait_send()
    for copy in ctx_copies + [cot_copy, bl_copy, low_copy]:
        copy.wait_send()
    ring_x.finish()
    ring_y.finish()

    def hand_on(d, sems, to):
        here = final.at[core, yl, chunk((z + 8 - d) % 8)]
        return remote(here, here, sems[0].at[d], sems[1].at[d], to)

    near_copies = [hand_on(d, (near_send, near_recv), near) for d in range(8)]
    diag_copies = [hand_on(d, (diag_send, diag_recv), diag) for d in range(8)]
    here = final.at[core, yl, chunk(z)]
    z_copies += [
        remote(here, here, z_send.at[1, d - 1], z_recv.at[1, d - 1], peers[d - 1]) for d in range(1, 8)
    ]

    @pl.when(filled[0])
    def _():
        piece = quarter[chunk(z), :].astype(F32)
        for d in range(1, 8):
            z_copies[d - 1].wait_recv()
            piece = piece + pieces[d - 1].astype(F32)
        final[core, yl, chunk(z), :] = piece.astype(BF16)
        for d in FAR_FIRST:
            z_copies[6 + d].start()
        near_copies[0].start()
        diag_copies[0].start()

    owner = x % 2 == z // 4
    mine = 2 * yh + x // 2
    spot = rows16((z % 4) * 80, 80)
    z4 = [
        remote(fdown.at[core, spot], fdown.at[core, spot], z4_send.at[d - 1], z4_recv.at[z % 4], peers[d - 1])
        for d in range(1, 8)
    ]

    @pl.when(owner)
    def _():
        for i in range(16):

            @pl.when(i != me)
            def _():
                remote(zs.at[0], zin2.at[i], z2_send.at[0, 0], z2_recv.at[i], twin).wait_recv()

            @pl.when(i == me)
            def _():
                zin2[i] = zs[mine]

        total = zin2[0].astype(F32)
        for i in range(1, 16):
            total = total + zin2[i].astype(F32)
        fdown[core, spot, :] = total.astype(BF16)
        for d in FAR_FIRST:
            z4[d - 1].start()

    for h in range(KVH):
        for copy in z1[h]:
            copy.wait_send()
    for elsewhere, copy in z2:
        pl.when(elsewhere)(copy.wait_send)
    for d in range(1, 8):
        pl.when(wanted[d])(z_copies[d - 1].wait_send)
    direct_xy.finish()
    direct_yx.finish()
    for d in (1, 7, 2, 6, 3, 5, 4):

        @pl.when(filled[d])
        def _():
            z_copies[6 + d].wait_recv()
            near_copies[d].start()
            diag_copies[d].start()

    here = final.at[core, yl, pl.ds(0, 320)]
    to_twin = remote(here, here, out_send.at[1], out_recv.at[1], twin)
    to_twin.start()
    for i in range(4):
        at = pl.ds(i * 80, 80)
        part = fdown.at[core, at]

        @pl.when(jnp.logical_not(owner) | (z % 4 != i))
        def _():
            remote(part, part, z4_send.at[0], z4_recv.at[i], twin).wait_recv()

    down_out = remote(fdown.at[core], fdown.at[core], out_send.at[3], out_recv.at[3], twin)
    down_out.start()

    for d in range(8):
        pl.when(filled[d])(near_copies[d].wait_recv)
        pl.when(filled[d])(diag_copies[d].wait_recv)
    to_twin.wait_recv()
    down_out.wait_recv()

    @pl.when(owner)
    def _():
        for copy in z4:
            copy.wait_send()

    @pl.when(filled[0])
    def _():
        for copy in z_copies[7:]:
            copy.wait_send()

    for d in range(8):
        pl.when(filled[d])(near_copies[d].wait_send)
        pl.when(filled[d])(diag_copies[d].wait_send)
    down_out.wait_send()
    to_twin.wait_send()


def lay_out(fdown, final, down_ref, up_ref):
    for k in range(2):
        down_ref[:, k * 128:(k + 1) * 128] = fdown[k].astype(F32)
        for row in range(0, 640, 32):
            part, at = row // 160 % 2, row // 320 * 160 + row % 160
            to, cols = k * 128 + row % 128, slice(row // 128 * 128, row // 128 * 128 + 128)
            up_ref[to:to + 32, cols] = final[k, part, at:at + 32, :].astype(F32)


def on_device(q, k, v, og, adv, branch, parents, wd, wu):
    hbm = pl.BlockSpec(memory_space=pl.ANY)
    vmem = pl.BlockSpec(memory_space=pltpu.VMEM)
    dma = pltpu.SemaphoreType.DMA
    sums = pl.pallas_call(
        kernel,
        name="adapter_gradients",
        out_shape=(
            jax.ShapeDtypeStruct((2, 320, 128), BF16),
            jax.ShapeDtypeStruct((2, 2, 384, 128), BF16),
        ),
        in_specs=[pl.BlockSpec(memory_space=pltpu.SMEM), vmem, vmem] + [hbm] * 6,
        out_specs=(vmem, vmem),
        scratch_shapes=[
            pltpu.VMEM((BLOCKS, KVH, 512, D), BF16),
            pltpu.VMEM((T, ATTN), BF16),
                pltpu.VMEM((RANK, FEATURES), BF16),
            pltpu.VMEM((ATTN, RANK), BF16),
            pltpu.VMEM((KVH, RANK, GROUP * D), BF16),
            pltpu.VMEM((T, FEATURES), BF16),
            pltpu.VMEM((T, FEATURES), BF16),
            pltpu.VMEM((T, RANK), F32),
            pltpu.VMEM((2, T, 128), BF16),
            pltpu.VMEM((T, 128), BF16),
            pltpu.VMEM((KVH, GROUP * D, T), BF16),
            pltpu.VMEM((KVH, GROUP * D, T), BF16),
            pltpu.VMEM((RANK, T), F32),
            pltpu.VMEM((2, 128, T), BF16),
            pltpu.VMEM((128, T), BF16),
            pltpu.VMEM((2, 4, GROUP, T, T), F32),
            pltpu.VMEM((2, GROUP, 8, T), F32),
            pltpu.VMEM((T, T), F32),
            pltpu.VMEM((2, D, 4 * T), BF16),
            pltpu.VMEM((KVH * GROUP, 8, T), F32),
            pltpu.VMEM((KVH * GROUP, 8, T), F32),
            pltpu.VMEM((KVH * GROUP, D, T), F32),
            pltpu.SMEM((BLOCKS,), F32),
            pltpu.VMEM((KVH, GROUP * D, 128), BF16),
            pltpu.VMEM((KVH, 7, 80, 128), BF16),
            pltpu.VMEM((KVH, 80, 128), BF16),
            pltpu.VMEM((16, 80, 128), BF16),
            pltpu.VMEM((2, 4, 640, 128), BF16),
            pltpu.VMEM((8, 2, 160, 128), BF16),
            pltpu.VMEM((8, 2, 160, 128), BF16),
            pltpu.VMEM((2, 320, 128), BF16),
            pltpu.VMEM((4, 160, 128), BF16),
            pltpu.VMEM((3, 160, 128), BF16),
            pltpu.VMEM((3, 160, 128), BF16),
            pltpu.VMEM((384, 128), BF16),
            pltpu.VMEM((7, 48, 128), BF16),
            dma((KVH, 2)),
            dma((4,)),
            dma((10, KVH)), dma((10, KVH)),
            dma((7,)), dma((7,)),
            dma((KVH, 7)), dma((KVH, 7)),
            dma((KVH, 2)), dma((16,)),
            dma((7,)), dma((4,)),
            dma((2, 6)), dma((2, 6)),
            dma((2, 3)), dma((2, 3)),
            dma((2, 7)), dma((2, 7)),
            dma((8,)), dma((8,)),
            dma((8,)), dma((8,)),
            dma((4,)), dma((4,)),
            pltpu.SemaphoreType.REGULAR((3,)),
        ],
        compiler_params=pltpu.CompilerParams(
            collective_id=0, has_side_effects=True, vmem_limit_bytes=60 * MIB
        ),
    )(parents, adv, branch[0], q[0], k[0], v[0], og[0], wu, wd)
    return pl.pallas_call(
        lay_out,
        name="lay_out",
        out_shape=(
            jax.ShapeDtypeStruct((320, RANK), F32),
            jax.ShapeDtypeStruct((RANK, 640), F32),
        ),
        in_specs=[vmem, vmem],
        out_specs=(vmem, vmem),
    )(*sums)


def solution(mesh):
    return jax.shard_map(
        on_device,
        mesh=mesh,
        in_specs=(
            P("dp", "ctx", None),
            P("dp", "ctx", None),
            P("dp", "ctx", None),
            P("dp", "ctx", None),
            P("dp", "ctx"),
            P("dp", "ctx", None),
            P("dp", None),
            P(),
            P(),
        ),
        out_specs=(P("ctx", None), P(None, "ctx")),
        check_vma=False,
    )
```
